32 devices in a mesh: expert: 8 (over z, x), dp: 4 (over y, core).
Axes of the slice: x: 2, y: 2, z: 4, core: 2. Of those that a mesh axis runs over, the one named last changes fastest.
Arguments:
- tokens: bfloat16 [32, 1024, 512], P(('expert', 'dp')), may hold values from -6 to 6
- segment_ids: int32 [32, 1024], P(('expert', 'dp')), may hold values from 0 to 7, never falling along the last dimension, each value on 1 to 512 neighbouring positions
- live_tokens: int32 [32], P(('expert', 'dp')), may hold values from 1 to 1024, 16384 in all
- cotangent: bfloat16 [32, 1024, 512], P(('expert', 'dp')), may hold values from -6 to 6
- ln1_gain: bfloat16 [512], replicated, may hold values from 0.5 to 1.5
- ln1_bias: bfloat16 [512], replicated, may hold values from -2 to 2
- qkv_weight: bfloat16 [512, 1536], replicated, may hold values from -0.25 to 0.25
- attn_weight: bfloat16 [512, 512], replicated, may hold values from -0.75 to 0.75
- ln2_gain: bfloat16 [512], replicated, may hold values from 0.5 to 1.5
- ln2_bias: bfloat16 [512], replicated, may hold values from -2 to 2
- task_logits: float32 [8, 2], P('expert'), may hold values from -3 to 3
- expert_in: bfloat16 [8, 512, 1024], P('expert'), may hold values from -0.25 to 0.25
- expert_out: bfloat16 [8, 1024, 512], P('expert'), may hold values from -0.125 to 0.125
Outputs:
- layer_out: bfloat16 [32, 1024, 512], P(('expert', 'dp'))
- input_grad: bfloat16 [32, 1024, 512], P(('expert', 'dp'))
- ln1_gain_grad: float32 [512], replicated
- ln1_bias_grad: float32 [512], replicated
- qkv_grad: float32 [512, 1536], replicated
- attn_grad: float32 [512, 512], replicated
- ln2_gain_grad: float32 [512], replicated
- ln2_bias_grad: float32 [512], replicated
- logits_grad: float32 [8, 2], P('expert')
- expert_in_grad: float32 [8, 512, 1024], P('expert')
- expert_out_grad: float32 [8, 1024, 512], P('expert')
The draws below stay inside these ranges and needn't reach their ends.
Inputs may be any that keep to these rules, and one draw needn't show every extreme that they name: `segment_ids`: within each packed row, segment ids never fall; each sentence has 1 to 512 tokens. `live_tokens`: the live counts of all rows sum to 16384; some row is wholly live.
All inputs are finite; a program needn't handle non-finite values. No bound on the sum of `live_tokens` on one device may be relied on, other than what follows from the above.
Results may differ from the reference program's by a relative error of at most 0.01.
Values may be sent and summed in bfloat16 or wider, within the bound.
A program may use at most 192 MiB of HBM per device.

```python
import math
import jax
import jax.numpy as jnp
import numpy as np
from jax import lax

D = 512
FF = 2048
SEQ = 1024
SEGS = 8
HEAD_DIM = 64
HALF = 1024
ROWS = 32
N_EXPERT = 8


def block_levels(own_key, dims, split, smallest, top_value):
    def one(dim, parts):
        draws = jax.random.uniform(jax.random.fold_in(jax.random.fold_in(own_key, 6), dim), (parts,), jnp.float32, smallest / len(split), top_value / len(split))
        return jnp.repeat(jnp.exp(draws), dims[dim] // parts).reshape((-1,) + (1,) * (len(dims) - dim - 1))

    level = one(*split[0])
    for cut in split[1:]:
        level = level * one(*cut)
    return level


def split_up(amount, total, most, skew):
    weights = [(1 << 20) // math.isqrt(rank ** skew) + 1 for rank in range(2, amount + 1)]
    surplus, counts = total - most - (amount - 1), [1] * (amount - 1)
    while surplus > 0:
        movable = [i for i in range(amount - 1) if counts[i] < most]
        mass, remaining = sum([weights[i] for i in movable]), surplus
        for i in movable:
            more = min(most - counts[i], max(1, remaining * weights[i] // mass), surplus)
            counts[i] = counts[i] + more
            surplus = surplus - more
    return np.array([most] + counts)


def ragged(key, amount, total, most, slope):
    if amount == 2:
        one = jax.random.randint(key, (), max(1, total - most), min(most, total - 1) + 1)
        return jnp.stack([one, total - one])
    lengths = jnp.asarray(split_up(amount, total, most, slope), jnp.int32)
    couples = (amount - 1) // 2
    donor, sink = lengths[1:1 + 2 * couples:2], lengths[2:2 + 2 * couples:2]
    room = jnp.minimum(donor - 1, most - sink)
    moved = jax.random.randint(jax.random.fold_in(key, 1), (couples,), 0, 1 << 20) % (room + 1)
    lengths = lengths.at[1:1 + 2 * couples:2].set(donor - moved).at[2:2 + 2 * couples:2].set(sink + moved)
    return lengths[jax.random.permutation(jax.random.fold_in(key, 2), amount)]


def scatter_about(stream_key, dims, deviation, most, cuts=(), held_as=jnp.bfloat16):
    level = block_levels(stream_key, dims, cuts, -0.22, 0.18) if cuts else 1.0
    entries = jax.random.normal(stream_key, dims, jnp.float32) * deviation * level
    return jnp.minimum(jnp.maximum(entries, -most), most).astype(held_as)


def setup_inputs(seed: int = 0) -> dict:
    seeds = jax.random.split(jax.random.key(seed), 14)
    return {
        "tokens": scatter_about(seeds[0], (ROWS, SEQ, D), 1.0, 6.0, ((0, 32),)),
        "segment_ids": jax.vmap(lambda own: jnp.searchsorted(jnp.cumsum(ragged(own, SEGS, SEQ, SEQ // 2, 2)), jnp.arange(SEQ), side="right"))(jax.random.split(seeds[1], ROWS)).reshape((ROWS, SEQ)).astype(jnp.int32),
        "live_tokens": ragged(seeds[2], ROWS, ROWS * SEQ // 2, SEQ, 2).astype(jnp.int32),
        "cotangent": scatter_about(seeds[3], (ROWS, SEQ, D), 1.0, 6.0, ((0, 32),)),
        "ln1_gain": jnp.clip(1.0 + 0.1 * jax.random.normal(seeds[4], (D,), jnp.float32), 0.5, 1.5).astype(jnp.bfloat16),
        "ln1_bias": scatter_about(seeds[5], (D,), 0.3, 2.0),
        "qkv_weight": scatter_about(seeds[6], (D, 3 * D), D ** -0.5, 0.25),
        "attn_weight": scatter_about(seeds[7], (D, D), (D // 8) ** -0.5, 0.75),
        "ln2_gain": jnp.clip(1.0 + 0.1 * jax.random.normal(seeds[8], (D,), jnp.float32), 0.5, 1.5).astype(jnp.bfloat16),
        "ln2_bias": scatter_about(seeds[9], (D,), 0.3, 2.0),
        "task_logits": scatter_about(seeds[10], (N_EXPERT, 2), 0.7, 3.0, ((0, 8),), jnp.float32),
        "expert_in": scatter_about(seeds[11], (N_EXPERT, D, HALF), D ** -0.5, 0.25, ((0, 8),)),
        "expert_out": scatter_about(seeds[12], (N_EXPERT, HALF, D), FF ** -0.5, 0.125, ((0, 8),)),
    }


@jax.custom_vjp
def low(v):
    return lax.optimization_barrier(v.astype(jnp.bfloat16)).astype(jnp.float32)

@jax.custom_vjp
def low_back(v):
    return v

def low_keep(v):
    return (low(v), None)

def low_pass(kept, grad):
    return (grad,)

def back_keep(v):
    return (v, None)

def back_low(kept, grad):
    return (low(grad),)
low.defvjp(low_keep, low_pass)
low_back.defvjp(back_keep, back_low)
norm_eps = 1e-05
highest = lax.Precision.HIGHEST

def product(left, right):
    return jnp.dot(left, right, precision=highest, preferred_element_type=jnp.float32)

def layer_norm(inputs, gain, shift):
    row_mean = lax.optimization_barrier(jnp.mean(inputs, axis=-1, keepdims=True))
    centred = inputs - row_mean
    variance = lax.optimization_barrier(jnp.mean(centred * centred, axis=-1, keepdims=True))
    return centred * lax.rsqrt(variance + norm_eps) * gain + shift

def layer_row(row_in, segments, live_count, task, params):
    ln1_gain, ln1_bias, qkv_weight, attn_weight, ln2_gain, ln2_bias, task_logits, expert_in, expert_out = params
    length, model_width = row_in.shape
    head_count = model_width // HEAD_DIM
    score_scale = HEAD_DIM ** (-0.5)
    normed_one = low(layer_norm(row_in, ln1_gain, ln1_bias))
    packed = low(low_back(product(normed_one, qkv_weight)))
    queries = packed[:, :model_width].reshape(length, head_count, HEAD_DIM)
    key_rows = packed[:, model_width:2 * model_width].reshape(length, head_count, HEAD_DIM)
    val_rows = packed[:, 2 * model_width:].reshape(length, head_count, HEAD_DIM)
    raw_scores = jnp.einsum('qhd,khd->hqk', queries, key_rows, precision=highest)
    scores = low_back(raw_scores * score_scale)
    positions = jnp.arange(length, dtype=jnp.int32)
    is_live = positions < live_count
    same_doc = (segments[:, None] == segments[None, :]) & is_live[None, :]
    keep_mask = jnp.where(is_live[:, None], same_doc, positions[:, None] == positions[None, :])[None]
    scores = jnp.where(keep_mask, scores, -1e+30)
    row_top = lax.optimization_barrier(jnp.max(scores, axis=-1, keepdims=True))
    exponent = jnp.exp(scores - row_top)
    attention = low(exponent / lax.optimization_barrier(jnp.sum(exponent, axis=-1, keepdims=True)))
    context = jnp.einsum('hqk,khd->qhd', attention, val_rows, precision=highest).reshape(length, model_width)
    context = low(low_back(context))
    middle = row_in + low_back(product(context, attn_weight))
    normed_two = low(layer_norm(middle, ln2_gain, ln2_bias))
    gate_probs = jax.nn.softmax(task_logits[task])
    first_expert = task // 2
    experts_all = expert_in.shape[0] // 2
    result = middle
    for slot_index in range(2):
        expert_idx = (first_expert + slot_index) % experts_all
        weight_in = jnp.concatenate([expert_in[2 * expert_idx], expert_in[2 * expert_idx + 1]], axis=1)
        weight_out = jnp.concatenate([expert_out[2 * expert_idx], expert_out[2 * expert_idx + 1]], axis=0)
        hidden = low(jax.nn.gelu(low_back(product(normed_two, weight_in))))
        result = result + gate_probs[slot_index] * low_back(product(hidden, weight_out))
    return result

def reference(tokens, segment_ids, live_tokens, cotangent, ln1_gain, ln1_bias, qkv_weight, attn_weight, ln2_gain, ln2_bias, task_logits, expert_in, expert_out):
    params = tuple((matrix.astype(jnp.float32) for matrix in (ln1_gain, ln1_bias, qkv_weight, attn_weight, ln2_gain, ln2_bias, task_logits, expert_in, expert_out)))
    row_count = tokens.shape[0]
    length = tokens.shape[1]
    per_task = row_count // task_logits.shape[0]

    def step(totals, item_tuple):
        row_in, segments, live_count, row_grad, row_index = item_tuple
        task = row_index // per_task

        def forward(inputs, weights):
            return layer_row(inputs, segments, live_count, task, weights)
        result, pullback = jax.vjp(forward, row_in.astype(jnp.float32), params)
        live_mask = (jnp.arange(length, dtype=jnp.int32) < live_count).astype(jnp.float32)[:, None]
        grad_in, grad_params = pullback(row_grad.astype(jnp.float32) * live_mask)
        totals = jax.tree.map(lambda left, right: left + right, totals, grad_params)
        return (totals, (result.astype(jnp.bfloat16), grad_in.astype(jnp.bfloat16)))
    zeros = jax.tree.map(jnp.zeros_like, params)
    totals, (outputs, grads) = lax.scan(step, zeros, (tokens, segment_ids, live_tokens, cotangent, jnp.arange(row_count, dtype=jnp.int32)))
    return (outputs, grads, totals[0], totals[1], totals[2], totals[3], totals[4], totals[5], totals[6], totals[7], totals[8])
```

```python
import functools

import jax
import jax.numpy as jnp
from jax import lax
from jax.experimental import pallas as pl
from jax.experimental.pallas import tpu as pltpu
from jax.sharding import PartitionSpec as P

F32 = jnp.float32
BF16 = jnp.bfloat16
HEAD_DIM = 64
NORM_EPS = 1e-05
MASKED = -1e30
LOG2E = 1.4426950408889634
GELU_A = 0.7978845608028654
GELU_B = 0.044715


def dot_nn(a, b):
    return jnp.dot(a, b, preferred_element_type=F32)


def dot_nt(a, b):
    return lax.dot_general(a, b, (((1,), (1,)), ((), ())), preferred_element_type=F32)


def dot_tn(a, b):
    return lax.dot_general(a, b, (((0,), (0,)), ((), ())), preferred_element_type=F32)


def dot_tt(a, b):
    return lax.dot_general(a, b, (((0,), (1,)), ((), ())), preferred_element_type=F32)


def norm_parts(inputs):
    row_mean = jnp.mean(inputs, axis=-1, keepdims=True)
    centred = inputs - row_mean
    variance = jnp.mean(centred * centred, axis=-1, keepdims=True)
    inverse = lax.rsqrt(variance + NORM_EPS)
    return centred * inverse, inverse


def norm_back(scaled, normal, inverse):
    return inverse * (
        scaled
        - jnp.mean(scaled, axis=-1, keepdims=True)
        - normal * jnp.mean(scaled * normal, axis=-1, keepdims=True)
    )


def split_three(value):
    high = value.astype(BF16)
    rest = value - high.astype(F32)
    middle = rest.astype(BF16)
    low = (rest - middle.astype(F32)).astype(BF16)
    return high.astype(F32), middle.astype(F32), low.astype(F32)


def scaled_queries(queries):
    scaled = queries.astype(F32) * (LOG2E * HEAD_DIM ** (-0.5))
    high = scaled.astype(BF16)
    return high, (scaled - high.astype(F32)).astype(BF16)


def mask_rows(segments, live, length):
    position = lax.broadcasted_iota(jnp.int32, (16, length), 1)
    row = lax.broadcasted_iota(jnp.int32, (16, length), 0)
    segment = jnp.broadcast_to(segments, (16, length))
    alive = position < live
    for_query = jnp.where(
        row < 8,
        jnp.where(segment != row, MASKED, 0.0),
        jnp.where((row == 8) & alive, MASKED, 0.0),
    )
    for_key = jnp.where(
        row < 8,
        jnp.where(segment == row, 1.0, 0.0),
        jnp.where((row == 8) & (~alive), 1.0, 0.0),
    )
    for_key_back = jnp.where((row >= 9) & (row < 12), 1.0, for_key)
    return for_query, for_key, for_key_back


def head_rows(head, part, width):
    return pl.ds(pl.multiple_of(part * width + head * HEAD_DIM, HEAD_DIM), HEAD_DIM)


def key_band(start, size, tile, length):
    low = max(0, (start - 511) // tile * tile)
    high = min(length, -(-(start + size + 511) // tile) * tile)
    return low, high


def attend_forward(head, qkv_t, ctx_t, lse, mask_q, alive_row, q_aug, k_aug, v_aug, tile):
    width, length = ctx_t.shape
    high, low = scaled_queries(qkv_t[head_rows(head, 0, width), :])
    q_aug[0:64, :] = high
    q_aug[64:128, :] = low
    q_aug[128:144, :] = mask_q[...]
    keys = qkv_t[head_rows(head, 1, width), :]
    k_aug[0:64, :] = keys
    k_aug[64:128, :] = keys
    v_aug[0:64, :] = qkv_t[head_rows(head, 2, width), :]
    for start in range(0, length, tile):
        at = pl.ds(start, tile)
        scores = dot_tn(k_aug[...], q_aug[:, at])
        top = jnp.max(scores, axis=0, keepdims=True)
        weights = jnp.exp2(scores - top).astype(BF16)
        summed = dot_nn(v_aug[...], weights)
        total = summed[64:65, :]
        context = summed[0:64, :] * (1.0 / total)
        own = v_aug[0:64, at].astype(F32)
        ctx_t[head_rows(head, 0, width), at] = jnp.where(
            alive_row[:, at] > 0, context, own
        ).astype(BF16)
        lse[head, :, at] = top + jnp.log(total) * LOG2E


def attend_backward(head, qkv_t, dctx_t, ctx_t, lse, mask_q, q_aug, k_aug, v_aug, d_aug, dk, dv, tile):
    width, length = ctx_t.shape
    scale = HEAD_DIM ** (-0.5)
    row = lax.broadcasted_iota(jnp.int32, (16, length), 0)
    high, low = scaled_queries(qkv_t[head_rows(head, 0, width), :])
    q_aug[0:64, :] = high
    q_aug[64:128, :] = low
    one, two, three = split_three(-lse[head])
    q_aug[128:144, :] = jnp.where(
        row == 9, one, jnp.where(row == 10, two, jnp.where(row == 11, three, mask_q[...].astype(F32)))
    ).astype(BF16)
    keys = qkv_t[head_rows(head, 1, width), :]
    k_aug[0:64, :] = keys
    k_aug[64:128, :] = keys
    v_aug[0:64, :] = qkv_t[head_rows(head, 2, width), :]
    grad = dctx_t[head_rows(head, 0, width), :]
    d_aug[0:64, :] = grad
    context = ctx_t[head_rows(head, 0, width), :].astype(F32)
    one, two, three = split_three(
        -jnp.sum(grad.astype(F32) * context, axis=0, keepdims=True)
    )
    d_aug[64:80, :] = jnp.where(
        row == 0, one, jnp.where(row == 1, two, jnp.where(row == 2, three, 0.0))
    ).astype(BF16)
    dk[...] = jnp.zeros(dk.shape, F32)
    dv[...] = jnp.zeros(dv.shape, F32)
    for start in range(0, length, tile):
        first, last = key_band(start, tile, tile, length)
        at, near = pl.ds(start, tile), pl.ds(first, last - first)
        weights = jnp.exp2(dot_tn(q_aug[:, at], k_aug[:, near]))
        dweights = dot_tn(d_aug[:, at], v_aug[:, near])
        dscores = (weights * dweights).astype(BF16)
        dv[:, near] += dot_nn(d_aug[0:64, at], weights.astype(BF16))
        dk[:, near] += dot_nn(qkv_t[head_rows(head, 0, width), at], dscores)
        qkv_t[head_rows(head, 0, width), at] = (
            dot_nt(k_aug[0:64, near], dscores) * scale
        ).astype(BF16)
    qkv_t[head_rows(head, 1, width), :] = (dk[...] * scale).astype(BF16)
    qkv_t[head_rows(head, 2, width), :] = dv[...].astype(BF16)


def gelu_parts(u):
    square = u * u
    bend = jnp.tanh(u * (GELU_A + (GELU_A * GELU_B) * square))
    half = 0.5 + 0.5 * bend
    slope = half + (0.5 * u) * (1.0 - bend * bend) * (GELU_A + (3.0 * GELU_A * GELU_B) * square)
    return u * half, slope


def kernel(
    tokens, cotangent, segments, live, ln1, ln2, wqkv_in, wattn_in, logits, weights_in,
    out, grad_in, grads_out, qkv_grad, attn_grad, vectors,
    x, dy, wqkv, wattn, w, a1, qkv_t, ctx_t, lse, mid, a2, dz, hid, dpre, z, total, da2,
    dctx_t, qkv_low, attn_low, alive_row, mask_q,
    q_aug, k_aug, v_aug, d_aug, dk, dv, load_sem, store_sem,
):
    length, width = x.shape
    tile = 256
    loads = [
        pltpu.make_async_copy(src, dst, load_sem.at[i])
        for i, (src, dst) in enumerate(
            [(tokens, x), (wqkv_in, wqkv), (wattn_in, wattn), (cotangent, dy), (weights_in, w)]
        )
    ]
    for load in loads:
        load.start()
    live_count = live[0]
    alive_row[...] = jnp.where(
        lax.broadcasted_iota(jnp.int32, (1, length), 1) < live_count, 1.0, 0.0
    )
    for_query, for_key, for_key_back = mask_rows(segments[...], live_count, length)
    mask_q[...] = for_query.astype(BF16)
    k_aug[128:144, :] = for_key.astype(BF16)
    v_aug[64:80, :] = jnp.where(
        lax.broadcasted_iota(jnp.int32, (16, length), 0) == 0, 1.0, 0.0
    ).astype(BF16)
    gain1, bias1 = ln1[0:1, :], ln1[1:2, :]
    gain2, bias2 = ln2[0:1, :], ln2[1:2, :]
    exponent = jnp.exp(logits[...] - jnp.max(logits[...], axis=1, keepdims=True))
    gates = exponent / jnp.sum(exponent, axis=1, keepdims=True)

    loads[0].wait()
    for start in range(0, length, tile):
        at = pl.ds(start, tile)
        normal, inverse = norm_parts(x[at, :].astype(F32))
        a1[at, :] = (normal * gain1 + bias1).astype(BF16)
    loads[1].wait()
    for start in range(0, 3 * width, 512):
        at = pl.ds(start, 512)
        qkv_t[at, :] = dot_tt(wqkv[:, at], a1[...]).astype(BF16)

    def forward_heads(head, carry):
        attend_forward(head, qkv_t, ctx_t, lse, mask_q, alive_row, q_aug, k_aug, v_aug, length)
        return carry

    lax.fori_loop(0, width // HEAD_DIM, forward_heads, 0, unroll=2)

    loads[2].wait()
    loads[3].wait()
    for start in range(0, length, tile):
        at = pl.ds(start, tile)
        middle = x[at, :].astype(F32) + dot_tn(ctx_t[:, at], wattn[...])
        mid[at, :] = middle
        normal, inverse = norm_parts(middle)
        a2[at, :] = (normal * gain2 + bias2).astype(BF16)
        alive = start + lax.broadcasted_iota(jnp.int32, (tile, 1), 0) < live_count
        dy[at, :] = jnp.where(alive, dy[at, :], jnp.zeros((), BF16))
    da2[...] = jnp.zeros(da2.shape, F32)

    loads[4].wait()
    gate_grads = []
    for expert in range(2):
        gate = gates[:, expert : expert + 1]
        for start in range(0, length, tile):
            at = pl.ds(start, tile)
            dz[at, :] = (gate * dy[at, :].astype(F32)).astype(BF16)
        z[...] = jnp.zeros(z.shape, F32)

        def one_half(half, carry):
            slot = 2 * expert + half
            for chunk in range(2):
                w_in, w_out = w.at[slot, 2 * chunk], w.at[slot, 2 * chunk + 1]
                for start in range(0, length, 512):
                    at = pl.ds(start, 512)
                    hidden, slope = gelu_parts(dot_nn(a2[at, :], w_in[...]))
                    hid[chunk, at, :] = hidden.astype(BF16)
                    dpre[chunk, at, :] = (dot_nt(dz[at, :], w_out[...]) * slope).astype(BF16)
                    z[at, :] += dot_nn(hid[chunk, at, :], w_out[...])
                    da2[at, :] += dot_nt(dpre[chunk, at, :], w_in[...])
            for chunk in range(2):
                w[slot, 2 * chunk] = dot_tn(a2[...], dpre[chunk]).astype(BF16)
                w[slot, 2 * chunk + 1] = dot_tn(hid[chunk], dz[...]).astype(BF16)
            return carry

        lax.fori_loop(0, 2, one_half, 0)
        gate_grad = jnp.zeros((1, width), F32)
        for start in range(0, length, tile):
            at = pl.ds(start, tile)
            gate_grad += jnp.sum(dy[at, :].astype(F32) * z[at, :], axis=0, keepdims=True)
            if expert == 0:
                total[at, :] = mid[at, :] + gate * z[at, :]
            else:
                dz[at, :] = (total[at, :] + gate * z[at, :]).astype(BF16)
        gate_grads.append(jnp.sum(gate_grad, axis=1, keepdims=True))
    stores = [
        pltpu.make_async_copy(src, dst, store_sem.at[i])
        for i, (src, dst) in enumerate(
            [(dz, out), (w, grads_out), (attn_low, attn_grad), (qkv_low, qkv_grad), (a2, grad_in)]
        )
    ]
    stores[0].start()
    stores[1].start()

    gain_sum = jnp.zeros((1, width), F32)
    bias_sum = jnp.zeros((1, width), F32)
    for start in range(0, length, tile):
        at = pl.ds(start, tile)
        normal, inverse = norm_parts(mid[at, :])
        grad = da2[at, :]
        gain_sum += jnp.sum(grad * normal, axis=0, keepdims=True)
        bias_sum += jnp.sum(grad, axis=0, keepdims=True)
        dmid = dy[at, :].astype(F32) + norm_back(grad * gain2, normal, inverse)
        mid[at, :] = dmid
        a2[at, :] = dmid.astype(BF16)
    vectors[2:3, :] = gain_sum
    vectors[3:4, :] = bias_sum
    lane = lax.broadcasted_iota(jnp.int32, (1, width), 1)
    vectors[4:5, :] = jnp.where(
        lane == 0, gate_grads[0], jnp.where(lane == 1, gate_grads[1], 0.0)
    )
    vectors[5:8, :] = jnp.zeros((3, width), F32)
    attn_low[...] = dot_nn(ctx_t[...], a2[...]).astype(BF16)
    stores[2].start()
    dctx_t[...] = dot_nt(wattn[...], a2[...]).astype(BF16)

    k_aug[128:144, :] = for_key_back.astype(BF16)
    v_aug[64:80, :] = jnp.where(
        lax.broadcasted_iota(jnp.int32, (16, length), 0) < 3, 1.0, 0.0
    ).astype(BF16)

    def backward_heads(head, carry):
        attend_backward(
            head, qkv_t, dctx_t, ctx_t, lse, mask_q, q_aug, k_aug, v_aug, d_aug, dk, dv, tile
        )
        return carry

    lax.fori_loop(0, width // HEAD_DIM, backward_heads, 0, unroll=2)
    for start in range(0, 3 * width, 512):
        at = pl.ds(start, 512)
        qkv_low[:, at] = dot_tt(a1[...], qkv_t[at, :]).astype(BF16)
    stores[3].start()
    gain_sum = jnp.zeros((1, width), F32)
    bias_sum = jnp.zeros((1, width), F32)
    for start in range(0, length, tile):
        at = pl.ds(start, tile)
        grad = dot_tt(qkv_t[:, at], wqkv[...])
        normal, inverse = norm_parts(x[at, :].astype(F32))
        gain_sum += jnp.sum(grad * normal, axis=0, keepdims=True)
        bias_sum += jnp.sum(grad, axis=0, keepdims=True)
        a2[at, :] = (mid[at, :] + norm_back(grad * gain1, normal, inverse)).astype(BF16)
    vectors[0:1, :] = gain_sum
    vectors[1:2, :] = bias_sum
    stores[4].start()
    for store in stores:
        store.wait()


def one_device(tokens, cotangent, segments, live, ln1, ln2, wqkv, wattn, logits, weights):
    length, width = tokens.shape
    vmem = pl.BlockSpec(memory_space=pltpu.VMEM)
    smem = pl.BlockSpec(memory_space=pltpu.SMEM)
    hbm = pl.BlockSpec(memory_space=pl.ANY)
    shape = jax.ShapeDtypeStruct
    scratch = [
        pltpu.VMEM((length, width), BF16),
        pltpu.VMEM((length, width), BF16),
        pltpu.VMEM(wqkv.shape, BF16),
        pltpu.VMEM(wattn.shape, BF16),
        pltpu.VMEM(weights.shape, BF16),
        pltpu.VMEM((length, width), BF16),
        pltpu.VMEM((3 * width, length), BF16),
        pltpu.VMEM((width, length), BF16),
        pltpu.VMEM((width // HEAD_DIM, 1, length), F32),
        pltpu.VMEM((length, width), F32),
        pltpu.VMEM((length, width), BF16),
        pltpu.VMEM((length, width), BF16),
        pltpu.VMEM((2, length, 512), BF16),
        pltpu.VMEM((2, length, 512), BF16),
        pltpu.VMEM((length, width), F32),
        pltpu.VMEM((length, width), F32),
        pltpu.VMEM((length, width), F32),
        pltpu.VMEM((width, length), BF16),
        pltpu.VMEM(wqkv.shape, BF16),
        pltpu.VMEM(wattn.shape, BF16),
        pltpu.VMEM((1, length), F32),
        pltpu.VMEM((16, length), BF16),
        pltpu.VMEM((144, length), BF16),
        pltpu.VMEM((144, length), BF16),
        pltpu.VMEM((80, length), BF16),
        pltpu.VMEM((80, length), BF16),
        pltpu.VMEM((HEAD_DIM, length), F32),
        pltpu.VMEM((HEAD_DIM, length), F32),
        pltpu.SemaphoreType.DMA((5,)),
        pltpu.SemaphoreType.DMA((5,)),
    ]
    return pl.pallas_call(
        kernel,
        in_specs=[hbm, hbm, vmem, smem, vmem, vmem, hbm, hbm, vmem, hbm],
        out_specs=[hbm, hbm, hbm, hbm, hbm, vmem],
        out_shape=[
            shape(tokens.shape, BF16),
            shape(tokens.shape, BF16),
            shape(weights.shape, BF16),
            shape(wqkv.shape, BF16),
            shape(wattn.shape, BF16),
            shape((8, width), F32),
        ],
        scratch_shapes=scratch,
        compiler_params=pltpu.CompilerParams(vmem_limit_bytes=60 * 1024 * 1024),
    )(tokens, cotangent, segments, live, ln1, ln2, wqkv, wattn, logits, weights)


def to_units(w_in, w_out):
    return jnp.stack([w_in[:, :512], w_out[:512], w_in[:, 512:], w_out[512:]])


def body(
    tokens, segment_ids, live_tokens, cotangent, ln1_gain, ln1_bias, qkv_weight, attn_weight,
    ln2_gain, ln2_bias, task_logits, expert_in, expert_out,
):
    experts = lax.axis_size("expert")
    flip = [(i, i ^ 1) for i in range(experts)]
    up = [(i, (i + 2) % experts) for i in range(experts)]
    down = [((i + 2) % experts, i) for i in range(experts)]
    own = to_units(expert_in[0], expert_out[0])
    following = lax.ppermute(own, "expert", down)
    partner = lax.ppermute(own, "expert", flip)
    following_partner = lax.ppermute(following, "expert", flip)
    weights = jnp.stack([own, partner, following, following_partner])
    ln1 = jnp.stack([ln1_gain, ln1_bias]).astype(F32)
    ln2 = jnp.stack([ln2_gain, ln2_bias]).astype(F32)
    out, grad_in, grads, qkv_grad, attn_grad, vectors = one_device(
        tokens[0], cotangent[0], segment_ids, live_tokens, ln1, ln2, qkv_weight, attn_weight,
        task_logits, weights,
    )
    here = grads[0].astype(F32) + lax.ppermute(grads[1], "expert", flip).astype(F32)
    there = grads[2].astype(F32) + lax.ppermute(grads[3], "expert", flip).astype(F32)
    here = here + lax.ppermute(there.astype(BF16), "expert", up).astype(F32)
    gate_grad = vectors[4, :2]
    here, gate_grad = lax.psum((here, gate_grad), "dp")
    gates = jax.nn.softmax(task_logits[0])
    logits_grad = (gates * (gate_grad - jnp.sum(gates * gate_grad)))[None]
    sums = lax.psum(
        (vectors[:4], qkv_grad.astype(F32), attn_grad.astype(F32)), ("expert", "dp")
    )
    expert_in_grad = jnp.concatenate([here[0], here[2]], axis=1)[None]
    expert_out_grad = jnp.concatenate([here[1], here[3]], axis=0)[None]
    return (
        out[None], grad_in[None], sums[0][0], sums[0][1], sums[1], sums[2], sums[0][2], sums[0][3],
        logits_grad, expert_in_grad, expert_out_grad,
    )


def solution(mesh):
    rows = ("expert", "dp")
    in_specs = (
        P(rows, None, None), P(rows, None), P(rows), P(rows, None, None), P(), P(), P(), P(), P(), P(),
        P("expert", None), P("expert", None, None), P("expert", None, None),
    )
    out_specs = (
        P(rows, None, None), P(rows, None, None), P(), P(), P(), P(), P(), P(),
        P("expert", None), P("expert", None, None), P("expert", None, None),
    )
    return jax.shard_map(body, mesh=mesh, in_specs=in_specs, out_specs=out_specs, check_vma=False)
```

```python
import functools

import jax
import jax.numpy as jnp
from jax import lax
from jax.experimental import pallas as pl
from jax.experimental.pallas import tpu as pltpu
from jax.sharding import PartitionSpec as P

F32 = jnp.float32
BF16 = jnp.bfloat16
HEAD_DIM = 64
NORM_EPS = 1e-05
MASKED = -1e30
LOG2E = 1.4426950408889634
GELU_A = 0.7978845608028654
GELU_B = 0.044715


def dot_nn(a, b):
    return jnp.dot(a, b, preferred_element_type=F32)


def dot_nt(a, b):
    return lax.dot_general(a, b, (((1,), (1,)), ((), ())), preferred_element_type=F32)


def dot_tn(a, b):
    return lax.dot_general(a, b, (((0,), (0,)), ((), ())), preferred_element_type=F32)


def dot_tt(a, b):
    return lax.dot_general(a, b, (((0,), (1,)), ((), ())), preferred_element_type=F32)


def norm_parts(inputs):
    row_mean = jnp.mean(inputs, axis=-1, keepdims=True)
    centred = inputs - row_mean
    variance = jnp.mean(centred * centred, axis=-1, keepdims=True)
    inverse = lax.rsqrt(variance + NORM_EPS)
    return centred * inverse, inverse


def norm_back(scaled, normal, inverse):
    return inverse * (
        scaled
        - jnp.mean(scaled, axis=-1, keepdims=True)
        - normal * jnp.mean(scaled * normal, axis=-1, keepdims=True)
    )


def split_three(value):
    high = value.astype(BF16)
    rest = value - high.astype(F32)
    middle = rest.astype(BF16)
    low = (rest - middle.astype(F32)).astype(BF16)
    return high.astype(F32), middle.astype(F32), low.astype(F32)


def scaled_queries(queries):
    scaled = queries.astype(F32) * (LOG2E * HEAD_DIM ** (-0.5))
    high = scaled.astype(BF16)
    return high, (scaled - high.astype(F32)).astype(BF16)


def mask_rows(segments, live, length):
    position = lax.broadcasted_iota(jnp.int32, (16, length), 1)
    row = lax.broadcasted_iota(jnp.int32, (16, length), 0)
    segment = jnp.broadcast_to(segments, (16, length))
    alive = position < live
    for_query = jnp.where(
        row < 8,
        jnp.where(segment != row, MASKED, 0.0),
        jnp.where((row == 8) & alive, MASKED, 0.0),
    )
    for_key = jnp.where(
        row < 8,
        jnp.where(segment == row, 1.0, 0.0),
        jnp.where((row == 8) & (~alive), 1.0, 0.0),
    )
    for_key_back = jnp.where((row >= 9) & (row < 12), 1.0, for_key)
    return for_query, for_key, for_key_back


def head_rows(head, part, width):
    return pl.ds(pl.multiple_of(part * width + head * HEAD_DIM, HEAD_DIM), HEAD_DIM)


def key_band(start, size, tile, length):
    low = max(0, (start - 511) // tile * tile)
    high = min(length, -(-(start + size + 511) // tile) * tile)
    return low, high


def attend_forward(head, qkv_t, ctx_t, lse, mask_q, alive_row, q_aug, k_aug, v_aug, tile):
    width, length = ctx_t.shape
    high, low = scaled_queries(qkv_t[head_rows(head, 0, width), :])
    q_aug[0:64, :] = high
    q_aug[64:128, :] = low
    q_aug[128:144, :] = mask_q[...]
    keys = qkv_t[head_rows(head, 1, width), :]
    k_aug[0:64, :] = keys
    k_aug[64:128, :] = keys
    v_aug[0:64, :] = qkv_t[head_rows(head, 2, width), :]
    for start in range(0, length, tile):
        at = pl.ds(start, tile)
        scores = dot_tn(k_aug[...], q_aug[:, at])
        top = jnp.max(scores, axis=0, keepdims=True)
        weights = jnp.exp2(scores - top).astype(BF16)
        summed = dot_nn(v_aug[...], weights)
        total = summed[64:65, :]
        context = summed[0:64, :] * (1.0 / total)
        own = v_aug[0:64, at].astype(F32)
        ctx_t[head_rows(head, 0, width), at] = jnp.where(
            alive_row[:, at] > 0, context, own
        ).astype(BF16)
        lse[head, :, at] = top + jnp.log(total) * LOG2E


def attend_backward(head, qkv_t, dctx_t, ctx_t, lse, mask_q, q_aug, k_aug, v_aug, d_aug, dk, dv, tile):
    width, length = ctx_t.shape
    scale = HEAD_DIM ** (-0.5)
    row = lax.broadcasted_iota(jnp.int32, (16, length), 0)
    high, low = scaled_queries(qkv_t[head_rows(head, 0, width), :])
    q_aug[0:64, :] = high
    q_aug[64:128, :] = low
    one, two, three = split_three(-lse[head])
    q_aug[128:144, :] = jnp.where(
        row == 9, one, jnp.where(row == 10, two, jnp.where(row == 11, three, mask_q[...].astype(F32)))
    ).astype(BF16)
    keys = qkv_t[head_rows(head, 1, width), :]
    k_aug[0:64, :] = keys
    k_aug[64:128, :] = keys
    v_aug[0:64, :] = qkv_t[head_rows(head, 2, width), :]
    grad = dctx_t[head_rows(head, 0, width), :]
    d_aug[0:64, :] = grad
    context = ctx_t[head_rows(head, 0, width), :].astype(F32)
    one, two, three = split_three(
        -jnp.sum(grad.astype(F32) * context, axis=0, keepdims=True)
    )
    d_aug[64:80, :] = jnp.where(
        row == 0, one, jnp.where(row == 1, two, jnp.where(row == 2, three, 0.0))
    ).astype(BF16)
    dk[...] = jnp.zeros(dk.shape, F32)
    dv[...] = jnp.zeros(dv.shape, F32)
    for start in range(0, length, tile):
        first, last = key_band(start, tile, tile, length)
        at, near = pl.ds(start, tile), pl.ds(first, last - first)
        weights = jnp.exp2(dot_tn(q_aug[:, at], k_aug[:, near]))
        dweights = dot_tn(d_aug[:, at], v_aug[:, near])
        dscores = (weights * dweights).astype(BF16)
        dv[:, near] += dot_nn(d_aug[0:64, at], weights.astype(BF16))
        dk[:, near] += dot_nn(qkv_t[head_rows(head, 0, width), at], dscores)
        qkv_t[head_rows(head, 0, width), at] = (
            dot_nt(k_aug[0:64, near], dscores) * scale
        ).astype(BF16)
    qkv_t[head_rows(head, 1, width), :] = (dk[...] * scale).astype(BF16)
    qkv_t[head_rows(head, 2, width), :] = dv[...].astype(BF16)


def gelu_parts(u):
    square = u * u
    bend = jnp.tanh(u * (GELU_A + (GELU_A * GELU_B) * square))
    half = 0.5 + 0.5 * bend
    slope = half + (0.5 * u) * (1.0 - bend * bend) * (GELU_A + (3.0 * GELU_A * GELU_B) * square)
    return u * half, slope


MESH = pl.DeviceIdType.MESH
GROUP = 8

W1X, W1Y, W1C, W1D, W2A, W2B, W2C, W2D = 0, 2, 4, 5, 6, 7, 8, 9
W3X, W3Y, W3C, W3D = 10, 11, 12, 13
GC, GX, GZ, GY, GF = 14, 22, 30, 34, 38
SUM, SUM_STEP = 42, 18
VD, VE = 78, 81
CROSS = 88


def kernel(
    experts,
    tokens, cotangent, segments, live, ln1, ln2, wqkv_in, wattn_in, logits, expert_in, expert_out,
    out, grad_in, in_grad, out_grad, qkv_grad, attn_grad, vectors, logits_grad,
    x, dy, wqkv, wattn, w, a1, qkv_t, ctx_t, lse, mid, a2, dz, hid, dpre, z, total, da2,
    dctx_t, alive_row, mask_q, q_aug, k_aug, v_aug, d_aug, dk, dv,
    rc, rx, rz, ry, fin, part, ac, ay, ae, across, done, vec_dp, vec_ex,
    load_sem, store_sem, send_sem, recv_sem,
):
    length, width = x.shape
    tile = 256
    expert = lax.axis_index("expert")
    dp = lax.axis_index("dp")
    core, row_y = dp % 2, dp // 2
    dp_core = dp + 1 - 2 * core
    dp_y = (dp + 2) % 4
    place = expert % GROUP
    base = expert - place
    mate_core = (expert, dp_core)
    mate_y = (expert, dp_y)
    mate_x = (expert + 1 - 2 * (expert % 2), dp)
    above = ((expert + 2) % experts, dp)
    below = ((expert + experts - 2) % experts, dp)
    groups = experts // GROUP

    def copy(src, dst, index, device):
        return pltpu.make_async_remote_copy(
            src_ref=src, dst_ref=dst, send_sem=send_sem.at[index], recv_sem=recv_sem.at[index],
            device_id=device, device_id_type=MESH,
        )

    def peer(step):
        return (base + (place + step) % GROUP, dp)

    def far(step):
        return ((expert + GROUP * step) % experts, dp)

    barrier = pltpu.get_barrier_semaphore()
    others = [mate_core, mate_y, (expert, (dp_core + 2) % 4)]
    others += [peer(step) for step in range(1, GROUP)]
    if groups > 1:
        others += [above, below] + [far(step) for step in range(1, groups)]
    for other in others:
        pl.semaphore_signal(barrier, inc=1, device_id=other, device_id_type=MESH)

    loads = [
        pltpu.make_async_copy(src, dst, load_sem.at[i])
        for i, (src, dst) in enumerate(
            [
                (expert_in.at[:, pl.ds(0, 512)], w.at[0, 0]),
                (expert_out.at[pl.ds(0, 512), :], w.at[0, 1]),
                (expert_in.at[:, pl.ds(512, 512)], w.at[0, 2]),
                (expert_out.at[pl.ds(512, 512), :], w.at[0, 3]),
                (tokens, x),
                (wqkv_in, wqkv),
                (wattn_in, wattn),
                (cotangent, dy),
            ]
        )
    ]
    for load in loads:
        load.start()
    live_count = live[0]
    alive_row[...] = jnp.where(
        lax.broadcasted_iota(jnp.int32, (1, length), 1) < live_count, 1.0, 0.0
    )
    for_query, for_key, for_key_back = mask_rows(segments[...], live_count, length)
    mask_q[...] = for_query.astype(BF16)
    k_aug[128:144, :] = for_key.astype(BF16)
    v_aug[64:80, :] = jnp.where(
        lax.broadcasted_iota(jnp.int32, (16, length), 0) == 0, 1.0, 0.0
    ).astype(BF16)
    gain1, bias1 = ln1[0:1, :], ln1[1:2, :]
    gain2, bias2 = ln2[0:1, :], ln2[1:2, :]
    exponent = jnp.exp(logits[...] - jnp.max(logits[...], axis=1, keepdims=True))
    gates = exponent / jnp.sum(exponent, axis=1, keepdims=True)

    def half(ref, index, part_index):
        return ref.at[index[0], index[1], pl.ds(256 * part_index, 256), :]

    w1x = [copy(half(w, (0, dp), h), half(w, (1, dp), h), W1X + h, mate_x) for h in range(2)]
    w1y = [copy(half(w, (1, dp), h), half(w, (1, dp), h), W1Y + h, mate_y) for h in range(2)]
    w1c = copy(w.at[1, dp], w.at[1, dp], W1C, mate_core)
    w1d = copy(w.at[1, dp_y], w.at[1, dp_y], W1D, mate_core)
    w2a = copy(w.at[0, dp], w.at[2, dp], W2A, below)
    w2b = copy(w.at[0, dp_y], w.at[2, dp_y], W2B, below)
    w2c = copy(w.at[2, dp], w.at[2, dp], W2C, mate_core)
    w2d = copy(w.at[2, dp_y], w.at[2, dp_y], W2D, mate_core)
    w3x = copy(w.at[2, dp], w.at[3, dp], W3X, mate_x)
    w3y = copy(w.at[3, dp], w.at[3, dp], W3Y, mate_y)
    w3c = copy(w.at[3, dp], w.at[3, dp], W3C, mate_core)
    w3d = copy(w.at[3, dp_y], w.at[3, dp_y], W3D, mate_core)

    for load in loads[:4]:
        load.wait()
    pl.semaphore_wait(barrier, len(others))
    w1x[0].start()
    w2a.start()
    w1x[1].start()

    loads[4].wait()
    for start in range(0, length, tile):
        at = pl.ds(start, tile)
        normal, inverse = norm_parts(x[at, :].astype(F32))
        a1[at, :] = (normal * gain1 + bias1).astype(BF16)
    loads[5].wait()
    for start in range(0, 3 * width, 512):
        at = pl.ds(start, 512)
        qkv_t[at, :] = dot_tt(wqkv[:, at], a1[...]).astype(BF16)

    def forward_heads(pair, carry):
        @pl.when(pair == 1)
        def _():
            w2b.start()

        @pl.when(pair == 2)
        def _():
            w1x[0].wait_recv()
            w1y[0].start()

        @pl.when(pair == 3)
        def _():
            w2a.wait_recv()
            w3x.start()
            w1x[1].wait_recv()
            w1y[1].start()
            w1c.start()

        for head in range(2):
            attend_forward(
                2 * pair + head, qkv_t, ctx_t, lse, mask_q, alive_row, q_aug, k_aug, v_aug, length
            )
        return carry

    lax.fori_loop(0, width // HEAD_DIM // 2, forward_heads, 0)

    loads[6].wait()
    loads[7].wait()
    for start in range(0, length, tile):
        at = pl.ds(start, tile)
        middle = x[at, :].astype(F32) + dot_tn(ctx_t[:, at], wattn[...])
        mid[at, :] = middle
        normal, inverse = norm_parts(middle)
        a2[at, :] = (normal * gain2 + bias2).astype(BF16)
        alive = start + lax.broadcasted_iota(jnp.int32, (tile, 1), 0) < live_count
        dy[at, :] = jnp.where(alive, dy[at, :], jnp.zeros((), BF16))
    da2[...] = jnp.zeros(da2.shape, F32)

    def add_into(target, *terms):
        value = target[...].astype(F32)
        for term in terms:
            value = value + term[...].astype(F32)
        target[...] = value.astype(BF16)

    def gc(slot, chunk):
        return copy(
            w.at[slot, 2 * chunk + 1 - core], rc.at[slot, chunk], GC + 2 * slot + chunk, mate_core
        )

    def add_core(slot):
        for chunk in range(2):
            gc(slot, chunk).wait_recv()
            add_into(w.at[slot, 2 * chunk + core], rc.at[slot, chunk])

    def piece(ref, slot, index):
        chunk, part_index = index // 2, index % 2
        return ref.at[slot, 2 * chunk + core, pl.ds(256 * part_index, 256), :]

    def landed(ref, index):
        return ref.at[index // 2, pl.ds(256 * (index % 2), 256), :]

    gx = [
        [copy(piece(w, 2 * s + 1, i), landed(rx.at[s], i), GX + 4 * s + i, mate_x) for i in range(4)]
        for s in range(2)
    ]
    gz = [copy(piece(w, 2, i), landed(rz, i), GZ + i, above) for i in range(4)]
    gy = [copy(piece(w, 0, i), landed(ry, i), GY + i, mate_y) for i in range(4)]

    def final(index):
        chunk, part_index = index // 2, index % 2
        return fin.at[2 * chunk + core, pl.ds(256 * part_index, 256), :]

    gf = [copy(final(i), final(i), GF + i, mate_core) for i in range(4)]

    def one_slot(slot, carry):
        gate = jnp.where(slot < 2, gates[:, 0:1], gates[:, 1:2])

        @pl.when(slot == 1)
        def _():
            w1y[0].wait_recv()
            w1y[1].wait_recv()
            w1d.start()
            w3x.wait_recv()
            w3y.start()
            w3c.start()
            w1c.wait_recv()
            w1d.wait_recv()

        @pl.when(slot == 2)
        def _():
            w2b.wait_recv()
            w2d.start()
            w2c.start()
            w2c.wait_recv()
            w2d.wait_recv()

        @pl.when(slot == 3)
        def _():
            w3c.wait_recv()
            w3d.wait_recv()

        @pl.when(slot % 2 == 0)
        def _():
            for start in range(0, length, tile):
                at = pl.ds(start, tile)
                dz[at, :] = (gate * dy[at, :].astype(F32)).astype(BF16)
            z[...] = jnp.zeros(z.shape, F32)

        for chunk in range(2):
            w_in, w_out = w.at[slot, 2 * chunk], w.at[slot, 2 * chunk + 1]
            for start in range(0, length, 512):
                at = pl.ds(start, 512)
                hidden, slope = gelu_parts(dot_nn(a2[at, :], w_in[...]))
                hid[chunk, at, :] = hidden.astype(BF16)
                dpre[chunk, at, :] = (dot_nt(dz[at, :], w_out[...]) * slope).astype(BF16)
                z[at, :] += dot_nn(hid[chunk, at, :], w_out[...])
                da2[at, :] += dot_nt(dpre[chunk, at, :], w_in[...])

        @pl.when(slot == 0)
        def _():
            for each in w1x + [w2a, w2b]:
                each.wait_send()

        @pl.when(slot == 1)
        def _():
            for each in w1y + [w1c, w1d]:
                each.wait_send()
            add_core(0)

        @pl.when(slot == 2)
        def _():
            for each in [w3x, w2c, w2d]:
                each.wait_send()
            w3y.wait_recv()
            w3d.start()
            add_core(1)
            for each in gx[0]:
                each.start()

        @pl.when(slot == 3)
        def _():
            for each in [w3y, w3c, w3d]:
                each.wait_send()
            add_core(2)

        for chunk in range(2):
            w[slot, 2 * chunk] = dot_tn(a2[...], dpre[chunk]).astype(BF16)
            w[slot, 2 * chunk + 1] = dot_tn(hid[chunk], dz[...]).astype(BF16)
            gc(slot, chunk).start()

        @pl.when(slot % 2 == 1)
        def _():
            gate_grad = jnp.zeros((1, width), F32)
            for start in range(0, length, tile):
                at = pl.ds(start, tile)
                branch = z[at, :]
                gate_grad += jnp.sum(dy[at, :].astype(F32) * branch, axis=0, keepdims=True)
                previous = jnp.where(slot == 1, mid[at, :], total[at, :])
                total[at, :] = previous + gate * branch
            vectors[pl.ds(4, 1), :] = jnp.where(slot == 1, gate_grad, vectors[pl.ds(4, 1), :])
            vectors[pl.ds(5, 1), :] = gate_grad

        return carry

    lax.fori_loop(0, 4, one_slot, 0)
    dz[...] = total[...].astype(BF16)
    stores = [pltpu.make_async_copy(dz, out, store_sem.at[0])]
    stores[0].start()

    gain_sum = jnp.zeros((1, width), F32)
    bias_sum = jnp.zeros((1, width), F32)
    for start in range(0, length, tile):
        at = pl.ds(start, tile)
        normal, inverse = norm_parts(mid[at, :])
        grad = da2[at, :]
        gain_sum += jnp.sum(grad * normal, axis=0, keepdims=True)
        bias_sum += jnp.sum(grad, axis=0, keepdims=True)
        dmid = dy[at, :].astype(F32) + norm_back(grad * gain2, normal, inverse)
        mid[at, :] = dmid
        a2[at, :] = dmid.astype(BF16)
    vectors[2:3, :] = gain_sum
    vectors[3:4, :] = bias_sum
    vectors[6:8, :] = jnp.zeros((2, width), F32)
    add_core(3)
    for each in gx[1]:
        each.start()
    for block in range(2):
        part[block] = dot_nn(ctx_t[...], a2[:, 256 * block : 256 * block + 256]).astype(BF16)
    dctx_t[...] = dot_nt(wattn[...], a2[...]).astype(BF16)

    def sum_round(index, low, high):
        blocks = pl.ds(low, high - low)
        first = SUM + SUM_STEP * index
        own_half = pl.ds(pl.multiple_of(256 * core, 256), 256)
        other_half = pl.ds(pl.multiple_of(256 * (1 - core), 256), 256)
        corner = 256 * core + 128 * row_y
        own_quarter = pl.ds(pl.multiple_of(corner, 128), 128)
        other_quarter = pl.ds(pl.multiple_of(256 * core + 128 * (1 - row_y), 128), 128)

        def rows(step):
            return pl.ds(pl.multiple_of(corner + 16 * ((place + step) % GROUP), 16), 16)

        to_core = copy(part.at[blocks, other_half, :], ac.at[blocks], first, mate_core)
        to_y = copy(part.at[blocks, other_quarter, :], ay.at[blocks], first + 1, mate_y)
        spread = [
            copy(part.at[blocks, rows(s), :], ae.at[s, blocks], first + 1 + s, peer(s))
            for s in range(1, GROUP)
        ]
        gather = [
            copy(done.at[blocks, rows(0), :], done.at[blocks, rows(0), :], first + 8 + s, peer(s))
            for s in range(1, GROUP)
        ]
        back_y = copy(done.at[blocks, own_quarter, :], done.at[blocks, own_quarter, :], first + 16, mate_y)
        back_core = copy(done.at[blocks, own_half, :], done.at[blocks, own_half, :], first + 17, mate_core)
        over = [
            copy(across.at[0, blocks], across.at[s, blocks], CROSS + (groups - 1) * index + s - 1, far(s))
            for s in range(1, groups)
        ]

        def step_core():
            to_core.start()

        def step_y():
            to_core.wait_recv()
            add_into(part.at[blocks, own_half, :], ac.at[blocks])
            to_y.start()

        def step_spread():
            to_y.wait_recv()
            add_into(part.at[blocks, own_quarter, :], ay.at[blocks])
            for each in spread:
                each.start()

        def step_gather():
            for each in spread:
                each.wait_recv()
            value = part[blocks, rows(0), :].astype(F32)
            for s in range(1, GROUP):
                value = value + ae[s, blocks].astype(F32)
            if groups > 1:
                across[0, blocks] = value.astype(BF16)
                for each in over:
                    each.start()
                for each in over:
                    each.wait_recv()
                value = jnp.zeros(value.shape, F32)

                def add_group(group, value):
                    step = (expert // GROUP - group + groups) % groups
                    return value + across[step, blocks].astype(F32)

                value = lax.fori_loop(0, groups, add_group, value)
            done[blocks, rows(0), :] = value.astype(BF16)
            for each in gather:
                each.start()

        def step_back_y():
            for each in gather:
                each.wait_recv()
            back_y.start()

        def step_back_core():
            back_y.wait_recv()
            back_core.start()

        def step_end():
            back_core.wait_recv()

        def finish():
            for each in [to_core, to_y, back_y, back_core] + spread + gather + over:
                each.wait_send()

        return step_core, step_y, step_spread, step_gather, step_back_y, step_back_core, step_end, finish

    round_a = sum_round(0, 0, 5)
    round_b = sum_round(1, 5, 8)

    k_aug[128:144, :] = for_key_back.astype(BF16)
    v_aug[64:80, :] = jnp.where(
        lax.broadcasted_iota(jnp.int32, (16, length), 0) < 3, 1.0, 0.0
    ).astype(BF16)

    def qkv_blocks(first, offset):
        for index in range(3):
            at = pl.ds(index * width + offset, 256)
            part[first + index] = dot_tt(a1[...], qkv_t[at, :]).astype(BF16)

    def pass_on_z(index):
        gx[1][index].wait_recv()
        add_into(piece(w, 2, index), landed(rx.at[1], index))
        gz[index].start()

    def pass_on_y(index):
        gz[index].wait_recv()
        add_into(piece(w, 0, index), landed(rz, index))
        gy[index].start()

    def pass_on_core(index):
        gy[index].wait_recv()
        final(index)[...] = (
            piece(w, 0, index)[...].astype(F32) + landed(ry, index)[...].astype(F32)
        ).astype(BF16)
        gf[index].start()

    def backward_heads(pair, carry):
        @pl.when(pair == 2)
        def _():
            qkv_blocks(2, 0)
            round_a[0]()
            for index in range(4):
                gx[0][index].wait_recv()
                add_into(piece(w, 0, index), landed(rx.at[0], index))

        @pl.when(pair == 3)
        def _():
            round_a[1]()
            pass_on_z(0)

        for head in range(2):
            attend_backward(
                2 * pair + head, qkv_t, dctx_t, ctx_t, lse, mask_q, q_aug, k_aug, v_aug, d_aug,
                dk, dv, tile,
            )
        return carry

    lax.fori_loop(0, width // HEAD_DIM // 2, backward_heads, 0)
    qkv_blocks(5, 256)
    round_b[0]()
    round_a[2]()
    pass_on_z(1)

    gain_sum = jnp.zeros((1, width), F32)
    bias_sum = jnp.zeros((1, width), F32)
    for start in range(0, length, tile):
        at = pl.ds(start, tile)
        grad = dot_tt(qkv_t[:, at], wqkv[...])
        normal, inverse = norm_parts(x[at, :].astype(F32))
        gain_sum += jnp.sum(grad * normal, axis=0, keepdims=True)
        bias_sum += jnp.sum(grad, axis=0, keepdims=True)
        a2[at, :] = (mid[at, :] + norm_back(grad * gain1, normal, inverse)).astype(BF16)
        if start == tile:
            round_b[1]()
            round_a[3]()
            pass_on_z(2)
    stores.append(pltpu.make_async_copy(a2, grad_in, store_sem.at[1]))
    stores[1].start()
    lane = lax.broadcasted_iota(jnp.int32, (1, width), 1)
    vectors[0:1, :] = gain_sum
    vectors[1:2, :] = bias_sum

    vec_dp[dp] = vectors[...]
    to_dp = [
        copy(vec_dp.at[dp], vec_dp.at[dp], VD + s - 1, (expert, (dp + s) % 4)) for s in range(1, 4)
    ]
    for each in to_dp:
        each.start()
    round_b[2]()
    pass_on_z(3)
    pass_on_y(0)
    for each in to_dp:
        each.wait_recv()
    row_sum = vec_dp[0] + vec_dp[1] + vec_dp[2] + vec_dp[3]
    vec_ex[expert] = row_sum
    to_ex = [
        copy(vec_ex.at[expert], vec_ex.at[expert], VE + s - 1, peer(s)) for s in range(1, GROUP)
    ]
    for each in to_ex:
        each.start()
    gate_sums = jnp.sum(row_sum[4:6, :], axis=1, keepdims=True)
    pair_lane = lax.broadcasted_iota(jnp.int32, (1, 2), 1)
    dgate = jnp.where(pair_lane == 0, gate_sums[0:1, :], gate_sums[1:2, :])
    logits_grad[...] = gates * (dgate - jnp.sum(gates * dgate, axis=1, keepdims=True))

    round_a[4]()
    pass_on_y(1)
    round_b[3]()
    pass_on_y(2)
    round_a[5]()
    pass_on_core(0)
    pass_on_y(3)
    round_b[4]()
    pass_on_core(1)
    for each in to_ex:
        each.wait_recv()
    sums = [to_dp, to_ex]
    if groups > 1:
        vec_group = vec_ex[base]
        for s in range(1, GROUP):
            vec_group = vec_group + vec_ex[base + s]
        vec_ex[experts + expert // GROUP] = vec_group
        to_far = [
            copy(
                vec_ex.at[experts + expert // GROUP], vec_ex.at[experts + expert // GROUP],
                CROSS + 2 * (groups - 1) + s - 1, far(s),
            )
            for s in range(1, groups)
        ]
        for each in to_far:
            each.start()
        for each in to_far:
            each.wait_recv()
        sums.append(to_far)
        value = vec_ex[experts]
        for s in range(1, groups):
            value = value + vec_ex[experts + s]
    else:
        value = vec_ex[0]
        for s in range(1, GROUP):
            value = value + vec_ex[s]
    vectors[...] = value
    pass_on_core(2)
    round_a[6]()
    for block in range(5):
        if block < 2:
            target = attn_grad.at[:, pl.ds(256 * block, 256)]
        else:
            target = qkv_grad.at[:, pl.ds((block - 2) * width, 256)]
        stores.append(pltpu.make_async_copy(done.at[block], target, store_sem.at[2 + block]))
        stores[-1].start()
    round_b[5]()
    pass_on_core(3)
    round_b[6]()
    for block in range(3):
        target = qkv_grad.at[:, pl.ds(block * width + 256, 256)]
        stores.append(pltpu.make_async_copy(done.at[5 + block], target, store_sem.at[7 + block]))
        stores[-1].start()
    for each in gf:
        each.wait_recv()
    for chunk in range(2):
        at = pl.ds(512 * chunk, 512)
        for kind, target in enumerate([in_grad.at[:, at], out_grad.at[at, :]]):
            index = 2 * chunk + kind
            stores.append(pltpu.make_async_copy(fin.at[index], target, store_sem.at[10 + index]))
            stores[-1].start()
    for slot in range(4):
        for chunk in range(2):
            gc(slot, chunk).wait_send()
    for group in [gx[0], gx[1], gz, gy, gf] + sums:
        for each in group:
            each.wait_send()
    round_a[7]()
    round_b[7]()
    for store in stores:
        store.wait()


def one_device(
    experts, tokens, cotangent, segments, live, ln1, ln2, wqkv, wattn, logits, expert_in, expert_out
):
    length, width = tokens.shape
    groups = experts // GROUP
    vmem = pl.BlockSpec(memory_space=pltpu.VMEM)
    smem = pl.BlockSpec(memory_space=pltpu.SMEM)
    hbm = pl.BlockSpec(memory_space=pl.ANY)
    shape = jax.ShapeDtypeStruct
    semaphores = CROSS + 3 * (groups - 1)
    scratch = [
        pltpu.VMEM((length, width), BF16),
        pltpu.VMEM((length, width), BF16),
        pltpu.VMEM(wqkv.shape, BF16),
        pltpu.VMEM(wattn.shape, BF16),
        pltpu.VMEM((4, 4, 512, 512), BF16),
        pltpu.VMEM((length, width), BF16),
        pltpu.VMEM((3 * width, length), BF16),
        pltpu.VMEM((width, length), BF16),
        pltpu.VMEM((width // HEAD_DIM, 1, length), F32),
        pltpu.VMEM((length, width), F32),
        pltpu.VMEM((length, width), BF16),
        pltpu.VMEM((length, width), BF16),
        pltpu.VMEM((2, length, 512), BF16),
        pltpu.VMEM((2, length, 512), BF16),
        pltpu.VMEM((length, width), F32),
        pltpu.VMEM((length, width), F32),
        pltpu.VMEM((length, width), F32),
        pltpu.VMEM((width, length), BF16),
        pltpu.VMEM((1, length), F32),
        pltpu.VMEM((16, length), BF16),
        pltpu.VMEM((144, length), BF16),
        pltpu.VMEM((144, length), BF16),
        pltpu.VMEM((80, length), BF16),
        pltpu.VMEM((80, length), BF16),
        pltpu.VMEM((HEAD_DIM, length), F32),
        pltpu.VMEM((HEAD_DIM, length), F32),
        pltpu.VMEM((4, 2, 512, 512), BF16),
        pltpu.VMEM((2, 2, 512, 512), BF16),
        pltpu.VMEM((2, 512, 512), BF16),
        pltpu.VMEM((2, 512, 512), BF16),
        pltpu.VMEM((4, 512, 512), BF16),
        pltpu.VMEM((8, 512, 256), BF16),
        pltpu.VMEM((8, 256, 256), BF16),
        pltpu.VMEM((8, 128, 256), BF16),
        pltpu.VMEM((GROUP, 8, 16, 256), BF16),
        pltpu.VMEM((groups, 8, 16, 256), BF16),
        pltpu.VMEM((8, 512, 256), BF16),
        pltpu.VMEM((4, 8, width), F32),
        pltpu.VMEM((experts + groups, 8, width), F32),
        pltpu.SemaphoreType.DMA((8,)),
        pltpu.SemaphoreType.DMA((14,)),
        pltpu.SemaphoreType.DMA((semaphores,)),
        pltpu.SemaphoreType.DMA((semaphores,)),
    ]
    return pl.pallas_call(
        functools.partial(kernel, experts),
        in_specs=[hbm, hbm, vmem, smem, vmem, vmem, hbm, hbm, vmem, hbm, hbm],
        out_specs=[hbm] * 6 + [vmem] * 2,
        out_shape=[
            shape(tokens.shape, BF16),
            shape(tokens.shape, BF16),
            shape(expert_in.shape, BF16),
            shape(expert_out.shape, BF16),
            shape(wqkv.shape, BF16),
            shape(wattn.shape, BF16),
            shape((8, width), F32),
            shape((1, 2), F32),
        ],
        scratch_shapes=scratch,
        compiler_params=pltpu.CompilerParams(
            vmem_limit_bytes=63 * 1024 * 1024, collective_id=0, has_side_effects=True
        ),
    )(tokens, cotangent, segments, live, ln1, ln2, wqkv, wattn, logits, expert_in, expert_out)


def body(
    tokens, segment_ids, live_tokens, cotangent, ln1_gain, ln1_bias, qkv_weight, attn_weight,
    ln2_gain, ln2_bias, task_logits, expert_in, expert_out,
):
    ln1 = jnp.stack([ln1_gain, ln1_bias]).astype(F32)
    ln2 = jnp.stack([ln2_gain, ln2_bias]).astype(F32)
    out, grad_in, in_grad, out_grad, qkv_grad, attn_grad, vectors, logits_grad = one_device(
        lax.axis_size("expert"), tokens[0], cotangent[0], segment_ids, live_tokens, ln1, ln2,
        qkv_weight, attn_weight, task_logits, expert_in[0], expert_out[0],
    )
    return (
        out[None], grad_in[None], vectors[0], vectors[1], qkv_grad.astype(F32),
        attn_grad.astype(F32), vectors[2], vectors[3], logits_grad,
        in_grad.astype(F32)[None], out_grad.astype(F32)[None],
    )


def solution(mesh):
    rows = ("expert", "dp")
    in_specs = (
        P(rows, None, None), P(rows, None), P(rows), P(rows, None, None), P(), P(), P(), P(), P(), P(),
        P("expert", None), P("expert", None, None), P("expert", None, None),
    )
    out_specs = (
        P(rows, None, None), P(rows, None, None), P(), P(), P(), P(), P(), P(),
        P("expert", None), P("expert", None, None), P("expert", None, None),
    )
    return jax.shard_map(body, mesh=mesh, in_specs=in_specs, out_specs=out_specs, check_vma=False)
```

```python
import functools

import jax
import jax.numpy as jnp
from jax import lax
from jax.experimental import pallas as pl
from jax.experimental.pallas import tpu as pltpu
from jax.sharding import PartitionSpec as P

F32 = jnp.float32
BF16 = jnp.bfloat16
HEAD_DIM = 64
NORM_EPS = 1e-05
MASKED = -1e30
LOG2E = 1.4426950408889634
GELU_A = 0.7978845608028654
GELU_B = 0.044715


def dot_nn(a, b):
    return jnp.dot(a, b, preferred_element_type=F32)


def dot_nt(a, b):
    return lax.dot_general(a, b, (((1,), (1,)), ((), ())), preferred_element_type=F32)


def dot_tn(a, b):
    return lax.dot_general(a, b, (((0,), (0,)), ((), ())), preferred_element_type=F32)


def dot_tt(a, b):
    return lax.dot_general(a, b, (((0,), (1,)), ((), ())), preferred_element_type=F32)


def norm_parts(inputs):
    row_mean = jnp.mean(inputs, axis=-1, keepdims=True)
    centred = inputs - row_mean
    variance = jnp.mean(centred * centred, axis=-1, keepdims=True)
    inverse = lax.rsqrt(variance + NORM_EPS)
    return centred * inverse, inverse


def norm_back(scaled, normal, inverse):
    return inverse * (
        scaled
        - jnp.mean(scaled, axis=-1, keepdims=True)
        - normal * jnp.mean(scaled * normal, axis=-1, keepdims=True)
    )


def split_three(value):
    high = value.astype(BF16)
    rest = value - high.astype(F32)
    middle = rest.astype(BF16)
    low = (rest - middle.astype(F32)).astype(BF16)
    return high.astype(F32), middle.astype(F32), low.astype(F32)


def scaled_queries(queries):
    scaled = queries.astype(F32) * (LOG2E * HEAD_DIM ** (-0.5))
    high = scaled.astype(BF16)
    return high, (scaled - high.astype(F32)).astype(BF16)


def mask_rows(segments, live, length):
    position = lax.broadcasted_iota(jnp.int32, (16, length), 1)
    row = lax.broadcasted_iota(jnp.int32, (16, length), 0)
    segment = jnp.broadcast_to(segments, (16, length))
    alive = position < live
    for_query = jnp.where(
        row < 8,
        jnp.where(segment != row, MASKED, 0.0),
        jnp.where((row == 8) & alive, MASKED, 0.0),
    )
    for_key = jnp.where(
        row < 8,
        jnp.where(segment == row, 1.0, 0.0),
        jnp.where((row == 8) & (~alive), 1.0, 0.0),
    )
    for_key_back = jnp.where((row >= 9) & (row < 12), 1.0, for_key)
    return for_query, for_key, for_key_back


def head_rows(head, part, width):
    return pl.ds(pl.multiple_of(part * width + head * HEAD_DIM, HEAD_DIM), HEAD_DIM)


def key_band(start, size, tile, length):
    low = max(0, (start - 511) // tile * tile)
    high = min(length, -(-(start + size + 511) // tile) * tile)
    return low, high


def attend_forward(head, qkv_t, ctx_t, lse, mask_q, alive_row, q_aug, k_aug, v_aug, tile):
    width, length = ctx_t.shape
    high, low = scaled_queries(qkv_t[head_rows(head, 0, width), :])
    q_aug[0:64, :] = high
    q_aug[64:128, :] = low
    q_aug[128:144, :] = mask_q[...]
    keys = qkv_t[head_rows(head, 1, width), :]
    k_aug[0:64, :] = keys
    k_aug[64:128, :] = keys
    v_aug[0:64, :] = qkv_t[head_rows(head, 2, width), :]
    for start in range(0, length, tile):
        at = pl.ds(start, tile)
        scores = dot_tn(k_aug[...], q_aug[:, at])
        top = jnp.max(scores, axis=0, keepdims=True)
        weights = jnp.exp2(scores - top).astype(BF16)
        summed = dot_nn(v_aug[...], weights)
        total = summed[64:65, :]
        context = summed[0:64, :] * (1.0 / total)
        own = v_aug[0:64, at].astype(F32)
        ctx_t[head_rows(head, 0, width), at] = jnp.where(
            alive_row[:, at] > 0, context, own
        ).astype(BF16)
        lse[head, :, at] = top + jnp.log(total) * LOG2E


def attend_backward(head, qkv_t, dctx_t, ctx_t, lse, mask_q, q_aug, k_aug, v_aug, d_aug, dk, dv, tile):
    width, length = ctx_t.shape
    scale = HEAD_DIM ** (-0.5)
    row = lax.broadcasted_iota(jnp.int32, (16, length), 0)
    high, low = scaled_queries(qkv_t[head_rows(head, 0, width), :])
    q_aug[0:64, :] = high
    q_aug[64:128, :] = low
    one, two, three = split_three(-lse[head])
    q_aug[128:144, :] = jnp.where(
        row == 9, one, jnp.where(row == 10, two, jnp.where(row == 11, three, mask_q[...].astype(F32)))
    ).astype(BF16)
    keys = qkv_t[head_rows(head, 1, width), :]
    k_aug[0:64, :] = keys
    k_aug[64:128, :] = keys
    v_aug[0:64, :] = qkv_t[head_rows(head, 2, width), :]
    grad = dctx_t[head_rows(head, 0, width), :]
    d_aug[0:64, :] = grad
    context = ctx_t[head_rows(head, 0, width), :].astype(F32)
    one, two, three = split_three(
        -jnp.sum(grad.astype(F32) * context, axis=0, keepdims=True)
    )
    d_aug[64:80, :] = jnp.where(
        row == 0, one, jnp.where(row == 1, two, jnp.where(row == 2, three, 0.0))
    ).astype(BF16)
    dk[...] = jnp.zeros(dk.shape, F32)
    dv[...] = jnp.zeros(dv.shape, F32)
    for start in range(0, length, tile):
        first, last = key_band(start, tile, tile, length)
        at, near = pl.ds(start, tile), pl.ds(first, last - first)
        weights = jnp.exp2(dot_tn(q_aug[:, at], k_aug[:, near]))
        dweights = dot_tn(d_aug[:, at], v_aug[:, near])
        dscores = (weights * dweights).astype(BF16)
        dv[:, near] += dot_nn(d_aug[0:64, at], weights.astype(BF16))
        dk[:, near] += dot_nn(qkv_t[head_rows(head, 0, width), at], dscores)
        qkv_t[head_rows(head, 0, width), at] = (
            dot_nt(k_aug[0:64, near], dscores) * scale
        ).astype(BF16)
    qkv_t[head_rows(head, 1, width), :] = (dk[...] * scale).astype(BF16)
    qkv_t[head_rows(head, 2, width), :] = dv[...].astype(BF16)


def gelu_parts(u):
    square = u * u
    bend = jnp.tanh(u * (GELU_A + (GELU_A * GELU_B) * square))
    half = 0.5 + 0.5 * bend
    slope = half + (0.5 * u) * (1.0 - bend * bend) * (GELU_A + (3.0 * GELU_A * GELU_B) * square)
    return u * half, slope


MESH = pl.DeviceIdType.MESH
GROUP = 8


class Numbers:
    def __init__(self):
        self.used = 0

    def take(self, count):
        first = self.used
        self.used += count
        return first


def number_copies(groups):
    numbers = Numbers()
    names = {}
    for name, count in [
        ("w1x", 2), ("w1y", 2), ("w1c", 1), ("w1d", 2), ("w2a", 2), ("w2b", 2), ("w2c", 1), ("w2d", 1),
        ("w3x", 2), ("w3y", 2), ("w3c", 1), ("w3d", 2), ("gc", 8), ("g1", 4), ("g3y", 2), ("g3x", 2),
        ("gzu", 2), ("gzm", 2), ("gyr", 2), ("gya", 2), ("gfa", 2), ("gfb", 2),
        ("vec_dp", 3), ("vec_ex", GROUP - 1), ("vec_far", groups - 1),
    ]:
        names[name] = numbers.take(count)
    for index in range(4):
        names["sum", index] = numbers.take(4 + 2 * (2 * GROUP - 1) + groups - 1)
    return names, numbers.used


ROUNDS = (896, 384, 384, 384)


def kernel(
    experts,
    tokens, cotangent, segments, live, ln1_gain, ln1_bias, ln2_gain, ln2_bias, wqkv_in, wattn_in, logits,
    expert_in, expert_out,
    out, grad_in, in_grad, out_grad, qkv_grad, attn_grad, vectors, logits_grad,
    x, dy, wqkv, wattn, w, a1, qkv_t, ctx_t, lse, mid, a2, dz, hid, dpre, total, da2,
    dctx_t, alive_row, mask_q, q_aug, k_aug, v_aug, d_aug, dk, dv, gate_sum,
    rc, r1, r3y, r3x, rz, ryr, fin, part, ac, ay, ae, across, done, vec_dp, vec_ex,
    load_sem, store_sem, send_sem, recv_sem,
):
    length, width = x.shape
    tile = 256
    groups = experts // GROUP
    names, _ = number_copies(groups)
    expert = lax.axis_index("expert")
    dp = lax.axis_index("dp")
    core, row_y = dp % 2, dp // 2
    dp_core = dp + 1 - 2 * core
    dp_y = (dp + 2) % 4
    place = expert % GROUP
    base = expert - place
    mate_core = (expert, dp_core)
    mate_y = (expert, dp_y)
    mate_x = (expert + 1 - 2 * (expert % 2), dp)
    above = ((expert + 2) % experts, dp)
    below = ((expert + experts - 2) % experts, dp)

    def copy(src, dst, index, device):
        return pltpu.make_async_remote_copy(
            src_ref=src, dst_ref=dst, send_sem=send_sem.at[index], recv_sem=recv_sem.at[index],
            device_id=device, device_id_type=MESH,
        )

    def peer(step):
        return (base + (place + step) % GROUP, dp)

    def peer_y(step):
        return (base + (place + step) % GROUP, dp_y)

    def far(step):
        return ((expert + GROUP * step) % experts, dp)

    barrier = pltpu.get_barrier_semaphore()
    others = [mate_core, mate_y, mate_x, above, below] + [far(step) for step in range(1, groups)]
    for other in others:
        pl.semaphore_signal(barrier, inc=1, device_id=other, device_id_type=MESH)

    loads = [
        pltpu.make_async_copy(src, dst, load_sem.at[i])
        for i, (src, dst) in enumerate(
            [
                (expert_in.at[:, pl.ds(0, 512)], w.at[0, 0]),
                (expert_out.at[pl.ds(0, 512), :], w.at[0, 1]),
                (expert_in.at[:, pl.ds(512, 512)], w.at[0, 2]),
                (expert_out.at[pl.ds(512, 512), :], w.at[0, 3]),
                (tokens, x),
                (wqkv_in, wqkv),
                (wattn_in, wattn),
                (cotangent, dy),
            ]
        )
    ]
    for load in loads:
        load.start()
    live_count = live[0]
    alive_row[...] = jnp.where(
        lax.broadcasted_iota(jnp.int32, (1, length), 1) < live_count, 1.0, 0.0
    )
    for_query, for_key, for_key_back = mask_rows(segments[...], live_count, length)
    mask_q[...] = for_query.astype(BF16)
    k_aug[128:144, :] = for_key.astype(BF16)
    v_aug[64:80, :] = jnp.where(
        lax.broadcasted_iota(jnp.int32, (16, length), 0) == 0, 1.0, 0.0
    ).astype(BF16)
    gain1, bias1, gain2, bias2 = (
        ref[...].astype(F32).reshape(1, width) for ref in (ln1_gain, ln1_bias, ln2_gain, ln2_bias)
    )
    exponent = jnp.exp(logits[...] - jnp.max(logits[...], axis=1, keepdims=True))
    gates = exponent / jnp.sum(exponent, axis=1, keepdims=True)

    def halves(name, slot, unit, to_slot, device):
        return [
            copy(
                w.at[slot, unit, pl.ds(256 * h, 256), :], w.at[to_slot, unit, pl.ds(256 * h, 256), :],
                names[name] + h, device,
            )
            for h in range(2)
        ]

    w1x = halves("w1x", 0, dp, 1, mate_x)
    w1y = halves("w1y", 1, dp, 1, mate_y)
    w1d = halves("w1d", 1, dp_y, 1, mate_core)
    w1c = copy(w.at[1, dp], w.at[1, dp], names["w1c"], mate_core)
    w2a = halves("w2a", 0, dp, 2, below)
    w2b = halves("w2b", 0, dp_y, 2, below)
    w2c = copy(w.at[2, dp], w.at[2, dp], names["w2c"], mate_core)
    w2d = copy(w.at[2, dp_y], w.at[2, dp_y], names["w2d"], mate_core)
    w3x = halves("w3x", 2, dp, 3, mate_x)
    w3y = halves("w3y", 3, dp, 3, mate_y)
    w3d = halves("w3d", 3, dp_y, 3, mate_core)
    w3c = copy(w.at[3, dp], w.at[3, dp], names["w3c"], mate_core)

    for load in loads[:4]:
        load.wait()
    pl.semaphore_wait(barrier, len(others))
    for h in range(2):
        w1x[h].start()
        w2a[h].start()
    for h in range(2):
        w2b[h].start()

    loads[4].wait()
    for start in range(0, length, tile):
        at = pl.ds(start, tile)
        normal, inverse = norm_parts(x[at, :].astype(F32))
        a1[at, :] = (normal * gain1 + bias1).astype(BF16)
    loads[5].wait()
    for start in range(0, 3 * width, 512):
        at = pl.ds(start, 512)
        qkv_t[at, :] = dot_tt(wqkv[:, at], a1[...]).astype(BF16)

    def forward_heads(pair, carry):
        @pl.when(pair == 2)
        def _():
            w1x[0].wait_recv()
            w1y[0].start()
            w2a[0].wait_recv()
            w3x[0].start()

        for head in range(2):
            attend_forward(
                2 * pair + head, qkv_t, ctx_t, lse, mask_q, alive_row, q_aug, k_aug, v_aug, length
            )
        return carry

    lax.fori_loop(0, width // HEAD_DIM // 2, forward_heads, 0)
    w1x[1].wait_recv()
    w1y[1].start()
    w1c.start()
    w2a[1].wait_recv()
    w3x[1].start()
    w2c.start()

    loads[6].wait()
    loads[7].wait()
    for start in range(0, length, tile):
        at = pl.ds(start, tile)
        middle = x[at, :].astype(F32) + dot_tn(ctx_t[:, at], wattn[...])
        mid[at, :] = middle
        total[at, :] = middle
        normal, inverse = norm_parts(middle)
        a2[at, :] = (normal * gain2 + bias2).astype(BF16)
        alive = start + lax.broadcasted_iota(jnp.int32, (tile, 1), 0) < live_count
        live_dy = jnp.where(alive, dy[at, :], jnp.zeros((), BF16))
        dy[at, :] = live_dy
        for k in range(2):
            dz[k, at, :] = (gates[:, k : k + 1] * live_dy.astype(F32)).astype(BF16)
    da2[...] = jnp.zeros(da2.shape, F32)
    gate_sum[...] = jnp.zeros(gate_sum.shape, F32)

    def add_into(target, *terms):
        value = target[...].astype(F32)
        for term in terms:
            value = value + term[...].astype(F32)
        target[...] = value.astype(BF16)

    own_rows = pl.ds(pl.multiple_of(256 * row_y, 256), 256)
    other_rows = pl.ds(pl.multiple_of(256 * (1 - row_y), 256), 256)

    def unit(slot, chunk, rows=pl.ds(0, 512)):
        return w.at[slot, 2 * chunk + core, rows, :]

    def gc(slot, chunk):
        return copy(
            w.at[slot, 2 * chunk + 1 - core], rc.at[slot, chunk], names["gc"] + 2 * slot + chunk, mate_core
        )

    def add_core(slot, chunk):
        gc(slot, chunk).wait_recv()
        add_into(unit(slot, chunk), rc.at[slot, chunk])

    def g1(chunk, h):
        rows = pl.ds(256 * h, 256)
        return copy(unit(1, chunk, rows), r1.at[chunk, rows, :], names["g1"] + 2 * chunk + h, mate_x)

    def final(chunk, rows):
        return fin.at[2 * chunk + core, rows, :]

    g3y = [copy(unit(3, k, other_rows), r3y.at[k], names["g3y"] + k, mate_y) for k in range(2)]
    g3x = [copy(unit(3, k, own_rows), r3x.at[k], names["g3x"] + k, mate_x) for k in range(2)]

    def gzu(chunk):
        return copy(unit(2, chunk, other_rows), rz.at[chunk, other_rows, :], names["gzu"] + chunk, above)

    gzm = [copy(unit(2, k, own_rows), rz.at[k, own_rows, :], names["gzm"] + k, above) for k in range(2)]
    gyr = [copy(unit(0, k, other_rows), ryr.at[k], names["gyr"] + k, mate_y) for k in range(2)]
    gya = [copy(final(k, own_rows), final(k, own_rows), names["gya"] + k, mate_y) for k in range(2)]
    gfa = [copy(final(k, own_rows), final(k, own_rows), names["gfa"] + k, mate_core) for k in range(2)]
    gfb = [copy(final(k, other_rows), final(k, other_rows), names["gfb"] + k, mate_core) for k in range(2)]

    def slot_pair(turn, carry):
        later = turn // 3
        slots = (2 * ((turn + 3) // 4) + (turn % 3) // 2, 1 + 2 * ((turn % 3) // 2) - later)
        flips = (later, (turn + 2) // 3)
        chunks = tuple(row_y + flip * (1 - 2 * row_y) for flip in flips)

        def part_of(index, at):
            slot, chunk = slots[index], chunks[index]
            k = slot // 2
            w_in, w_out = w.at[slot, 2 * chunk], w.at[slot, 2 * chunk + 1]
            hidden, slope = gelu_parts(dot_nn(a2[at, :], w_in[...]))
            hid[index, at, :] = hidden.astype(BF16)
            dhidden = dot_nt(dz[k, at, :], w_out[...])
            dpre[index, at, :] = (dhidden * slope).astype(BF16)
            gate_sum[k] += jnp.sum(hidden * dhidden, axis=0, keepdims=True)

        blocks = [pl.ds(start, 512) for start in range(0, length, 512)]

        @pl.when(turn == 1)
        def _():
            w1y[1].wait_recv()
            w1d[1].start()
            w2c.wait_recv()

        @pl.when(turn == 2)
        def _():
            w3c.wait_recv()
            w3y[0].wait_recv()
            w3d[0].start()

        @pl.when(turn == 3)
        def _():
            w2d.wait_recv()

        for at in blocks:
            part_of(0, at)

        @pl.when(turn == 0)
        def _():
            w3x[0].wait_recv()
            w3y[0].start()
            w1y[0].wait_recv()
            w1d[0].start()
            w1c.wait_recv()

        @pl.when(turn == 1)
        def _():
            w3x[1].wait_recv()
            w3y[1].start()
            w3c.start()
            for h in range(2):
                w2b[h].wait_recv()
            w2d.start()
            for h in range(2):
                w1d[h].wait_recv()

        @pl.when(turn == 2)
        def _():
            w3y[1].wait_recv()
            w3d[1].start()
            add_core(2, row_y)
            add_core(1, 1 - row_y)
            for h in range(2):
                g1(1 - row_y, h).start()
            gzu(row_y).start()
            for h in range(2):
                w3d[h].wait_recv()

        for at in blocks:
            part_of(1, at)
            value = total[at, :]
            back = da2[at, :]
            for index in range(2):
                slot, chunk = slots[index], chunks[index]
                gate = jnp.where(slot < 2, gates[:, 0:1], gates[:, 1:2])
                value = value + gate * dot_nn(hid[index, at, :], w[slot, 2 * chunk + 1])
                back = back + dot_nt(dpre[index, at, :], w[slot, 2 * chunk])
            total[at, :] = value
            da2[at, :] = back

        @pl.when(turn == 0)
        def _():
            for each in w1x + w2a + w1y + [w1c]:
                each.wait_send()

        @pl.when(turn == 1)
        def _():
            for each in w3x + w1d + [w2c]:
                each.wait_send()
            add_core(0, row_y)
            add_core(1, row_y)
            for h in range(2):
                g1(row_y, h).start()

        @pl.when(turn == 2)
        def _():
            for each in w3y + w3d + [w3c]:
                each.wait_send()

        @pl.when(turn == 3)
        def _():
            for each in w2b + [w2d]:
                each.wait_send()
            for k in range(2):
                add_core(3, k)
                g3y[k].start()

        for index in range(2):
            slot, chunk = slots[index], chunks[index]
            k = slot // 2
            w[slot, 2 * chunk] = dot_tn(a2[...], dpre[index]).astype(BF16)
            w[slot, 2 * chunk + 1] = dot_tn(hid[index], dz[k]).astype(BF16)
            gc(slot, chunk).start()
        return carry

    lax.fori_loop(0, 4, slot_pair, 0)

    gain_sum = jnp.zeros((1, width), F32)
    bias_sum = jnp.zeros((1, width), F32)
    for start in range(0, length, tile):
        at = pl.ds(start, tile)
        normal, inverse = norm_parts(mid[at, :])
        grad = da2[at, :]
        gain_sum += jnp.sum(grad * normal, axis=0, keepdims=True)
        bias_sum += jnp.sum(grad, axis=0, keepdims=True)
        dmid = dy[at, :].astype(F32) + norm_back(grad * gain2, normal, inverse)
        mid[at, :] = dmid
        a2[at, :] = dmid.astype(BF16)
    vectors[2:3, :] = gain_sum
    vectors[3:4, :] = bias_sum
    vectors[4:5, :] = gate_sum[0]
    vectors[5:6, :] = gate_sum[1]
    vectors[6:8, :] = jnp.zeros((2, width), F32)
    add_core(2, 1 - row_y)
    gzu(1 - row_y).start()
    add_core(0, 1 - row_y)
    dctx_t[...] = dot_nt(wattn[...], a2[...]).astype(BF16)

    def sum_round(index, flat):
        first = names["sum", index]
        columns = ROUNDS[index]
        mine, landed, by_y, pieces, cross, result = (
            ref[index] for ref in (part, ac, ay, ae, across, done)
        )
        own_half = pl.ds(pl.multiple_of(256 * core, 256), 256)
        other_half = pl.ds(pl.multiple_of(256 * (1 - core), 256), 256)
        corner = 256 * core + 128 * row_y
        own_quarter = pl.ds(pl.multiple_of(corner, 128), 128)
        other_quarter = pl.ds(pl.multiple_of(256 * core + 128 * (1 - row_y), 128), 128)

        def rows(step, beyond=False):
            start = 256 * core + 128 * (1 - row_y) if beyond else corner
            return pl.ds(pl.multiple_of(start + 16 * ((place + step) % GROUP), 16), 16)

        to_core = copy(mine.at[other_half, :], landed, first, mate_core)
        to_y = copy(mine.at[other_quarter, :], by_y, first + 1, mate_y)
        back_y = copy(result.at[own_quarter, :], result.at[own_quarter, :], first + 2, mate_y)
        back_core = copy(result.at[own_half, :], result.at[own_half, :], first + 3, mate_core)
        routes = [(s, rows(s), peer(s)) for s in range(1, GROUP)]
        if flat:
            routes += [(GROUP + s, rows(s, True), peer_y(s)) for s in range(GROUP)]
        spread = [copy(mine.at[at, :], pieces.at[s], first + 3 + s, to) for s, at, to in routes]
        gather = [
            copy(result.at[rows(0), :], result.at[rows(0), :], first + 2 + 2 * GROUP + s, to)
            for s, _, to in routes
        ]
        over = [
            copy(cross.at[0], cross.at[s], first + 1 + 4 * GROUP + s, far(s)) for s in range(1, groups)
        ]

        def begin():
            to_core.start()

        def step_y():
            to_core.wait_recv()
            add_into(mine.at[own_half, :], landed)
            if flat:
                for each in spread:
                    each.start()
            else:
                to_y.start()

        def step_spread():
            to_y.wait_recv()
            add_into(mine.at[own_quarter, :], by_y)
            for each in spread:
                each.start()

        def step_gather():
            for each in spread:
                each.wait_recv()
            value = mine[rows(0), :].astype(F32)
            for s, _, _ in routes:
                value = value + pieces[s].astype(F32)
            if groups > 1:
                cross[0] = value.astype(BF16)
                for each in over:
                    each.start()
                for each in over:
                    each.wait_recv()

                def add_group(group, value):
                    step = (expert // GROUP - group + groups) % groups
                    return value + cross[step].astype(F32)

                value = lax.fori_loop(0, groups, add_group, jnp.zeros(value.shape, F32))
            result[rows(0), :] = value.astype(BF16)
            for each in gather:
                each.start()

        def step_back_y():
            for each in gather:
                each.wait_recv()
            if flat:
                back_core.start()
            else:
                back_y.start()

        def step_back_core():
            back_y.wait_recv()
            back_core.start()

        def end():
            back_core.wait_recv()

        def finish():
            for each in [to_core, back_core] + ([] if flat else [to_y, back_y]) + spread + gather + over:
                each.wait_send()

        if flat:
            return [begin, step_y, step_gather, step_back_y, end, finish]
        return [begin, step_y, step_spread, step_gather, step_back_y, step_back_core, end, finish]

    rounds = [sum_round(index, index == 3) for index in range(4)]

    k_aug[128:144, :] = for_key_back.astype(BF16)
    v_aug[64:80, :] = jnp.where(
        lax.broadcasted_iota(jnp.int32, (16, length), 0) < 3, 1.0, 0.0
    ).astype(BF16)

    def qkv_columns(pair):
        target = part[pair]
        first = target.shape[1] - 384
        for index in range(3):
            at = pl.ds(index * width + 128 * pair, 128)
            target[:, pl.ds(first + 128 * index, 128)] = dot_tt(a1[...], qkv_t[at, :]).astype(BF16)

    def take_x(k):
        g3y[k].wait_recv()
        add_into(unit(3, k, own_rows), r3y.at[k])
        g3x[k].start()

    def take_z(k):
        g3x[k].wait_recv()
        add_into(unit(2, k, own_rows), r3x.at[k])
        gzm[k].start()

    def take_y(k):
        gzu(k).wait_recv()
        add_into(unit(0, k, other_rows), rz.at[k, other_rows, :])
        gyr[k].start()

    def take_final(k):
        gyr[k].wait_recv()
        gzm[k].wait_recv()
        value = unit(0, k, own_rows)[...].astype(F32) + rz[k, own_rows, :].astype(F32)
        final(k, own_rows)[...] = (value + ryr[k].astype(F32)).astype(BF16)
        gya[k].start()
        gfa[k].start()

    def take_last(k):
        gya[k].wait_recv()
        gfb[k].start()

    def backward_heads(pair, carry):
        @pl.when(pair == 1)
        def _():
            part[0][:, 0:512] = dot_nn(ctx_t[...], a2[...]).astype(BF16)
            qkv_columns(0)
            rounds[0][0]()
            take_x(0)
            for k in range(2):
                for h in range(2):
                    g1(k, h).wait_recv()
                add_into(unit(0, k), r1.at[k])

        @pl.when(pair == 2)
        def _():
            qkv_columns(1)
            rounds[1][0]()
            rounds[0][1]()
            take_x(1)
            for k in range(2):
                take_y(k)

        @pl.when(pair == 3)
        def _():
            qkv_columns(2)
            rounds[2][0]()
            rounds[1][1]()
            rounds[0][2]()
            take_z(0)

        for head in range(2):
            attend_backward(
                2 * pair + head, qkv_t, dctx_t, ctx_t, lse, mask_q, q_aug, k_aug, v_aug, d_aug,
                dk, dv, tile,
            )
        return carry

    lax.fori_loop(0, width // HEAD_DIM // 2, backward_heads, 0)
    qkv_columns(3)
    rounds[3][0]()
    rounds[2][1]()
    rounds[1][2]()
    rounds[0][3]()
    take_z(1)

    stores = []

    def store(src, dst):
        stores.append(pltpu.make_async_copy(src, dst, store_sem.at[len(stores)]))
        stores[-1].start()

    dz[0] = total[...].astype(BF16)
    store(dz.at[0], out)
    gain_sum = jnp.zeros((1, width), F32)
    bias_sum = jnp.zeros((1, width), F32)
    for start in range(0, length, tile):
        at = pl.ds(start, tile)
        grad = dot_tt(qkv_t[:, at], wqkv[...])
        normal, inverse = norm_parts(x[at, :].astype(F32))
        gain_sum += jnp.sum(grad * normal, axis=0, keepdims=True)
        bias_sum += jnp.sum(grad, axis=0, keepdims=True)
        a2[at, :] = (mid[at, :] + norm_back(grad * gain1, normal, inverse)).astype(BF16)
        if start == tile:
            rounds[3][1]()
            rounds[2][2]()
            rounds[1][3]()
            rounds[0][4]()
    store(a2, grad_in)
    vectors[0:1, :] = gain_sum
    vectors[1:2, :] = bias_sum

    vec_dp[dp] = vectors[...]
    to_dp = [
        copy(vec_dp.at[dp], vec_dp.at[dp], names["vec_dp"] + s - 1, (expert, (dp + s) % 4))
        for s in range(1, 4)
    ]
    for each in to_dp:
        each.start()
    take_final(0)
    rounds[2][3]()
    rounds[1][4]()
    rounds[0][5]()
    for each in to_dp:
        each.wait_recv()
    row_sum = vec_dp[0] + vec_dp[1] + vec_dp[2] + vec_dp[3]
    vec_ex[expert] = row_sum
    to_ex = [
        copy(vec_ex.at[expert], vec_ex.at[expert], names["vec_ex"] + s - 1, peer(s))
        for s in range(1, GROUP)
    ]
    for each in to_ex:
        each.start()
    scaled = jnp.sum(row_sum[4:6, :], axis=1, keepdims=True)
    pair_lane = lax.broadcasted_iota(jnp.int32, (1, 2), 1)
    scaled_pair = jnp.where(pair_lane == 0, scaled[0:1, :], scaled[1:2, :])
    logits_grad[...] = scaled_pair - gates * jnp.sum(scaled_pair, axis=1, keepdims=True)

    rounds[3][2]()
    take_final(1)
    rounds[2][4]()
    rounds[1][5]()
    rounds[0][6]()
    store(done[0].at[:, pl.ds(0, 512)], attn_grad)

    def store_columns(pair):
        first = ROUNDS[pair] - 384
        for index in range(3):
            store(
                done[pair].at[:, pl.ds(first + 128 * index, 128)],
                qkv_grad.at[:, pl.ds(index * width + 128 * pair, 128)],
            )

    store_columns(0)
    take_last(0)
    for each in to_ex:
        each.wait_recv()
    sums = [to_dp, to_ex]
    if groups > 1:
        vec_group = vec_ex[base]
        for s in range(1, GROUP):
            vec_group = vec_group + vec_ex[base + s]
        here = experts + expert // GROUP
        vec_ex[here] = vec_group
        to_far = [
            copy(vec_ex.at[here], vec_ex.at[here], names["vec_far"] + s - 1, far(s))
            for s in range(1, groups)
        ]
        for each in to_far:
            each.start()
        for each in to_far:
            each.wait_recv()
        sums.append(to_far)
        value = vec_ex[experts]
        for s in range(1, groups):
            value = value + vec_ex[experts + s]
    else:
        value = vec_ex[0]
        for s in range(1, GROUP):
            value = value + vec_ex[s]
    vectors[...] = value
    rounds[1][6]()
    store_columns(1)
    rounds[2][5]()
    rounds[3][3]()
    take_last(1)
    rounds[2][6]()
    store_columns(2)
    rounds[3][4]()
    store_columns(3)
    for each in gfa + gfb:
        each.wait_recv()
    for chunk in range(2):
        at = pl.ds(512 * chunk, 512)
        store(fin.at[2 * chunk], in_grad.at[:, at])
        store(fin.at[2 * chunk + 1], out_grad.at[at, :])
    for chunk in range(2):
        for slot in range(4):
            gc(slot, chunk).wait_send()
        gzu(chunk).wait_send()
        for h in range(2):
            g1(chunk, h).wait_send()
    for group in [g3y, g3x, gzm, gyr, gya, gfa, gfb] + sums:
        for each in group:
            each.wait_send()
    for steps in rounds:
        steps[-1]()
    for each in stores:
        each.wait()


def one_device(
    experts, tokens, cotangent, segments, live, ln1_gain, ln1_bias, ln2_gain, ln2_bias, wqkv, wattn,
    logits, expert_in, expert_out,
):
    length, width = tokens.shape
    groups = experts // GROUP
    _, semaphores = number_copies(groups)
    vmem = pl.BlockSpec(memory_space=pltpu.VMEM)
    smem = pl.BlockSpec(memory_space=pltpu.SMEM)
    hbm = pl.BlockSpec(memory_space=pl.ANY)
    shape = jax.ShapeDtypeStruct

    def by_round(*leading):
        return [pltpu.VMEM((*leading, columns), BF16) for columns in ROUNDS]

    scratch = [
        pltpu.VMEM((length, width), BF16),
        pltpu.VMEM((length, width), BF16),
        pltpu.VMEM(wqkv.shape, BF16),
        pltpu.VMEM(wattn.shape, BF16),
        pltpu.VMEM((4, 4, 512, 512), BF16),
        pltpu.VMEM((length, width), BF16),
        pltpu.VMEM((3 * width, length), BF16),
        pltpu.VMEM((width, length), BF16),
        pltpu.VMEM((width // HEAD_DIM, 1, length), F32),
        pltpu.VMEM((length, width), F32),
        pltpu.VMEM((length, width), BF16),
        pltpu.VMEM((2, length, width), BF16),
        pltpu.VMEM((2, length, 512), BF16),
        pltpu.VMEM((2, length, 512), BF16),
        pltpu.VMEM((length, width), F32),
        pltpu.VMEM((length, width), F32),
        pltpu.VMEM((width, length), BF16),
        pltpu.VMEM((1, length), F32),
        pltpu.VMEM((16, length), BF16),
        pltpu.VMEM((144, length), BF16),
        pltpu.VMEM((144, length), BF16),
        pltpu.VMEM((80, length), BF16),
        pltpu.VMEM((80, length), BF16),
        pltpu.VMEM((HEAD_DIM, length), F32),
        pltpu.VMEM((HEAD_DIM, length), F32),
        pltpu.VMEM((2, 1, 512), F32),
        pltpu.VMEM((4, 2, 512, 512), BF16),
        pltpu.VMEM((2, 512, 512), BF16),
        pltpu.VMEM((2, 256, 512), BF16),
        pltpu.VMEM((2, 256, 512), BF16),
        pltpu.VMEM((2, 512, 512), BF16),
        pltpu.VMEM((2, 256, 512), BF16),
        pltpu.VMEM((4, 512, 512), BF16),
        by_round(512),
        by_round(256),
        by_round(128),
        by_round(2 * GROUP, 16),
        by_round(groups, 16),
        by_round(512),
        pltpu.VMEM((4, 8, width), F32),
        pltpu.VMEM((experts + groups, 8, width), F32),
        pltpu.SemaphoreType.DMA((8,)),
        pltpu.SemaphoreType.DMA((19,)),
        pltpu.SemaphoreType.DMA((semaphores,)),
        pltpu.SemaphoreType.DMA((semaphores,)),
    ]
    return pl.pallas_call(
        functools.partial(kernel, experts),
        in_specs=[hbm, hbm, vmem, smem] + [vmem] * 4 + [hbm, hbm, vmem, hbm, hbm],
        out_specs=[hbm] * 6 + [vmem] * 2,
        out_shape=[
            shape(tokens.shape, BF16),
            shape(tokens.shape, BF16),
            shape(expert_in.shape, BF16),
            shape(expert_out.shape, BF16),
            shape(wqkv.shape, BF16),
            shape(wattn.shape, BF16),
            shape((8, width), F32),
            shape((1, 2), F32),
        ],
        scratch_shapes=scratch,
        compiler_params=pltpu.CompilerParams(
            vmem_limit_bytes=63 * 1024 * 1024, collective_id=0, has_side_effects=True
        ),
    )(
        tokens, cotangent, segments, live, ln1_gain, ln1_bias, ln2_gain, ln2_bias, wqkv, wattn, logits,
        expert_in, expert_out,
    )


def body(
    tokens, segment_ids, live_tokens, cotangent, ln1_gain, ln1_bias, qkv_weight, attn_weight,
    ln2_gain, ln2_bias, task_logits, expert_in, expert_out,
):
    out, grad_in, in_grad, out_grad, qkv_grad, attn_grad, vectors, logits_grad = one_device(
        lax.axis_size("expert"), tokens[0], cotangent[0], segment_ids, live_tokens, ln1_gain, ln1_bias,
        ln2_gain, ln2_bias, qkv_weight, attn_weight, task_logits, expert_in[0], expert_out[0],
    )
    return (
        out[None], grad_in[None], vectors[0], vectors[1], qkv_grad.astype(F32),
        attn_grad.astype(F32), vectors[2], vectors[3], logits_grad,
        in_grad.astype(F32)[None], out_grad.astype(F32)[None],
    )


def solution(mesh):
    rows = ("expert", "dp")
    in_specs = (
        P(rows, None, None), P(rows, None), P(rows), P(rows, None, None), P(), P(), P(), P(), P(), P(),
        P("expert", None), P("expert", None, None), P("expert", None, None),
    )
    out_specs = (
        P(rows, None, None), P(rows, None, None), P(), P(), P(), P(), P(), P(),
        P("expert", None), P("expert", None, None), P("expert", None, None),
    )
    return jax.shard_map(body, mesh=mesh, in_specs=in_specs, out_specs=out_specs, check_vma=False)
```

```python
import functools
import itertools

import jax
import jax.numpy as jnp
from jax import lax
from jax.experimental import pallas as pl
from jax.experimental.pallas import tpu as pltpu
from jax.sharding import PartitionSpec as P

F32 = jnp.float32
BF16 = jnp.bfloat16
HEAD_DIM = 64
NORM_EPS = 1e-05
MASKED = -1e30
LOG2E = 1.4426950408889634
GELU_A = 0.7978845608028654
GELU_B = 0.044715


def dot_nn(a, b):
    return jnp.dot(a, b, preferred_element_type=F32)


def dot_nt(a, b):
    return lax.dot_general(a, b, (((1,), (1,)), ((), ())), preferred_element_type=F32)


def dot_tn(a, b):
    return lax.dot_general(a, b, (((0,), (0,)), ((), ())), preferred_element_type=F32)


def dot_tt(a, b):
    return lax.dot_general(a, b, (((0,), (1,)), ((), ())), preferred_element_type=F32)


def norm_parts(inputs):
    row_mean = jnp.mean(inputs, axis=-1, keepdims=True)
    centred = inputs - row_mean
    variance = jnp.mean(centred * centred, axis=-1, keepdims=True)
    inverse = lax.rsqrt(variance + NORM_EPS)
    return centred * inverse, inverse


def norm_back(scaled, normal, inverse):
    return inverse * (
        scaled
        - jnp.mean(scaled, axis=-1, keepdims=True)
        - normal * jnp.mean(scaled * normal, axis=-1, keepdims=True)
    )


def split_three(value):
    high = value.astype(BF16)
    rest = value - high.astype(F32)
    middle = rest.astype(BF16)
    low = (rest - middle.astype(F32)).astype(BF16)
    return high.astype(F32), middle.astype(F32), low.astype(F32)


def scaled_queries(queries):
    scaled = queries.astype(F32) * (LOG2E * HEAD_DIM ** (-0.5))
    high = scaled.astype(BF16)
    return high, (scaled - high.astype(F32)).astype(BF16)


def mask_rows(segments, live, length):
    position = lax.broadcasted_iota(jnp.int32, (16, length), 1)
    row = lax.broadcasted_iota(jnp.int32, (16, length), 0)
    segment = jnp.broadcast_to(segments, (16, length))
    alive = position < live
    for_query = jnp.where(
        row < 8,
        jnp.where(segment != row, MASKED, 0.0),
        jnp.where((row == 8) & alive, MASKED, 0.0),
    )
    for_key = jnp.where(
        row < 8,
        jnp.where(segment == row, 1.0, 0.0),
        jnp.where((row == 8) & (~alive), 1.0, 0.0),
    )
    for_key_back = jnp.where((row >= 9) & (row < 12), 1.0, for_key)
    return for_query, for_key, for_key_back


def head_rows(head, part, width):
    return pl.ds(pl.multiple_of(part * width + head * HEAD_DIM, HEAD_DIM), HEAD_DIM)


def key_band(start, size, tile, length):
    low = max(0, (start - 511) // tile * tile)
    high = min(length, -(-(start + size + 511) // tile) * tile)
    return low, high


def attend_forward(head, qkv_t, ctx_t, lse, mask_q, alive_row, q_aug, k_aug, v_aug, tile):
    width, length = ctx_t.shape
    high, low = scaled_queries(qkv_t[head_rows(head, 0, width), :])
    q_aug[0:64, :] = high
    q_aug[64:128, :] = low
    q_aug[128:144, :] = mask_q[...]
    keys = qkv_t[head_rows(head, 1, width), :]
    k_aug[0:64, :] = keys
    k_aug[64:128, :] = keys
    v_aug[0:64, :] = qkv_t[head_rows(head, 2, width), :]
    for start in range(0, length, tile):
        at = pl.ds(start, tile)
        scores = dot_tn(k_aug[...], q_aug[:, at])
        top = jnp.max(scores, axis=0, keepdims=True)
        weights = jnp.exp2(scores - top)
        total = jnp.sum(weights, axis=0, keepdims=True)
        context = dot_nn(v_aug[0:64, :], (weights * (1.0 / total)).astype(BF16))
        own = v_aug[0:64, at].astype(F32)
        ctx_t[head_rows(head, 0, width), at] = jnp.where(
            alive_row[:, at] > 0, context, own
        ).astype(BF16)
        lse[head, :, at] = top + jnp.log(total) * LOG2E


def attend_backward(head, qkv_t, dctx_t, ctx_t, lse, mask_q, q_aug, k_aug, v_aug, d_aug, dk, dv, tile):
    width, length = ctx_t.shape
    scale = HEAD_DIM ** (-0.5)
    row = lax.broadcasted_iota(jnp.int32, (16, length), 0)
    high, low = scaled_queries(qkv_t[head_rows(head, 0, width), :])
    q_aug[0:64, :] = high
    q_aug[64:128, :] = low
    one, two, three = split_three(-lse[head])
    q_aug[128:144, :] = jnp.where(
        row == 9, one, jnp.where(row == 10, two, jnp.where(row == 11, three, mask_q[...].astype(F32)))
    ).astype(BF16)
    keys = qkv_t[head_rows(head, 1, width), :]
    k_aug[0:64, :] = keys
    k_aug[64:128, :] = keys
    v_aug[0:64, :] = qkv_t[head_rows(head, 2, width), :]
    grad = dctx_t[head_rows(head, 0, width), :]
    d_aug[0:64, :] = grad
    context = ctx_t[head_rows(head, 0, width), :].astype(F32)
    one, two, three = split_three(
        -jnp.sum(grad.astype(F32) * context, axis=0, keepdims=True)
    )
    d_aug[64:80, :] = jnp.where(
        row == 0, one, jnp.where(row == 1, two, jnp.where(row == 2, three, 0.0))
    ).astype(BF16)
    dk[...] = jnp.zeros(dk.shape, F32)
    dv[...] = jnp.zeros(dv.shape, F32)
    for start in range(0, length, tile):
        first, last = key_band(start, tile, tile, length)
        at, near = pl.ds(start, tile), pl.ds(first, last - first)
        weights = jnp.exp2(dot_tn(q_aug[:, at], k_aug[:, near]))
        dweights = dot_tn(d_aug[:, at], v_aug[:, near])
        dscores = (weights * dweights).astype(BF16)
        dv[:, near] += dot_nn(d_aug[0:64, at], weights.astype(BF16))
        dk[:, near] += dot_nn(qkv_t[head_rows(head, 0, width), at], dscores)
        qkv_t[head_rows(head, 0, width), at] = (
            dot_nt(k_aug[0:64, near], dscores) * scale
        ).astype(BF16)
    qkv_t[head_rows(head, 1, width), :] = (dk[...] * scale).astype(BF16)
    qkv_t[head_rows(head, 2, width), :] = dv[...].astype(BF16)


def gelu_parts(u):
    square = u * u
    bend = jnp.tanh(u * (GELU_A + (GELU_A * GELU_B) * square))
    half = 0.5 + 0.5 * bend
    slope = half + (0.5 * u) * (1.0 - bend * bend) * (GELU_A + (3.0 * GELU_A * GELU_B) * square)
    return u * half, slope


MESH = pl.DeviceIdType.MESH
GROUP = 8


class Numbers:
    def __init__(self):
        self.used = 0

    def take(self, count):
        first = self.used
        self.used += count
        return first


def number_copies(groups):
    numbers = Numbers()
    names = {}
    for name, count in [
        ("w1x", 2), ("w1y", 2), ("w1c", 1), ("w1d", 2), ("w2a", 2), ("w2b", 2), ("w2c", 1), ("w2d", 1),
        ("w3x", 2), ("w3y", 2), ("w3c", 1), ("w3d", 2), ("gc", 8), ("g1", 4), ("g3y", 4), ("g3x", 4),
        ("gzu", 2), ("gzm", 4), ("gyr", 2), ("gya", 4), ("gfa", 4), ("gfb", 4),
        ("vec_dp", 3), ("vec_ex", GROUP - 1), ("vec_far", groups - 1),
    ]:
        names[name] = numbers.take(count)
    for index, levels in enumerate(LEVELS):
        copies = sum(len(level_steps(level)) for level in levels)
        names["sum", index] = numbers.take(2 * copies + groups - 1)
    return names, numbers.used


ROUNDS = (512, 384, 384, 384, 384)
LEVELS = (("c", "x", "yz"), ("c", "y", "x", "z"), ("c", "x", "yz"), ("c", "x", "yz"), ("c", "x", "yz"))
ORDER = {
    "h0": [("a", 0), ("p", "y"), ("y", "y"), ("x", 0), ("p", "n"), ("x", 1)],
    "h1": [("a", 0), ("x", 2)],
    "h2": [("a", 1), ("z", 0), ("x", 3)],
    "h3": [("y", "n"), ("a", 1), ("z", 1)],
    "h4": [("a", 2), ("a", 0)],
    "h5": [("a", 2), ("z", 2)],
    "h6": [("a", 3), ("z", 3), ("f", 0), ("f", 1)],
    "h7": [("a", 3), ("a", 2), ("a", 1)],
    "E": [("a", 4), ("a", 0), ("f", 2), ("l", 0)],
    "L1": [("f", 3), ("a", 4), ("a", 3)],
    "L2": [("a", 1), ("l", 1)],
    "L3": [("a", 2)],
    "L4": [("a", 0), ("a", 4)],
    "tail": [
        ("l", 2), ("a", 1), ("l", 3), ("a", 0), ("a", 3), ("a", 0), ("a", 2), ("a", 1),
        ("a", 4), ("vex",), ("a", 3), ("a", 2), ("a", 1), ("a", 2), ("a", 4), ("a", 3),
        ("a", 1), ("vend",), ("a", 3), ("a", 4), ("a", 1), ("a", 4),
    ],
}
AXES = {"x": 2, "y": 2, "c": 2, "z": GROUP // 2}


def level_steps(level):
    ranges = [range(AXES[axis] if axis in level else 1) for axis in "xycz"]
    return [steps for steps in itertools.product(*ranges) if any(steps)]


def share(rows, axes, place):
    start, first = 0, 0
    count, lanes = rows, 512
    if "x" in axes:
        count = count // AXES["x"]
        start = start + count * place[0]
    if "z" in axes:
        count = count // AXES["z"]
        start = start + count * place[3]
    if "c" in axes:
        lanes = lanes // AXES["c"]
        first = first + lanes * place[2]
    if "y" in axes:
        lanes = lanes // AXES["y"]
        first = first + lanes * place[1]
    rows_at = pl.ds(0, count) if isinstance(start, int) else pl.ds(pl.multiple_of(start, 16), count)
    return rows_at, pl.ds(pl.multiple_of(first, 128), lanes)


def kernel(
    experts,
    tokens, cotangent, segments, live, ln1_gain, ln1_bias, ln2_gain, ln2_bias, wqkv_in, wattn_in, logits,
    expert_in, expert_out,
    out, grad_in, in_grad, out_grad, qkv_grad, attn_grad, vectors, logits_grad,
    x, dy, wqkv, wattn, w, a1, qkv_t, ctx_t, lse, mid, a2, dz, hid, dpre, total, da2,
    dctx_t, alive_row, mask_q, q_aug, k_aug, v_aug, d_aug, dk, dv, gate_sum,
    rc, r1, r3y, r3x, rz, ryr, fin, part, landed, across, done, vec_dp, vec_ex,
    load_sem, store_sem, send_sem, recv_sem,
):
    length, width = x.shape
    tile = 256
    groups = experts // GROUP
    names, _ = number_copies(groups)
    expert = lax.axis_index("expert")
    dp = lax.axis_index("dp")
    core, row_y = dp % 2, dp // 2
    dp_core = dp + 1 - 2 * core
    here = (expert % 2, row_y, core, expert % GROUP // 2)
    dp_y = (dp + 2) % 4
    place = expert % GROUP
    base = expert - place
    mate_core = (expert, dp_core)
    mate_y = (expert, dp_y)
    mate_x = (expert + 1 - 2 * (expert % 2), dp)
    above = ((expert + 2) % experts, dp)
    below = ((expert + experts - 2) % experts, dp)

    def copy(src, dst, index, device):
        return pltpu.make_async_remote_copy(
            src_ref=src, dst_ref=dst, send_sem=send_sem.at[index], recv_sem=recv_sem.at[index],
            device_id=device, device_id_type=MESH,
        )

    def peer(step):
        return (base + (place + step) % GROUP, dp)

    def far(step):
        return ((expert + GROUP * step) % experts, dp)

    barrier = pltpu.get_barrier_semaphore()
    others = [mate_core, mate_y, mate_x, above, below] + [far(step) for step in range(1, groups)]
    for other in others:
        pl.semaphore_signal(barrier, inc=1, device_id=other, device_id_type=MESH)

    loads = [
        pltpu.make_async_copy(src, dst, load_sem.at[i])
        for i, (src, dst) in enumerate(
            [
                (expert_in.at[:, pl.ds(0, 512)], w.at[0, 0]),
                (expert_out.at[pl.ds(0, 512), :], w.at[0, 1]),
                (expert_in.at[:, pl.ds(512, 512)], w.at[0, 2]),
                (expert_out.at[pl.ds(512, 512), :], w.at[0, 3]),
                (tokens, x),
                (wqkv_in, wqkv),
                (wattn_in, wattn),
                (cotangent, dy),
            ]
        )
    ]
    for load in loads:
        load.start()
    live_count = live[0]
    alive_row[...] = jnp.where(
        lax.broadcasted_iota(jnp.int32, (1, length), 1) < live_count, 1.0, 0.0
    )
    for_query, for_key, for_key_back = mask_rows(segments[...], live_count, length)
    mask_q[...] = for_query.astype(BF16)
    k_aug[128:144, :] = for_key.astype(BF16)
    gain1, bias1, gain2, bias2 = (
        ref[...].astype(F32).reshape(1, width) for ref in (ln1_gain, ln1_bias, ln2_gain, ln2_bias)
    )
    exponent = jnp.exp(logits[...] - jnp.max(logits[...], axis=1, keepdims=True))
    gates = exponent / jnp.sum(exponent, axis=1, keepdims=True)

    def halves(name, slot, unit, to_slot, device):
        return [
            copy(
                w.at[slot, unit, pl.ds(256 * h, 256), :], w.at[to_slot, unit, pl.ds(256 * h, 256), :],
                names[name] + h, device,
            )
            for h in range(2)
        ]

    w1x = halves("w1x", 0, dp, 1, mate_x)
    w1y = halves("w1y", 1, dp, 1, mate_y)
    w1d = halves("w1d", 1, dp_y, 1, mate_core)
    w1c = copy(w.at[1, dp], w.at[1, dp], names["w1c"], mate_core)
    w2a = halves("w2a", 0, dp, 2, below)
    w2b = halves("w2b", 0, dp_y, 2, below)
    w2c = copy(w.at[2, dp], w.at[2, dp], names["w2c"], mate_core)
    w2d = copy(w.at[2, dp_y], w.at[2, dp_y], names["w2d"], mate_core)
    w3x = halves("w3x", 2, dp, 3, mate_x)
    w3y = halves("w3y", 3, dp, 3, mate_y)
    w3d = halves("w3d", 3, dp_y, 3, mate_core)
    w3c = copy(w.at[3, dp], w.at[3, dp], names["w3c"], mate_core)

    for load in loads[:4]:
        load.wait()
    pl.semaphore_wait(barrier, len(others))
    for h in range(2):
        w1x[h].start()
        w2a[h].start()
    for h in range(2):
        w2b[h].start()

    loads[4].wait()
    for start in range(0, length, tile):
        at = pl.ds(start, tile)
        normal, inverse = norm_parts(x[at, :].astype(F32))
        a1[at, :] = (normal * gain1 + bias1).astype(BF16)
    loads[5].wait()
    for start in range(0, 3 * width, 512):
        at = pl.ds(start, 512)
        qkv_t[at, :] = dot_tt(wqkv[:, at], a1[...]).astype(BF16)

    def forward_heads(pair, carry):
        @pl.when(pair == 2)
        def _():
            w1x[0].wait_recv()
            w1y[0].start()
            w2a[0].wait_recv()
            w3x[0].start()

        for head in range(2):
            attend_forward(
                2 * pair + head, qkv_t, ctx_t, lse, mask_q, alive_row, q_aug, k_aug, v_aug, length
            )
        return carry

    lax.fori_loop(0, width // HEAD_DIM // 2, forward_heads, 0)
    w1x[1].wait_recv()
    w1y[1].start()
    w1c.start()
    w2a[1].wait_recv()
    w3x[1].start()
    w2c.start()

    loads[6].wait()
    loads[7].wait()
    for start in range(0, length, tile):
        at = pl.ds(start, tile)
        middle = x[at, :].astype(F32) + dot_tn(ctx_t[:, at], wattn[...])
        mid[at, :] = middle
        total[at, :] = middle
        normal, inverse = norm_parts(middle)
        a2[at, :] = (normal * gain2 + bias2).astype(BF16)
        alive = start + lax.broadcasted_iota(jnp.int32, (tile, 1), 0) < live_count
        live_dy = jnp.where(alive, dy[at, :], jnp.zeros((), BF16))
        dy[at, :] = live_dy
        for k in range(2):
            dz[k, at, :] = (gates[:, k : k + 1] * live_dy.astype(F32)).astype(BF16)
    da2[...] = jnp.zeros(da2.shape, F32)
    gate_sum[...] = jnp.zeros(gate_sum.shape, F32)

    def add_into(target, *terms):
        value = target[...].astype(F32)
        for term in terms:
            value = value + term[...].astype(F32)
        target[...] = value.astype(BF16)

    own_rows = pl.ds(pl.multiple_of(256 * row_y, 256), 256)
    other_rows = pl.ds(pl.multiple_of(256 * (1 - row_y), 256), 256)

    def unit(slot, chunk, rows=pl.ds(0, 512)):
        return w.at[slot, 2 * chunk + core, rows, :]

    def gc(slot, chunk):
        return copy(
            w.at[slot, 2 * chunk + 1 - core], rc.at[slot, chunk], names["gc"] + 2 * slot + chunk, mate_core
        )

    def add_core(slot, chunk):
        gc(slot, chunk).wait_recv()
        add_into(unit(slot, chunk), rc.at[slot, chunk])

    def g1(chunk, h):
        rows = pl.ds(256 * h, 256)
        return copy(unit(1, chunk, rows), r1.at[chunk, rows, :], names["g1"] + 2 * chunk + h, mate_x)

    def final(chunk, rows):
        return fin.at[2 * chunk + core, rows, :]

    def quarter(own, h):
        start = row_y if own else 1 - row_y
        return pl.ds(pl.multiple_of(256 * start + 128 * h, 128), 128)

    def pieces(name, device, src, dst):
        return [
            copy(src(k, h), dst(k, h), names[name] + 2 * k + h, device) for k in range(2) for h in range(2)
        ]

    def half_of(ref, k, h):
        return ref.at[k, pl.ds(128 * h, 128), :]

    g3y = pieces("g3y", mate_y, lambda k, h: unit(3, k, quarter(False, h)), functools.partial(half_of, r3y))
    g3x = pieces("g3x", mate_x, lambda k, h: unit(3, k, quarter(True, h)), functools.partial(half_of, r3x))
    gzm = pieces(
        "gzm", above, lambda k, h: unit(2, k, quarter(True, h)), lambda k, h: rz.at[k, quarter(True, h), :]
    )

    def gzu(chunk):
        return copy(unit(2, chunk, other_rows), rz.at[chunk, other_rows, :], names["gzu"] + chunk, above)

    def gyr(chunk):
        return copy(unit(0, chunk, other_rows), ryr.at[chunk], names["gyr"] + chunk, mate_y)

    def own_final(k, h):
        return final(k, quarter(True, h))

    def other_final(k, h):
        return final(k, quarter(False, h))

    gya = pieces("gya", mate_y, own_final, own_final)
    gfa = pieces("gfa", mate_core, own_final, own_final)
    gfb = pieces("gfb", mate_core, other_final, other_final)

    def slot_pair(turn, carry):
        later = turn // 3
        slots = (2 * ((turn + 3) // 4) + (turn % 3) // 2, 1 + 2 * ((turn % 3) // 2) - later)
        flips = (later, (turn + 2) // 3)
        chunks = tuple(row_y + flip * (1 - 2 * row_y) for flip in flips)

        def part_of(index, at):
            slot, chunk = slots[index], chunks[index]
            k = slot // 2
            w_in, w_out = w.at[slot, 2 * chunk], w.at[slot, 2 * chunk + 1]
            hidden, slope = gelu_parts(dot_nn(a2[at, :], w_in[...]))
            hid[index, at, :] = hidden.astype(BF16)
            dhidden = dot_nt(dz[k, at, :], w_out[...])
            dpre[index, at, :] = (dhidden * slope).astype(BF16)

        blocks = [pl.ds(start, 512) for start in range(0, length, 512)]

        @pl.when(turn == 1)
        def _():
            w1y[1].wait_recv()
            w1d[1].start()
            w2c.wait_recv()

        @pl.when(turn == 2)
        def _():
            w3c.wait_recv()
            w3y[0].wait_recv()
            w3d[0].start()

        @pl.when(turn == 3)
        def _():
            w2d.wait_recv()

        for at in blocks:
            part_of(0, at)

        @pl.when(turn == 0)
        def _():
            w3x[0].wait_recv()
            w3y[0].start()
            w1y[0].wait_recv()
            w1d[0].start()
            w1c.wait_recv()

        @pl.when(turn == 1)
        def _():
            w3x[1].wait_recv()
            w3y[1].start()
            w3c.start()
            for h in range(2):
                w2b[h].wait_recv()
            w2d.start()
            for h in range(2):
                w1d[h].wait_recv()

        @pl.when(turn == 2)
        def _():
            w3y[1].wait_recv()
            w3d[1].start()
            add_core(2, row_y)
            add_core(1, 1 - row_y)
            for h in range(2):
                g1(1 - row_y, h).start()
            gzu(row_y).start()
            for h in range(2):
                w3d[h].wait_recv()

        for at in blocks:
            part_of(1, at)
            value = total[at, :]
            back = da2[at, :]
            live_dy = dy[at, :].astype(F32)
            for index in range(2):
                slot, chunk = slots[index], chunks[index]
                gate = jnp.where(slot < 2, gates[:, 0:1], gates[:, 1:2])
                branch = dot_nn(hid[index, at, :], w[slot, 2 * chunk + 1])
                gate_sum[slot // 2] += jnp.sum(branch * live_dy, axis=0, keepdims=True)
                value = value + gate * branch
                back = back + dot_nt(dpre[index, at, :], w[slot, 2 * chunk])
            total[at, :] = value
            da2[at, :] = back

        @pl.when(turn == 0)
        def _():
            for each in w1x + w2a + w1y + [w1c]:
                each.wait_send()

        @pl.when(turn == 1)
        def _():
            for each in w3x + w1d + [w2c]:
                each.wait_send()
            add_core(0, row_y)
            add_core(1, row_y)
            for h in range(2):
                g1(row_y, h).start()

        @pl.when(turn == 2)
        def _():
            for each in w3y + w3d + [w3c]:
                each.wait_send()

        @pl.when(turn == 3)
        def _():
            for each in w2b + [w2d]:
                each.wait_send()
            for k in range(2):
                add_core(3, k)
                for h in range(2):
                    g3y[2 * k + h].start()

        for index in range(2):
            slot, chunk = slots[index], chunks[index]
            k = slot // 2
            w[slot, 2 * chunk] = dot_tn(a2[...], dpre[index]).astype(BF16)
            w[slot, 2 * chunk + 1] = dot_tn(hid[index], dz[k]).astype(BF16)
            gc(slot, chunk).start()
        return carry

    lax.fori_loop(0, 4, slot_pair, 0)

    gain_sum = jnp.zeros((1, width), F32)
    bias_sum = jnp.zeros((1, width), F32)
    for start in range(0, length, tile):
        at = pl.ds(start, tile)
        normal, inverse = norm_parts(mid[at, :])
        grad = da2[at, :]
        gain_sum += jnp.sum(grad * normal, axis=0, keepdims=True)
        bias_sum += jnp.sum(grad, axis=0, keepdims=True)
        dmid = dy[at, :].astype(F32) + norm_back(grad * gain2, normal, inverse)
        mid[at, :] = dmid
        a2[at, :] = dmid.astype(BF16)
    vectors[2:3, :] = gain_sum
    vectors[3:4, :] = bias_sum
    vectors[4:5, :] = gate_sum[0]
    vectors[5:6, :] = gate_sum[1]
    vectors[6:8, :] = jnp.zeros((2, width), F32)
    add_core(2, 1 - row_y)
    gzu(1 - row_y).start()
    add_core(0, 1 - row_y)
    dctx_t[...] = dot_nt(wattn[...], a2[...]).astype(BF16)

    def sum_round(index):
        rows, levels = ROUNDS[index], LEVELS[index]
        mine, cross, result = part[index], across[index], done[index]
        number = names["sum", index]
        scatter, gather, done_axes = [], [], []
        axes = ""
        for level, buffer in zip(levels, landed[index]):
            axes = axes + level
            done_axes.append(axes)
            there, back = [], []
            for slot, steps in enumerate(level_steps(level)):
                x_there = here[0] + steps[0] * (1 - 2 * here[0])
                y_there = here[1] + steps[1] * (1 - 2 * here[1])
                c_there = here[2] + steps[2] * (1 - 2 * here[2])
                z_there = (here[3] + steps[3]) % AXES["z"]
                device = (base + 2 * z_there + x_there, 2 * y_there + c_there)
                away = share(rows, axes, (x_there, y_there, c_there, z_there))
                there.append(copy(mine.at[away], buffer.at[slot], number, device))
                at = share(rows, axes, here)
                back.append(copy(result.at[at], result.at[at], number + 1, device))
                number += 2
            scatter.append(there)
            gather.append(back)
        over = [copy(cross.at[0], cross.at[s], number + s - 1, far(s)) for s in range(1, groups)]
        last = len(levels) - 1

        def start_all(copies):
            for each in copies:
                each.start()

        def wait_all(copies):
            for each in copies:
                each.wait_recv()

        def begin():
            start_all(scatter[0])

        def add_up(level):
            wait_all(scatter[level])
            at = share(rows, done_axes[level], here)
            value = mine[at].astype(F32)
            for slot in range(len(scatter[level])):
                value = value + landed[index][level][slot].astype(F32)
            if level < last:
                mine[at] = value.astype(BF16)
                start_all(scatter[level + 1])
                return
            if groups > 1:
                cross[0] = value.astype(BF16)
                start_all(over)
                wait_all(over)

                def add_group(group, value):
                    step = (expert // GROUP - group + groups) % groups
                    return value + cross[step].astype(F32)

                value = lax.fori_loop(0, groups, add_group, jnp.zeros(value.shape, F32))
            result[at] = value.astype(BF16)
            start_all(gather[last])

        def pass_back(level):
            wait_all(gather[level])
            if level > 0:
                start_all(gather[level - 1])

        def finish():
            for copies in scatter + gather + [over]:
                for each in copies:
                    each.wait_send()

        steps = [begin] + [functools.partial(add_up, level) for level in range(last + 1)]
        steps += [functools.partial(pass_back, level) for level in range(last, -1, -1)]
        return steps, finish

    rounds = [sum_round(index) for index in range(len(ROUNDS))]
    progress = [0] * len(rounds)

    def advance(index):
        if progress[index] == 0 and index == 0:
            part[0][...] = dot_nn(ctx_t[...], a2[...]).astype(BF16)
        elif progress[index] == 0:
            qkv_rows(index - 1)
        rounds[index][0][progress[index]]()
        progress[index] += 1
        if progress[index] == len(rounds[index][0]):
            if index == 0:
                store(done[0], attn_grad)
            else:
                store_pair(index - 1)

    k_aug[128:144, :] = for_key_back.astype(BF16)
    v_aug[64:80, :] = jnp.where(
        lax.broadcasted_iota(jnp.int32, (16, length), 0) < 3, 1.0, 0.0
    ).astype(BF16)

    def qkv_rows(pair):
        for index in range(3):
            at = pl.ds(index * width + 128 * pair, 128)
            part[1 + pair][128 * index : 128 * index + 128, :] = dot_nn(qkv_t[at, :], a1[...]).astype(BF16)

    def take_x(p):
        g3y[p].wait_recv()
        add_into(unit(3, p // 2, quarter(True, p % 2)), half_of(r3y, p // 2, p % 2))
        g3x[p].start()

    def take_z(p):
        g3x[p].wait_recv()
        add_into(unit(2, p // 2, quarter(True, p % 2)), half_of(r3x, p // 2, p % 2))
        gzm[p].start()

    def take_partner(k):
        for h in range(2):
            g1(k, h).wait_recv()
        add_into(unit(0, k), r1.at[k])

    def take_y(k):
        gzu(k).wait_recv()
        add_into(unit(0, k, other_rows), rz.at[k, other_rows, :])
        gyr(k).start()

    def take_final(p):
        k, h = p // 2, p % 2
        if h == 0:
            gyr(k).wait_recv()
        gzm[p].wait_recv()
        value = unit(0, k, quarter(True, h))[...].astype(F32) + rz[k, quarter(True, h), :].astype(F32)
        own_final(k, h)[...] = (value + ryr[k, pl.ds(128 * h, 128), :].astype(F32)).astype(BF16)
        gya[p].start()
        gfa[p].start()

    def take_last(p):
        gya[p].wait_recv()
        gfb[p].start()

    def take(steps):
        for name, *which in steps:
            if name == "a":
                advance(*which)
            elif name == "x":
                take_x(*which)
            elif name == "z":
                take_z(*which)
            elif name == "p":
                take_partner(row_y if which[0] == "y" else 1 - row_y)
            elif name == "y":
                take_y(row_y if which[0] == "y" else 1 - row_y)
            elif name == "f":
                take_final(*which)
            elif name == "l":
                take_last(*which)
            elif name == "vex":
                vectors_over_experts()
            else:
                vectors_end()

    def backward_heads(head, carry):
        for index in range(width // HEAD_DIM):
            pl.when(head == index)(functools.partial(take, ORDER[f"h{index}"]))
        attend_backward(
            head, qkv_t, dctx_t, ctx_t, lse, mask_q, q_aug, k_aug, v_aug, d_aug, dk, dv, tile
        )
        return carry

    lax.fori_loop(0, width // HEAD_DIM, backward_heads, 0)
    take(ORDER["E"])

    stores = []

    def store(src, dst):
        stores.append(pltpu.make_async_copy(src, dst, store_sem.at[len(stores)]))
        stores[-1].start()

    dz[0] = total[...].astype(BF16)
    store(dz.at[0], out)
    gain_sum = jnp.zeros((1, width), F32)
    bias_sum = jnp.zeros((1, width), F32)
    for index, start in enumerate(range(0, length, tile)):
        at = pl.ds(start, tile)
        grad = dot_tt(qkv_t[:, at], wqkv[...])
        normal, inverse = norm_parts(x[at, :].astype(F32))
        gain_sum += jnp.sum(grad * normal, axis=0, keepdims=True)
        bias_sum += jnp.sum(grad, axis=0, keepdims=True)
        a2[at, :] = (mid[at, :] + norm_back(grad * gain1, normal, inverse)).astype(BF16)
        take(ORDER[f"L{index + 1}"])
    store(a2, grad_in)
    vectors[0:1, :] = gain_sum
    vectors[1:2, :] = bias_sum

    vec_dp[dp] = vectors[...]
    to_dp = [
        copy(vec_dp.at[dp], vec_dp.at[dp], names["vec_dp"] + s - 1, (expert, (dp + s) % 4))
        for s in range(1, 4)
    ]
    for each in to_dp:
        each.start()
    to_ex = [
        copy(vec_ex.at[expert], vec_ex.at[expert], names["vec_ex"] + s - 1, peer(s))
        for s in range(1, GROUP)
    ]
    sums = [to_dp, to_ex]

    def vectors_over_experts():
        for each in to_dp:
            each.wait_recv()
        row_sum = vec_dp[0] + vec_dp[1] + vec_dp[2] + vec_dp[3]
        vec_ex[expert] = row_sum
        for each in to_ex:
            each.start()
        scaled = jnp.sum(row_sum[4:6, :], axis=1, keepdims=True)
        pair_lane = lax.broadcasted_iota(jnp.int32, (1, 2), 1)
        dgate = jnp.where(pair_lane == 0, scaled[0:1, :], scaled[1:2, :])
        logits_grad[...] = gates * (dgate - jnp.sum(gates * dgate, axis=1, keepdims=True))

    def vectors_end():
        for each in to_ex:
            each.wait_recv()
        if groups > 1:
            vec_group = vec_ex[base]
            for s in range(1, GROUP):
                vec_group = vec_group + vec_ex[base + s]
            own = experts + expert // GROUP
            vec_ex[own] = vec_group
            to_far = [
                copy(vec_ex.at[own], vec_ex.at[own], names["vec_far"] + s - 1, far(s))
                for s in range(1, groups)
            ]
            for each in to_far:
                each.start()
            for each in to_far:
                each.wait_recv()
            sums.append(to_far)
            value = vec_ex[experts]
            for s in range(1, groups):
                value = value + vec_ex[experts + s]
        else:
            value = vec_ex[0]
            for s in range(1, GROUP):
                value = value + vec_ex[s]
        vectors[...] = value

    def store_pair(pair):
        for index in range(3):
            store(
                done[1 + pair].at[pl.ds(128 * index, 128), :],
                qkv_grad.at[pl.ds(index * width + 128 * pair, 128), :],
            )

    take(ORDER["tail"])
    for each in gfa + gfb:
        each.wait_recv()
    for chunk in range(2):
        at = pl.ds(512 * chunk, 512)
        store(fin.at[2 * chunk], in_grad.at[:, at])
        store(fin.at[2 * chunk + 1], out_grad.at[at, :])
    for chunk in range(2):
        for slot in range(4):
            gc(slot, chunk).wait_send()
        gzu(chunk).wait_send()
        gyr(chunk).wait_send()
        for h in range(2):
            g1(chunk, h).wait_send()
    for group in [g3y, g3x, gzm, gya, gfa, gfb] + sums:
        for each in group:
            each.wait_send()
    for index, (steps, finish) in enumerate(rounds):
        assert progress[index] == len(steps), (index, progress[index], len(steps))
        finish()
    for each in stores:
        each.wait()


def last_kernel(
    out_low, grad_low, in_low, outg_low, qkv_low, attn_low, vectors,
    out, grad_in, gain1, bias1, qkv_grad, attn_grad, gain2, bias2, in_grad, out_grad,
    out_v, grad_v, in_v, outg_v, qkv_v, attn_v, in_f, outg_f, qkv_f, attn_f, load_sem, store_sem,
):
    loads = [
        pltpu.make_async_copy(src, dst, load_sem.at[i])
        for i, (src, dst) in enumerate(
            [
                (qkv_low, qkv_v), (in_low, in_v), (outg_low, outg_v), (attn_low, attn_v),
                (out_low, out_v), (grad_low, grad_v),
            ]
        )
    ]
    for each in loads:
        each.start()
    for row, target in enumerate([gain1, bias1, gain2, bias2]):
        target[...] = vectors[row : row + 1, :].reshape(target.shape)
    width = attn_v.shape[0]
    stores = []

    def store(src, dst):
        stores.append(pltpu.make_async_copy(src, dst, store_sem.at[len(stores)]))
        stores[-1].start()

    loads[0].wait()
    for index in range(3):
        at = pl.ds(index * width, width)
        qkv_f[:, at] = qkv_v[at, :].astype(F32).T
        store(qkv_f.at[:, at], qkv_grad.at[:, at])
    for index, (low, wide, target) in enumerate(
        [(in_v, in_f, in_grad), (outg_v, outg_f, out_grad), (attn_v, attn_f, attn_grad)]
    ):
        loads[1 + index].wait()
        wide[...] = low[...].astype(F32)
        store(wide, target)
    for index, (low, target) in enumerate([(out_v, out), (grad_v, grad_in)]):
        loads[4 + index].wait()
        store(low, target)
    for each in stores:
        each.wait()


def widen(out, grad_in, in_grad, out_grad, qkv_grad, attn_grad, vectors):
    width = attn_grad.shape[0]
    vmem = pl.BlockSpec(memory_space=pltpu.VMEM)
    hbm = pl.BlockSpec(memory_space=pl.ANY)
    shape = jax.ShapeDtypeStruct
    low = [out.shape, grad_in.shape, in_grad.shape, out_grad.shape, qkv_grad.shape, attn_grad.shape]
    wide = [in_grad.shape, out_grad.shape, (width, 3 * width), attn_grad.shape]
    vector = shape((width,), F32)
    return pl.pallas_call(
        last_kernel,
        in_specs=[hbm] * 6 + [vmem],
        out_specs=[hbm] * 2 + [vmem] * 2 + [hbm] * 2 + [vmem] * 2 + [hbm] * 2,
        out_shape=[
            shape(out.shape, BF16), shape(grad_in.shape, BF16), vector, vector, shape(wide[2], F32),
            shape(wide[3], F32), vector, vector, shape(wide[0], F32), shape(wide[1], F32),
        ],
        scratch_shapes=[pltpu.VMEM(each, BF16) for each in low]
        + [pltpu.VMEM(each, F32) for each in wide]
        + [pltpu.SemaphoreType.DMA((6,)), pltpu.SemaphoreType.DMA((8,))],
        compiler_params=pltpu.CompilerParams(vmem_limit_bytes=63 * 1024 * 1024),
    )(out, grad_in, in_grad, out_grad, qkv_grad, attn_grad, vectors)


def one_device(
    experts, tokens, cotangent, segments, live, ln1_gain, ln1_bias, ln2_gain, ln2_bias, wqkv, wattn,
    logits, expert_in, expert_out,
):
    length, width = tokens.shape
    groups = experts // GROUP
    _, semaphores = number_copies(groups)
    vmem = pl.BlockSpec(memory_space=pltpu.VMEM)
    smem = pl.BlockSpec(memory_space=pltpu.SMEM)
    hbm = pl.BlockSpec(memory_space=pl.ANY)
    shape = jax.ShapeDtypeStruct

    def by_round(*leading):
        return [pltpu.VMEM((*leading, rows, width), BF16) for rows in ROUNDS]

    def level_buffers(rows, levels):
        axes, buffers = "", []
        for level in levels:
            axes = axes + level
            at, lanes = share(rows, axes, (0, 0, 0, 0))
            buffers.append(pltpu.VMEM((len(level_steps(level)), at.size, lanes.size), BF16))
        return buffers

    def crossing(rows, levels):
        at, lanes = share(rows, "".join(levels), (0, 0, 0, 0))
        return pltpu.VMEM((groups, at.size, lanes.size), BF16)

    scratch = [
        pltpu.VMEM((length, width), BF16),
        pltpu.VMEM((length, width), BF16),
        pltpu.VMEM(wqkv.shape, BF16),
        pltpu.VMEM(wattn.shape, BF16),
        pltpu.VMEM((4, 4, 512, 512), BF16),
        pltpu.VMEM((length, width), BF16),
        pltpu.VMEM((3 * width, length), BF16),
        pltpu.VMEM((width, length), BF16),
        pltpu.VMEM((width // HEAD_DIM, 1, length), F32),
        pltpu.VMEM((length, width), F32),
        pltpu.VMEM((length, width), BF16),
        pltpu.VMEM((2, length, width), BF16),
        pltpu.VMEM((2, length, 512), BF16),
        pltpu.VMEM((2, length, 512), BF16),
        pltpu.VMEM((length, width), F32),
        pltpu.VMEM((length, width), F32),
        pltpu.VMEM((width, length), BF16),
        pltpu.VMEM((1, length), F32),
        pltpu.VMEM((16, length), BF16),
        pltpu.VMEM((144, length), BF16),
        pltpu.VMEM((144, length), BF16),
        pltpu.VMEM((80, length), BF16),
        pltpu.VMEM((80, length), BF16),
        pltpu.VMEM((HEAD_DIM, length), F32),
        pltpu.VMEM((HEAD_DIM, length), F32),
        pltpu.VMEM((2, 1, 512), F32),
        pltpu.VMEM((4, 2, 512, 512), BF16),
        pltpu.VMEM((2, 512, 512), BF16),
        pltpu.VMEM((2, 256, 512), BF16),
        pltpu.VMEM((2, 256, 512), BF16),
        pltpu.VMEM((2, 512, 512), BF16),
        pltpu.VMEM((2, 256, 512), BF16),
        pltpu.VMEM((4, 512, 512), BF16),
        by_round(),
        [level_buffers(rows, levels) for rows, levels in zip(ROUNDS, LEVELS)],
        [crossing(rows, levels) for rows, levels in zip(ROUNDS, LEVELS)],
        by_round(),
        pltpu.VMEM((4, 8, width), F32),
        pltpu.VMEM((experts + groups, 8, width), F32),
        pltpu.SemaphoreType.DMA((8,)),
        pltpu.SemaphoreType.DMA((19,)),
        pltpu.SemaphoreType.DMA((semaphores,)),
        pltpu.SemaphoreType.DMA((semaphores,)),
    ]
    return pl.pallas_call(
        functools.partial(kernel, experts),
        in_specs=[hbm, hbm, vmem, smem] + [vmem] * 4 + [hbm, hbm, vmem, hbm, hbm],
        out_specs=[hbm] * 6 + [vmem] * 2,
        out_shape=[
            shape(tokens.shape, BF16),
            shape(tokens.shape, BF16),
            shape(expert_in.shape, BF16),
            shape(expert_out.shape, BF16),
            shape((3 * width, width), BF16),
            shape(wattn.shape, BF16),
            shape((8, width), F32),
            shape((1, 2), F32),
        ],
        scratch_shapes=scratch,
        compiler_params=pltpu.CompilerParams(
            vmem_limit_bytes=63 * 1024 * 1024, collective_id=0, has_side_effects=True
        ),
    )(
        tokens, cotangent, segments, live, ln1_gain, ln1_bias, ln2_gain, ln2_bias, wqkv, wattn, logits,
        expert_in, expert_out,
    )


def body(
    tokens, segment_ids, live_tokens, cotangent, ln1_gain, ln1_bias, qkv_weight, attn_weight,
    ln2_gain, ln2_bias, task_logits, expert_in, expert_out,
):
    out, grad_in, in_grad, out_grad, qkv_grad, attn_grad, vectors, logits_grad = one_device(
        lax.axis_size("expert"), tokens[0], cotangent[0], segment_ids, live_tokens, ln1_gain, ln1_bias,
        ln2_gain, ln2_bias, qkv_weight, attn_weight, task_logits, expert_in[0], expert_out[0],
    )
    (
        out, grad_in, gain1, bias1, qkv_grad, attn_grad, gain2, bias2, in_grad, out_grad
    ) = widen(out, grad_in, in_grad, out_grad, qkv_grad, attn_grad, vectors)
    return (
        out[None], grad_in[None], gain1, bias1, qkv_grad, attn_grad, gain2, bias2, logits_grad,
        in_grad[None], out_grad[None],
    )


def solution(mesh):
    rows = ("expert", "dp")
    in_specs = (
        P(rows, None, None), P(rows, None), P(rows), P(rows, None, None), P(), P(), P(), P(), P(), P(),
        P("expert", None), P("expert", None, None), P("expert", None, None),
    )
    out_specs = (
        P(rows, None, None), P(rows, None, None), P(), P(), P(), P(), P(), P(),
        P("expert", None), P("expert", None, None), P("expert", None, None),
    )
    return jax.shard_map(body, mesh=mesh, in_specs=in_specs, out_specs=out_specs, check_vma=False)
```

```python
import functools
import itertools

import jax
import jax.numpy as jnp
from jax import lax
from jax.experimental import pallas as pl
from jax.experimental.pallas import tpu as pltpu
from jax.sharding import PartitionSpec as P

F32 = jnp.float32
BF16 = jnp.bfloat16
HEAD_DIM = 64
NORM_EPS = 1e-05
MASKED = -1e30
LOG2E = 1.4426950408889634
GELU_A = 0.7978845608028654
GELU_B = 0.044715


def dot_nn(a, b):
    return jnp.dot(a, b, preferred_element_type=F32)


def dot_nt(a, b):
    return lax.dot_general(a, b, (((1,), (1,)), ((), ())), preferred_element_type=F32)


def dot_tn(a, b):
    return lax.dot_general(a, b, (((0,), (0,)), ((), ())), preferred_element_type=F32)


def dot_tt(a, b):
    return lax.dot_general(a, b, (((0,), (1,)), ((), ())), preferred_element_type=F32)


def norm_parts(inputs):
    row_mean = jnp.mean(inputs, axis=-1, keepdims=True)
    centred = inputs - row_mean
    variance = jnp.mean(centred * centred, axis=-1, keepdims=True)
    inverse = lax.rsqrt(variance + NORM_EPS)
    return centred * inverse, inverse


def norm_back(scaled, normal, inverse):
    return inverse * (
        scaled
        - jnp.mean(scaled, axis=-1, keepdims=True)
        - normal * jnp.mean(scaled * normal, axis=-1, keepdims=True)
    )


def split_three(value):
    high = value.astype(BF16)
    rest = value - high.astype(F32)
    middle = rest.astype(BF16)
    low = (rest - middle.astype(F32)).astype(BF16)
    return high.astype(F32), middle.astype(F32), low.astype(F32)


def scaled_queries(queries):
    scaled = queries.astype(F32) * (LOG2E * HEAD_DIM ** (-0.5))
    high = scaled.astype(BF16)
    return high, (scaled - high.astype(F32)).astype(BF16)


def mask_rows(segments, live, length):
    position = lax.broadcasted_iota(jnp.int32, (16, length), 1)
    row = lax.broadcasted_iota(jnp.int32, (16, length), 0)
    segment = jnp.broadcast_to(segments, (16, length))
    alive = position < live
    for_query = jnp.where(
        row < 8,
        jnp.where(segment != row, MASKED, 0.0),
        jnp.where((row == 8) & alive, MASKED, 0.0),
    )
    for_key = jnp.where(
        row < 8,
        jnp.where(segment == row, 1.0, 0.0),
        jnp.where((row == 8) & (~alive), 1.0, 0.0),
    )
    for_key_back = jnp.where((row >= 9) & (row < 12), 1.0, for_key)
    return for_query, for_key, for_key_back


def head_rows(head, part, width):
    return pl.ds(pl.multiple_of(part * width + head * HEAD_DIM, HEAD_DIM), HEAD_DIM)


def key_band(start, size, tile, length):
    low = max(0, (start - 511) // tile * tile)
    high = min(length, -(-(start + size + 511) // tile) * tile)
    return low, high


def attend_forward(head, qkv_t, ctx_t, lse, mask_q, alive_row, q_aug, k_aug, v_aug, tile):
    width, length = ctx_t.shape
    high, low = scaled_queries(qkv_t[head_rows(head, 0, width), :])
    q_aug[0:64, :] = high
    q_aug[64:128, :] = low
    q_aug[128:144, :] = mask_q[...]
    keys = qkv_t[head_rows(head, 1, width), :]
    k_aug[0:64, :] = keys
    k_aug[64:128, :] = keys
    v_aug[0:64, :] = qkv_t[head_rows(head, 2, width), :]
    for start in range(0, length, tile):
        at = pl.ds(start, tile)
        scores = dot_tn(k_aug[...], q_aug[:, at])
        top = jnp.max(scores, axis=0, keepdims=True)
        weights = jnp.exp2(scores - top)
        total = jnp.sum(weights, axis=0, keepdims=True)
        context = dot_nn(v_aug[0:64, :], (weights * (1.0 / total)).astype(BF16))
        own = v_aug[0:64, at].astype(F32)
        ctx_t[head_rows(head, 0, width), at] = jnp.where(
            alive_row[:, at] > 0, context, own
        ).astype(BF16)
        lse[head, :, at] = top + jnp.log(total) * LOG2E


def attend_backward_begin(head, qkv_t, dctx_t, ctx_t, lse, mask_q, q_aug, k_aug, v_aug, d_aug, dk, dv):
    width, length = ctx_t.shape
    row = lax.broadcasted_iota(jnp.int32, (16, length), 0)
    high, low = scaled_queries(qkv_t[head_rows(head, 0, width), :])
    q_aug[0:64, :] = high
    q_aug[64:128, :] = low
    one, two, three = split_three(-lse[head])
    q_aug[128:144, :] = jnp.where(
        row == 9, one, jnp.where(row == 10, two, jnp.where(row == 11, three, mask_q[...].astype(F32)))
    ).astype(BF16)
    keys = qkv_t[head_rows(head, 1, width), :]
    k_aug[0:64, :] = keys
    k_aug[64:128, :] = keys
    v_aug[0:64, :] = qkv_t[head_rows(head, 2, width), :]
    grad = dctx_t[head_rows(head, 0, width), :]
    d_aug[0:64, :] = grad
    context = ctx_t[head_rows(head, 0, width), :].astype(F32)
    one, two, three = split_three(
        -jnp.sum(grad.astype(F32) * context, axis=0, keepdims=True)
    )
    d_aug[64:80, :] = jnp.where(
        row == 0, one, jnp.where(row == 1, two, jnp.where(row == 2, three, 0.0))
    ).astype(BF16)
    dk[...] = jnp.zeros(dk.shape, F32)
    dv[...] = jnp.zeros(dv.shape, F32)


def attend_backward_tile(head, qkv_t, q_aug, k_aug, v_aug, d_aug, dk, dv, start, tile):
    length = qkv_t.shape[1]
    queries = head_rows(head, 0, qkv_t.shape[0] // 3)
    first, last = key_band(start, tile, tile, length)
    at, near = pl.ds(start, tile), pl.ds(first, last - first)
    weights = jnp.exp2(dot_tn(q_aug[:, at], k_aug[:, near]))
    dweights = dot_tn(d_aug[:, at], v_aug[:, near])
    dscores = (weights * dweights).astype(BF16)
    dv[:, near] += dot_nn(d_aug[0:64, at], weights.astype(BF16))
    dk[:, near] += dot_nn(qkv_t[queries, at], dscores)
    qkv_t[queries, at] = (dot_nt(k_aug[0:64, near], dscores) * HEAD_DIM ** (-0.5)).astype(BF16)


def attend_backward_end(head, qkv_t, dk, dv):
    width = qkv_t.shape[0] // 3
    qkv_t[head_rows(head, 1, width), :] = (dk[...] * HEAD_DIM ** (-0.5)).astype(BF16)
    qkv_t[head_rows(head, 2, width), :] = dv[...].astype(BF16)


def gelu_parts(u):
    square = u * u
    bend = jnp.tanh(u * (GELU_A + (GELU_A * GELU_B) * square))
    half = 0.5 + 0.5 * bend
    slope = half + (0.5 * u) * (1.0 - bend * bend) * (GELU_A + (3.0 * GELU_A * GELU_B) * square)
    return u * half, slope


MESH = pl.DeviceIdType.MESH
GROUP = 8


class Numbers:
    def __init__(self):
        self.used = 0

    def take(self, count):
        first = self.used
        self.used += count
        return first


def number_copies(groups):
    numbers = Numbers()
    names = {}
    for name, count in [
        ("w1x", 2), ("w1y", 2), ("w1c", 1), ("w1d", 2), ("w2a", 2), ("w2b", 2), ("w2c", 1), ("w2d", 1),
        ("w3x", 2), ("w3y", 2), ("w3c", 1), ("w3d", 2), ("gc", 8), ("g1", 4), ("g3y", 4), ("g3x", 4),
        ("gzu", 2), ("gzm", 4), ("gyr", 2), ("gya", 4), ("gfa", 4), ("gfb", 4),
        ("vec_dp", 3), ("vec_ex", GROUP - 1), ("vec_far", groups - 1),
    ]:
        names[name] = numbers.take(count)
    for index, levels in enumerate(LEVELS):
        copies = sum(len(level_steps(level)) for level in levels)
        names["sum", index] = numbers.take(2 * copies + groups - 1)
    return names, numbers.used


ROUNDS = (512, 384, 384, 384, 384)
LEVELS = (("c", "x", "yz"), ("c", "y", "xz"), ("c", "x", "yz"), ("c", "y", "xz"), ("c", "x", "yz"))
ORDER = {
    "h0": [("a", 0, 0), ("p", "y"), ("y", "y"), ("x", 0), ("p", "n"), ("x", 1)],
    "h1": [("a", 0, 1), ("x", 2)],
    "h2": [("a", 1, 0), ("z", 0), ("x", 3), ("y", "n")],
    "h3": [("a", 1, 1), ("z", 1)],
    "h4": [("a", 2, 0), ("a", 0, 2)],
    "h5": [("a", 2, 1), ("z", 2)],
    "h6": [("a", 3, 0), ("z", 3), ("f", 0), ("f", 1)],
    "h7": [("a", 1, 2), ("a", 3, 1), ("a", 2, 2)],
    "E": [("a", 4, 0), ("a", 0, 3), ("f", 2), ("l", 0)],
    "L1": [("f", 3), ("a", 4, 1)],
    "L2": [("a", 1, 3), ("l", 1)],
    "L3": [("a", 3, 2)],
    "L4": [("a", 4, 2), ("a", 2, 3)],
    "tail": [
        ("a", 0, 4), ("a", 1, 4), ("l", 2), ("a", 3, 3), ("l", 3), ("a", 0, 5), ("a", 4, 3), ("a", 0, 6),
        ("vex",), ("a", 2, 4), ("a", 1, 5), ("a", 3, 4), ("a", 1, 6), ("a", 4, 4), ("a", 2, 5), ("a", 3, 5),
        ("a", 2, 6), ("vend",), ("a", 3, 6), ("a", 4, 5), ("a", 4, 6),
    ],
}
AXES = {"x": 2, "y": 2, "c": 2, "z": GROUP // 2}


def level_steps(level):
    ranges = [range(AXES[axis] if axis in level else 1) for axis in "xycz"]
    return [steps for steps in itertools.product(*ranges) if any(steps)]


def share(rows, axes, place):
    start, first = 0, 0
    count, lanes = rows, 512
    if "x" in axes:
        count = count // AXES["x"]
        start = start + count * place[0]
    if "z" in axes:
        count = count // AXES["z"]
        start = start + count * place[3]
    if "c" in axes:
        lanes = lanes // AXES["c"]
        first = first + lanes * place[2]
    if "y" in axes:
        lanes = lanes // AXES["y"]
        first = first + lanes * place[1]
    rows_at = pl.ds(0, count) if isinstance(start, int) else pl.ds(pl.multiple_of(start, 16), count)
    return rows_at, pl.ds(pl.multiple_of(first, 128), lanes)


def kernel(
    experts,
    tokens, cotangent, segments_in, live, ln1_gain_in, ln1_bias_in, ln2_gain_in, ln2_bias_in, wqkv_in,
    wattn_in, logits_in, expert_in, expert_out,
    out, grad_in, in_grad, out_grad, qkv_grad, attn_grad, vectors_out, logits_grad_out,
    segments, ln1_gain, ln1_bias, ln2_gain, ln2_bias, logits, vectors, logits_grad,
    x, dy, wqkv, wattn, w, a1, qkv_t, ctx_t, lse, mid, a2, dz, hid, dpre, total, da2,
    dctx_t, alive_row, mask_q, q_aug, k_aug, v_aug, d_aug, dk, dv, gate_sum,
    rc, r1, r3y, r3x, rz, ryr, fin, part, landed, across, done, vec_dp, vec_ex, vec_sum,
    load_sem, store_sem, send_sem, recv_sem,
):
    length, width = x.shape
    tile = 256
    groups = experts // GROUP
    names, _ = number_copies(groups)
    expert = lax.axis_index("expert")
    dp = lax.axis_index("dp")
    core, row_y = dp % 2, dp // 2
    dp_core = dp + 1 - 2 * core
    here = (expert % 2, row_y, core, expert % GROUP // 2)
    dp_y = (dp + 2) % 4
    place = expert % GROUP
    base = expert - place
    mate_core = (expert, dp_core)
    mate_y = (expert, dp_y)
    mate_x = (expert + 1 - 2 * (expert % 2), dp)
    above = ((expert + 2) % experts, dp)
    below = ((expert + experts - 2) % experts, dp)

    def copy(src, dst, index, device):
        return pltpu.make_async_remote_copy(
            src_ref=src, dst_ref=dst, send_sem=send_sem.at[index], recv_sem=recv_sem.at[index],
            device_id=device, device_id_type=MESH,
        )

    def peer(step):
        return (base + (place + step) % GROUP, dp)

    def far(step):
        return ((expert + GROUP * step) % experts, dp)

    barrier = pltpu.get_barrier_semaphore()
    others = [mate_core, mate_y, mate_x, above, below] + [far(step) for step in range(1, groups)]
    for other in others:
        pl.semaphore_signal(barrier, inc=1, device_id=other, device_id_type=MESH)

    loads = [
        pltpu.make_async_copy(src, dst, load_sem.at[i])
        for i, (src, dst) in enumerate(
            [
                (expert_in.at[:, pl.ds(0, 512)], w.at[0, 0]),
                (expert_out.at[pl.ds(0, 512), :], w.at[0, 1]),
                (expert_in.at[:, pl.ds(512, 512)], w.at[0, 2]),
                (expert_out.at[pl.ds(512, 512), :], w.at[0, 3]),
                (tokens, x),
                (wqkv_in, wqkv),
                (wattn_in, wattn),
                (cotangent, dy),
                (segments_in, segments),
                (ln1_gain_in, ln1_gain),
                (ln1_bias_in, ln1_bias),
                (ln2_gain_in, ln2_gain),
                (ln2_bias_in, ln2_bias),
                (logits_in, logits),
            ]
        )
    ]
    for load in loads[8:] + loads[4:5] + loads[:4] + loads[5:8]:
        load.start()
    live_count = live[0]
    alive_row[...] = jnp.where(
        lax.broadcasted_iota(jnp.int32, (1, length), 1) < live_count, 1.0, 0.0
    )
    for load in loads[8:]:
        load.wait()
    for_query, for_key, for_key_back = mask_rows(segments[...], live_count, length)
    mask_q[...] = for_query.astype(BF16)
    for head in range(2):
        k_aug[head, 128:144, :] = for_key.astype(BF16)
    gain1, bias1, gain2, bias2 = (
        ref[...].astype(F32).reshape(1, width) for ref in (ln1_gain, ln1_bias, ln2_gain, ln2_bias)
    )
    exponent = jnp.exp(logits[...] - jnp.max(logits[...], axis=1, keepdims=True))
    gates = exponent / jnp.sum(exponent, axis=1, keepdims=True)

    def halves(name, slot, unit, to_slot, device):
        return [
            copy(
                w.at[slot, unit, pl.ds(256 * h, 256), :], w.at[to_slot, unit, pl.ds(256 * h, 256), :],
                names[name] + h, device,
            )
            for h in range(2)
        ]

    w1x = halves("w1x", 0, dp, 1, mate_x)
    w1y = halves("w1y", 1, dp, 1, mate_y)
    w1d = halves("w1d", 1, dp_y, 1, mate_core)
    w1c = copy(w.at[1, dp], w.at[1, dp], names["w1c"], mate_core)
    w2a = halves("w2a", 0, dp, 2, below)
    w2b = halves("w2b", 0, dp_y, 2, below)
    w2c = copy(w.at[2, dp], w.at[2, dp], names["w2c"], mate_core)
    w2d = copy(w.at[2, dp_y], w.at[2, dp_y], names["w2d"], mate_core)
    w3x = halves("w3x", 2, dp, 3, mate_x)
    w3y = halves("w3y", 3, dp, 3, mate_y)
    w3d = halves("w3d", 3, dp_y, 3, mate_core)
    w3c = copy(w.at[3, dp], w.at[3, dp], names["w3c"], mate_core)

    loads[4].wait()
    for start in range(0, length, tile):
        at = pl.ds(start, tile)
        normal, inverse = norm_parts(x[at, :].astype(F32))
        a1[at, :] = (normal * gain1 + bias1).astype(BF16)
    for load in loads[:4]:
        load.wait()
    pl.semaphore_wait(barrier, len(others))
    for h in range(2):
        w1x[h].start()
        w2a[h].start()
    for h in range(2):
        w2b[h].start()

    loads[5].wait()
    for start in range(0, 3 * width, 512):
        at = pl.ds(start, 512)
        qkv_t[at, :] = dot_tt(wqkv[:, at], a1[...]).astype(BF16)

    def forward_heads(pair, carry):
        @pl.when(pair == 2)
        def _():
            w1x[0].wait_recv()
            w1y[0].start()
            w2a[0].wait_recv()
            w3x[0].start()

        for head in range(2):
            attend_forward(
                2 * pair + head, qkv_t, ctx_t, lse, mask_q, alive_row, q_aug.at[head], k_aug.at[head],
                v_aug.at[head], length,
            )
        return carry

    lax.fori_loop(0, width // HEAD_DIM // 2, forward_heads, 0)
    w1x[1].wait_recv()
    w1y[1].start()
    w1c.start()
    w2a[1].wait_recv()
    w3x[1].start()
    w2c.start()

    loads[6].wait()
    loads[7].wait()
    for start in range(0, length, tile):
        at = pl.ds(start, tile)
        middle = x[at, :].astype(F32) + dot_tn(ctx_t[:, at], wattn[...])
        mid[at, :] = middle
        total[at, :] = middle
        normal, inverse = norm_parts(middle)
        a2[at, :] = (normal * gain2 + bias2).astype(BF16)
        alive = start + lax.broadcasted_iota(jnp.int32, (tile, 1), 0) < live_count
        live_dy = jnp.where(alive, dy[at, :], jnp.zeros((), BF16))
        dy[at, :] = live_dy
        for k in range(2):
            dz[k, at, :] = (gates[:, k : k + 1] * live_dy.astype(F32)).astype(BF16)
    da2[...] = jnp.zeros(da2.shape, F32)
    gate_sum[...] = jnp.zeros(gate_sum.shape, F32)

    def add_into(target, *terms):
        value = target[...].astype(F32)
        for term in terms:
            value = value + term[...].astype(F32)
        target[...] = value.astype(BF16)

    own_rows = pl.ds(pl.multiple_of(256 * row_y, 256), 256)
    other_rows = pl.ds(pl.multiple_of(256 * (1 - row_y), 256), 256)

    def unit(slot, chunk, rows=pl.ds(0, 512)):
        return w.at[slot, 2 * chunk + core, rows, :]

    def gc(slot, chunk):
        return copy(
            w.at[slot, 2 * chunk + 1 - core], rc.at[slot, chunk], names["gc"] + 2 * slot + chunk, mate_core
        )

    def add_core(slot, chunk):
        gc(slot, chunk).wait_recv()
        add_into(unit(slot, chunk), rc.at[slot, chunk])

    def g1(chunk, h):
        rows = pl.ds(256 * h, 256)
        return copy(unit(1, chunk, rows), r1.at[chunk, rows, :], names["g1"] + 2 * chunk + h, mate_x)

    def final(chunk, rows):
        return fin.at[2 * chunk + core, rows, :]

    def quarter(own, h):
        start = row_y if own else 1 - row_y
        return pl.ds(pl.multiple_of(256 * start + 128 * h, 128), 128)

    def pieces(name, device, src, dst):
        return [
            copy(src(k, h), dst(k, h), names[name] + 2 * k + h, device) for k in range(2) for h in range(2)
        ]

    def half_of(ref, k, h):
        return ref.at[k, pl.ds(128 * h, 128), :]

    g3y = pieces("g3y", mate_y, lambda k, h: unit(3, k, quarter(False, h)), functools.partial(half_of, r3y))
    g3x = pieces("g3x", mate_x, lambda k, h: unit(3, k, quarter(True, h)), functools.partial(half_of, r3x))
    gzm = pieces(
        "gzm", above, lambda k, h: unit(2, k, quarter(True, h)), lambda k, h: rz.at[k, quarter(True, h), :]
    )

    def gzu(chunk):
        return copy(unit(2, chunk, other_rows), rz.at[chunk, other_rows, :], names["gzu"] + chunk, above)

    def gyr(chunk):
        return copy(unit(0, chunk, other_rows), ryr.at[chunk], names["gyr"] + chunk, mate_y)

    def own_final(k, h):
        return final(k, quarter(True, h))

    def other_final(k, h):
        return final(k, quarter(False, h))

    gya = pieces("gya", mate_y, own_final, own_final)
    gfa = pieces("gfa", mate_core, own_final, own_final)
    gfb = pieces("gfb", mate_core, other_final, other_final)

    def slot_pair(turn, carry):
        later = turn // 3
        slots = (2 * ((turn + 3) // 4) + (turn % 3) // 2, 1 + 2 * ((turn % 3) // 2) - later)
        flips = (later, (turn + 2) // 3)
        chunks = tuple(row_y + flip * (1 - 2 * row_y) for flip in flips)

        def part_of(index, at):
            slot, chunk = slots[index], chunks[index]
            k = slot // 2
            w_in, w_out = w.at[slot, 2 * chunk], w.at[slot, 2 * chunk + 1]
            hidden, slope = gelu_parts(dot_nn(a2[at, :], w_in[...]))
            hid[index, at, :] = hidden.astype(BF16)
            dhidden = dot_nt(dz[k, at, :], w_out[...])
            dpre[index, at, :] = (dhidden * slope).astype(BF16)

        blocks = [pl.ds(start, 512) for start in range(0, length, 512)]

        @pl.when(turn == 1)
        def _():
            w1y[1].wait_recv()
            w1d[1].start()
            w2c.wait_recv()

        @pl.when(turn == 2)
        def _():
            w3c.wait_recv()
            w3y[0].wait_recv()
            w3d[0].start()

        @pl.when(turn == 3)
        def _():
            w2d.wait_recv()

        for at in blocks:
            part_of(0, at)

        @pl.when(turn == 0)
        def _():
            w3x[0].wait_recv()
            w3y[0].start()
            w1y[0].wait_recv()
            w1d[0].start()
            w1c.wait_recv()

        @pl.when(turn == 1)
        def _():
            w3x[1].wait_recv()
            w3y[1].start()
            w3c.start()
            for h in range(2):
                w2b[h].wait_recv()
            w2d.start()
            for h in range(2):
                w1d[h].wait_recv()

        @pl.when(turn == 2)
        def _():
            w3y[1].wait_recv()
            w3d[1].start()
            add_core(2, row_y)
            add_core(1, 1 - row_y)
            for h in range(2):
                g1(1 - row_y, h).start()
            gzu(row_y).start()
            for h in range(2):
                w3d[h].wait_recv()

        for at in blocks:
            part_of(1, at)
            value = total[at, :]
            back = da2[at, :]
            live_dy = dy[at, :].astype(F32)
            for index in range(2):
                slot, chunk = slots[index], chunks[index]
                gate = jnp.where(slot < 2, gates[:, 0:1], gates[:, 1:2])
                branch = dot_nn(hid[index, at, :], w[slot, 2 * chunk + 1])
                gate_sum[slot // 2] += jnp.sum(branch * live_dy, axis=0, keepdims=True)
                value = value + gate * branch
                back = back + dot_nt(dpre[index, at, :], w[slot, 2 * chunk])
            total[at, :] = value
            da2[at, :] = back

        @pl.when(turn == 0)
        def _():
            for each in w1x + w2a + w1y + [w1c]:
                each.wait_send()

        @pl.when(turn == 1)
        def _():
            for each in w3x + w1d + [w2c]:
                each.wait_send()
            add_core(0, row_y)
            add_core(1, row_y)
            for h in range(2):
                g1(row_y, h).start()

        @pl.when(turn == 2)
        def _():
            for each in w3y + w3d + [w3c]:
                each.wait_send()

        @pl.when(turn == 3)
        def _():
            for each in w2b + [w2d]:
                each.wait_send()
            for k in range(2):
                add_core(3, k)
                for h in range(2):
                    g3y[2 * k + h].start()

        for index in range(2):
            slot, chunk = slots[index], chunks[index]
            k = slot // 2
            w[slot, 2 * chunk] = dot_tn(a2[...], dpre[index]).astype(BF16)
            w[slot, 2 * chunk + 1] = dot_tn(hid[index], dz[k]).astype(BF16)
            gc(slot, chunk).start()
        return carry

    lax.fori_loop(0, 4, slot_pair, 0)

    gain_sum = jnp.zeros((1, width), F32)
    bias_sum = jnp.zeros((1, width), F32)
    for start in range(0, length, tile):
        at = pl.ds(start, tile)
        normal, inverse = norm_parts(mid[at, :])
        grad = da2[at, :]
        gain_sum += jnp.sum(grad * normal, axis=0, keepdims=True)
        bias_sum += jnp.sum(grad, axis=0, keepdims=True)
        dmid = dy[at, :].astype(F32) + norm_back(grad * gain2, normal, inverse)
        mid[at, :] = dmid
        a2[at, :] = dmid.astype(BF16)
    vectors[2:3, :] = gain_sum
    vectors[3:4, :] = bias_sum
    vectors[4:5, :] = gate_sum[0]
    vectors[5:6, :] = gate_sum[1]
    vectors[6:8, :] = jnp.zeros((2, width), F32)
    add_core(2, 1 - row_y)
    gzu(1 - row_y).start()
    add_core(0, 1 - row_y)
    dctx_t[...] = dot_nt(wattn[...], a2[...]).astype(BF16)

    def sum_round(index):
        rows, levels = ROUNDS[index], LEVELS[index]
        mine, cross, result = part[index], across[index], done[index]
        number = names["sum", index]
        scatter, gather, done_axes = [], [], []
        axes = ""
        for level, buffer in zip(levels, landed[index]):
            axes = axes + level
            done_axes.append(axes)
            there, back = [], []
            for slot, steps in enumerate(level_steps(level)):
                x_there = here[0] + steps[0] * (1 - 2 * here[0])
                y_there = here[1] + steps[1] * (1 - 2 * here[1])
                c_there = here[2] + steps[2] * (1 - 2 * here[2])
                z_there = (here[3] + steps[3]) % AXES["z"]
                device = (base + 2 * z_there + x_there, 2 * y_there + c_there)
                away = share(rows, axes, (x_there, y_there, c_there, z_there))
                there.append(copy(mine.at[away], buffer.at[slot], number, device))
                at = share(rows, axes, here)
                back.append(copy(result.at[at], result.at[at], number + 1, device))
                number += 2
            scatter.append(there)
            gather.append(back)
        over = [copy(cross.at[0], cross.at[s], number + s - 1, far(s)) for s in range(1, groups)]
        last = len(levels) - 1

        def start_all(copies):
            for each in copies:
                each.start()

        def wait_all(copies):
            for each in copies:
                each.wait_recv()

        def begin():
            start_all(scatter[0])

        def add_up(level):
            wait_all(scatter[level])
            at = share(rows, done_axes[level], here)
            value = mine[at].astype(F32)
            for slot in range(len(scatter[level])):
                value = value + landed[index][level][slot].astype(F32)
            if level < last:
                mine[at] = value.astype(BF16)
                start_all(scatter[level + 1])
                return
            if groups > 1:
                cross[0] = value.astype(BF16)
                start_all(over)
                wait_all(over)

                def add_group(group, value):
                    step = (expert // GROUP - group + groups) % groups
                    return value + cross[step].astype(F32)

                value = lax.fori_loop(0, groups, add_group, jnp.zeros(value.shape, F32))
            result[at] = value.astype(BF16)
            start_all(gather[last])

        def pass_back(level):
            wait_all(gather[level])
            if level > 0:
                start_all(gather[level - 1])

        def finish():
            for copies in scatter + gather + [over]:
                for each in copies:
                    each.wait_send()

        steps = [begin] + [functools.partial(add_up, level) for level in range(last + 1)]
        steps += [functools.partial(pass_back, level) for level in range(last, -1, -1)]
        return steps, finish

    rounds = [sum_round(index) for index in range(len(ROUNDS))]
    def advance(index, step):
        steps = rounds[index][0]
        if step == 0 and index == 0:
            part[0][...] = dot_nn(ctx_t[...], a2[...]).astype(BF16)
        elif step == 0:
            qkv_rows(index - 1)
        steps[step]()
        if step == len(steps) - 1 and index == 0:
            store(done[0], attn_grad)
        elif step == len(steps) - 1:
            store_pair(index - 1)

    for head in range(2):
        k_aug[head, 128:144, :] = for_key_back.astype(BF16)
        v_aug[head, 64:80, :] = jnp.where(
            lax.broadcasted_iota(jnp.int32, (16, length), 0) < 3, 1.0, 0.0
        ).astype(BF16)

    def qkv_rows(pair):
        for index in range(3):
            at = pl.ds(index * width + 128 * pair, 128)
            part[1 + pair][128 * index : 128 * index + 128, :] = dot_nn(qkv_t[at, :], a1[...]).astype(BF16)

    def take_x(p):
        g3y[p].wait_recv()
        add_into(unit(3, p // 2, quarter(True, p % 2)), half_of(r3y, p // 2, p % 2))
        g3x[p].start()

    def take_z(p):
        g3x[p].wait_recv()
        add_into(unit(2, p // 2, quarter(True, p % 2)), half_of(r3x, p // 2, p % 2))
        gzm[p].start()

    def take_partner(k):
        for h in range(2):
            g1(k, h).wait_recv()
        add_into(unit(0, k), r1.at[k])

    def take_y(k):
        gzu(k).wait_recv()
        add_into(unit(0, k, other_rows), rz.at[k, other_rows, :])
        gyr(k).start()

    def take_final(p):
        k, h = p // 2, p % 2
        if h == 0:
            gyr(k).wait_recv()
        gzm[p].wait_recv()
        value = unit(0, k, quarter(True, h))[...].astype(F32) + rz[k, quarter(True, h), :].astype(F32)
        own_final(k, h)[...] = (value + ryr[k, pl.ds(128 * h, 128), :].astype(F32)).astype(BF16)
        gya[p].start()
        gfa[p].start()

    def take_last(p):
        gya[p].wait_recv()
        gfb[p].start()

    def take(steps):
        for name, *which in steps:
            if name == "a":
                advance(*which)
            elif name == "x":
                take_x(*which)
            elif name == "z":
                take_z(*which)
            elif name == "p":
                take_partner(row_y if which[0] == "y" else 1 - row_y)
            elif name == "y":
                take_y(row_y if which[0] == "y" else 1 - row_y)
            elif name == "f":
                take_final(*which)
            elif name == "l":
                take_last(*which)
            elif name == "vex":
                vectors_over_experts()
            else:
                vectors_end()

    def backward_heads(pair, carry):
        def hook(part_of_pair):
            for index in range(part_of_pair, width // HEAD_DIM, 2):
                pl.when(2 * pair + part_of_pair == index)(functools.partial(take, ORDER[f"h{index}"]))

        buffers = [[ref.at[head] for ref in (q_aug, k_aug, v_aug, d_aug, dk, dv)] for head in range(2)]
        hook(0)
        for head in range(2):
            attend_backward_begin(2 * pair + head, qkv_t, dctx_t, ctx_t, lse, mask_q, *buffers[head])
        for start in range(0, length, tile):
            if start == length // 2:
                hook(1)
            for head in range(2):
                attend_backward_tile(2 * pair + head, qkv_t, *buffers[head], start, tile)
        for head in range(2):
            attend_backward_end(2 * pair + head, qkv_t, dk.at[head], dv.at[head])
        return carry

    lax.fori_loop(0, width // HEAD_DIM // 2, backward_heads, 0)
    take(ORDER["E"])

    stores = []

    def store(src, dst):
        stores.append(pltpu.make_async_copy(src, dst, store_sem.at[len(stores)]))
        stores[-1].start()

    dz[0] = total[...].astype(BF16)
    store(dz.at[0], out)
    gain_sum = jnp.zeros((1, width), F32)
    bias_sum = jnp.zeros((1, width), F32)
    for index, start in enumerate(range(0, length, tile)):
        at = pl.ds(start, tile)
        grad = dot_tt(qkv_t[:, at], wqkv[...])
        normal, inverse = norm_parts(x[at, :].astype(F32))
        gain_sum += jnp.sum(grad * normal, axis=0, keepdims=True)
        bias_sum += jnp.sum(grad, axis=0, keepdims=True)
        a2[at, :] = (mid[at, :] + norm_back(grad * gain1, normal, inverse)).astype(BF16)
        take(ORDER[f"L{index + 1}"])
    store(a2, grad_in)
    vectors[0:1, :] = gain_sum
    vectors[1:2, :] = bias_sum

    vec_dp[dp] = vectors[...]
    to_dp = [
        copy(vec_dp.at[dp], vec_dp.at[dp], names["vec_dp"] + s - 1, (expert, (dp + s) % 4))
        for s in range(1, 4)
    ]
    for each in to_dp:
        each.start()
    to_ex = [
        copy(vec_ex.at[expert], vec_ex.at[expert], names["vec_ex"] + s - 1, peer(s))
        for s in range(1, GROUP)
    ]
    sums = [to_dp, to_ex]

    def vectors_over_experts():
        for each in to_dp:
            each.wait_recv()
        row_sum = vec_dp[0] + vec_dp[1] + vec_dp[2] + vec_dp[3]
        vec_ex[expert] = row_sum[0:4, :]
        for each in to_ex:
            each.start()
        scaled = jnp.sum(row_sum[4:6, :], axis=1, keepdims=True)
        pair_lane = lax.broadcasted_iota(jnp.int32, (1, 2), 1)
        dgate = jnp.where(pair_lane == 0, scaled[0:1, :], scaled[1:2, :])
        logits_grad[...] = gates * (dgate - jnp.sum(gates * dgate, axis=1, keepdims=True))

    def vectors_end():
        for each in to_ex:
            each.wait_recv()
        if groups > 1:
            vec_group = vec_ex[base]
            for s in range(1, GROUP):
                vec_group = vec_group + vec_ex[base + s]
            own = experts + expert // GROUP
            vec_ex[own] = vec_group
            to_far = [
                copy(vec_ex.at[own], vec_ex.at[own], names["vec_far"] + s - 1, far(s))
                for s in range(1, groups)
            ]
            for each in to_far:
                each.start()
            for each in to_far:
                each.wait_recv()
            sums.append(to_far)
            value = vec_ex[experts]
            for s in range(1, groups):
                value = value + vec_ex[experts + s]
        else:
            value = vec_ex[0]
            for s in range(1, GROUP):
                value = value + vec_ex[s]
        vec_sum[...] = value
        store(vec_sum, vectors_out)
        store(logits_grad, logits_grad_out)

    def store_pair(pair):
        for index in range(3):
            store(
                done[1 + pair].at[pl.ds(128 * index, 128), :],
                qkv_grad.at[pl.ds(index * width + 128 * pair, 128), :],
            )

    take(ORDER["tail"])
    for each in gfa + gfb:
        each.wait_recv()
    for chunk in range(2):
        at = pl.ds(512 * chunk, 512)
        store(fin.at[2 * chunk], in_grad.at[:, at])
        store(fin.at[2 * chunk + 1], out_grad.at[at, :])
    for chunk in range(2):
        for slot in range(4):
            gc(slot, chunk).wait_send()
        gzu(chunk).wait_send()
        gyr(chunk).wait_send()
        for h in range(2):
            g1(chunk, h).wait_send()
    for group in [g3y, g3x, gzm, gya, gfa, gfb] + sums:
        for each in group:
            each.wait_send()
    for _, finish in rounds:
        finish()
    for each in stores:
        each.wait()


def last_kernel(
    out_low, grad_low, in_low, outg_low, qkv_low, attn_low, vectors_in, logits_in,
    out, grad_in, gain1, bias1, qkv_grad, attn_grad, gain2, bias2, logits_grad, in_grad, out_grad,
    out_v, grad_v, in_v, outg_v, qkv_v, attn_v, vectors, logits_v, in_f, outg_f, qkv_f, attn_f, rows_f,
    load_sem, store_sem,
):
    loads = [
        pltpu.make_async_copy(src, dst, load_sem.at[i])
        for i, (src, dst) in enumerate(
            [
                (qkv_low, qkv_v), (in_low, in_v), (outg_low, outg_v), (attn_low, attn_v),
                (out_low, out_v), (grad_low, grad_v), (vectors_in, vectors), (logits_in, logits_v),
            ]
        )
    ]
    for each in loads[6:] + loads[:6]:
        each.start()
    stores = []

    def store(src, dst):
        stores.append(pltpu.make_async_copy(src, dst, store_sem.at[len(stores)]))
        stores[-1].start()

    loads[6].wait()
    loads[7].wait()
    for row, target in enumerate([gain1, bias1, gain2, bias2]):
        rows_f[row][...] = vectors[row : row + 1, :].reshape(target.shape)
        store(rows_f[row], target)
    store(logits_v, logits_grad)
    width = attn_v.shape[0]
    loads[0].wait()
    for index in range(3):
        at = pl.ds(index * width, width)
        qkv_f[:, at] = qkv_v[at, :].astype(F32).T
        store(qkv_f.at[:, at], qkv_grad.at[:, at])
    for index, (low, wide, target) in enumerate(
        [(in_v, in_f, in_grad), (outg_v, outg_f, out_grad), (attn_v, attn_f, attn_grad)]
    ):
        loads[1 + index].wait()
        wide[...] = low[...].astype(F32)
        store(wide, target)
    for index, (low, target) in enumerate([(out_v, out), (grad_v, grad_in)]):
        loads[4 + index].wait()
        store(low, target)
    for each in stores:
        each.wait()


def widen(out, grad_in, in_grad, out_grad, qkv_grad, attn_grad, vectors, logits_grad):
    width = attn_grad.shape[0]
    hbm = pl.BlockSpec(memory_space=pl.ANY)
    shape = jax.ShapeDtypeStruct
    low = [out.shape, grad_in.shape, in_grad.shape, out_grad.shape, qkv_grad.shape, attn_grad.shape]
    wide = [in_grad.shape, out_grad.shape, (width, 3 * width), attn_grad.shape]
    vector = shape((width,), F32)
    return pl.pallas_call(
        last_kernel,
        in_specs=[hbm] * 8,
        out_specs=[hbm] * 11,
        out_shape=[
            shape(out.shape, BF16), shape(grad_in.shape, BF16), vector, vector, shape(wide[2], F32),
            shape(wide[3], F32), vector, vector, shape(logits_grad.shape, F32), shape(wide[0], F32),
            shape(wide[1], F32),
        ],
        scratch_shapes=[pltpu.VMEM(each, BF16) for each in low]
        + [pltpu.VMEM(vectors.shape, F32), pltpu.VMEM(logits_grad.shape, F32)]
        + [pltpu.VMEM(each, F32) for each in wide]
        + [[pltpu.VMEM(vector.shape, F32) for _ in range(4)]]
        + [pltpu.SemaphoreType.DMA((8,)), pltpu.SemaphoreType.DMA((13,))],
        compiler_params=pltpu.CompilerParams(vmem_limit_bytes=63 * 1024 * 1024),
    )(out, grad_in, in_grad, out_grad, qkv_grad, attn_grad, vectors, logits_grad)


def one_device(
    experts, tokens, cotangent, segments, live, ln1_gain, ln1_bias, ln2_gain, ln2_bias, wqkv, wattn,
    logits, expert_in, expert_out,
):
    length, width = tokens.shape
    groups = experts // GROUP
    _, semaphores = number_copies(groups)
    smem = pl.BlockSpec(memory_space=pltpu.SMEM)
    hbm = pl.BlockSpec(memory_space=pl.ANY)
    shape = jax.ShapeDtypeStruct

    def by_round(*leading):
        return [pltpu.VMEM((*leading, rows, width), BF16) for rows in ROUNDS]

    def level_buffers(rows, levels):
        axes, buffers = "", []
        for level in levels:
            axes = axes + level
            at, lanes = share(rows, axes, (0, 0, 0, 0))
            buffers.append(pltpu.VMEM((len(level_steps(level)), at.size, lanes.size), BF16))
        return buffers

    def crossing(rows, levels):
        at, lanes = share(rows, "".join(levels), (0, 0, 0, 0))
        return pltpu.VMEM((groups, at.size, lanes.size), BF16)

    scratch = [
        pltpu.VMEM(segments.shape, jnp.int32),
        pltpu.VMEM(ln1_gain.shape, BF16),
        pltpu.VMEM(ln1_bias.shape, BF16),
        pltpu.VMEM(ln2_gain.shape, BF16),
        pltpu.VMEM(ln2_bias.shape, BF16),
        pltpu.VMEM(logits.shape, F32),
        pltpu.VMEM((8, width), F32),
        pltpu.VMEM(logits.shape, F32),
        pltpu.VMEM((length, width), BF16),
        pltpu.VMEM((length, width), BF16),
        pltpu.VMEM(wqkv.shape, BF16),
        pltpu.VMEM(wattn.shape, BF16),
        pltpu.VMEM((4, 4, 512, 512), BF16),
        pltpu.VMEM((length, width), BF16),
        pltpu.VMEM((3 * width, length), BF16),
        pltpu.VMEM((width, length), BF16),
        pltpu.VMEM((width // HEAD_DIM, 1, length), F32),
        pltpu.VMEM((length, width), F32),
        pltpu.VMEM((length, width), BF16),
        pltpu.VMEM((2, length, width), BF16),
        pltpu.VMEM((2, length, 512), BF16),
        pltpu.VMEM((2, length, 512), BF16),
        pltpu.VMEM((length, width), F32),
        pltpu.VMEM((length, width), F32),
        pltpu.VMEM((width, length), BF16),
        pltpu.VMEM((1, length), F32),
        pltpu.VMEM((16, length), BF16),
        pltpu.VMEM((2, 144, length), BF16),
        pltpu.VMEM((2, 144, length), BF16),
        pltpu.VMEM((2, 80, length), BF16),
        pltpu.VMEM((2, 80, length), BF16),
        pltpu.VMEM((2, HEAD_DIM, length), F32),
        pltpu.VMEM((2, HEAD_DIM, length), F32),
        pltpu.VMEM((2, 1, 512), F32),
        pltpu.VMEM((4, 2, 512, 512), BF16),
        pltpu.VMEM((2, 512, 512), BF16),
        pltpu.VMEM((2, 256, 512), BF16),
        pltpu.VMEM((2, 256, 512), BF16),
        pltpu.VMEM((2, 512, 512), BF16),
        pltpu.VMEM((2, 256, 512), BF16),
        pltpu.VMEM((4, 512, 512), BF16),
        by_round(),
        [level_buffers(rows, levels) for rows, levels in zip(ROUNDS, LEVELS)],
        [crossing(rows, levels) for rows, levels in zip(ROUNDS, LEVELS)],
        by_round(),
        pltpu.VMEM((4, 8, width), F32),
        pltpu.VMEM((experts + groups, 4, width), F32),
        pltpu.VMEM((4, width), F32),
        pltpu.SemaphoreType.DMA((14,)),
        pltpu.SemaphoreType.DMA((21,)),
        pltpu.SemaphoreType.DMA((semaphores,)),
        pltpu.SemaphoreType.DMA((semaphores,)),
    ]
    return pl.pallas_call(
        functools.partial(kernel, experts),
        in_specs=[hbm] * 3 + [smem] + [hbm] * 9,
        out_specs=[hbm] * 8,
        out_shape=[
            shape(tokens.shape, BF16),
            shape(tokens.shape, BF16),
            shape(expert_in.shape, BF16),
            shape(expert_out.shape, BF16),
            shape((3 * width, width), BF16),
            shape(wattn.shape, BF16),
            shape((4, width), F32),
            shape((1, 2), F32),
        ],
        scratch_shapes=scratch,
        compiler_params=pltpu.CompilerParams(
            vmem_limit_bytes=63 * 1024 * 1024, collective_id=0, has_side_effects=True
        ),
    )(
        tokens, cotangent, segments, live, ln1_gain, ln1_bias, ln2_gain, ln2_bias, wqkv, wattn, logits,
        expert_in, expert_out,
    )


def body(
    tokens, segment_ids, live_tokens, cotangent, ln1_gain, ln1_bias, qkv_weight, attn_weight,
    ln2_gain, ln2_bias, task_logits, expert_in, expert_out,
):
    out, grad_in, in_grad, out_grad, qkv_grad, attn_grad, vectors, logits_grad = one_device(
        lax.axis_size("expert"), tokens[0], cotangent[0], segment_ids, live_tokens, ln1_gain, ln1_bias,
        ln2_gain, ln2_bias, qkv_weight, attn_weight, task_logits, expert_in[0], expert_out[0],
    )
    (
        out, grad_in, gain1, bias1, qkv_grad, attn_grad, gain2, bias2, logits_grad, in_grad, out_grad
    ) = widen(out, grad_in, in_grad, out_grad, qkv_grad, attn_grad, vectors, logits_grad)
    return (
        out[None], grad_in[None], gain1, bias1, qkv_grad, attn_grad, gain2, bias2, logits_grad,
        in_grad[None], out_grad[None],
    )


def solution(mesh):
    rows = ("expert", "dp")
    in_specs = (
        P(rows, None, None), P(rows, None), P(rows), P(rows, None, None), P(), P(), P(), P(), P(), P(),
        P("expert", None), P("expert", None, None), P("expert", None, None),
    )
    out_specs = (
        P(rows, None, None), P(rows, None, None), P(), P(), P(), P(), P(), P(),
        P("expert", None), P("expert", None, None), P("expert", None, None),
    )
    return jax.shard_map(body, mesh=mesh, in_specs=in_specs, out_specs=out_specs, check_vma=False)
```

```python
import functools
import itertools

import jax
import jax.numpy as jnp
from jax import lax
from jax.experimental import pallas as pl
from jax.experimental.pallas import tpu as pltpu
from jax.sharding import PartitionSpec as P

F32 = jnp.float32
BF16 = jnp.bfloat16
HEAD_DIM = 64
NORM_EPS = 1e-05
MASKED = -1e30
LOG2E = 1.4426950408889634
GELU_A = 0.7978845608028654
GELU_B = 0.044715


def dot_nn(a, b):
    return jnp.dot(a, b, preferred_element_type=F32)


def dot_nt(a, b):
    return lax.dot_general(a, b, (((1,), (1,)), ((), ())), preferred_element_type=F32)


def dot_tn(a, b):
    return lax.dot_general(a, b, (((0,), (0,)), ((), ())), preferred_element_type=F32)


def dot_tt(a, b):
    return lax.dot_general(a, b, (((0,), (1,)), ((), ())), preferred_element_type=F32)


def norm_parts(inputs):
    row_mean = jnp.mean(inputs, axis=-1, keepdims=True)
    centred = inputs - row_mean
    variance = jnp.mean(centred * centred, axis=-1, keepdims=True)
    inverse = lax.rsqrt(variance + NORM_EPS)
    return centred * inverse, inverse


def norm_back(scaled, normal, inverse):
    return inverse * (
        scaled
        - jnp.mean(scaled, axis=-1, keepdims=True)
        - normal * jnp.mean(scaled * normal, axis=-1, keepdims=True)
    )


def split_three(value):
    high = value.astype(BF16)
    rest = value - high.astype(F32)
    middle = rest.astype(BF16)
    low = (rest - middle.astype(F32)).astype(BF16)
    return high.astype(F32), middle.astype(F32), low.astype(F32)


def scaled_queries(queries):
    scaled = queries.astype(F32) * (LOG2E * HEAD_DIM ** (-0.5))
    high = scaled.astype(BF16)
    return high, (scaled - high.astype(F32)).astype(BF16)


def mask_rows(segments, live, length):
    position = lax.broadcasted_iota(jnp.int32, (16, length), 1)
    row = lax.broadcasted_iota(jnp.int32, (16, length), 0)
    segment = jnp.broadcast_to(segments, (16, length))
    alive = position < live
    for_query = jnp.where(
        row < 8,
        jnp.where(segment != row, MASKED, 0.0),
        jnp.where((row == 8) & alive, MASKED, 0.0),
    )
    for_key = jnp.where(
        row < 8,
        jnp.where(segment == row, 1.0, 0.0),
        jnp.where((row == 8) & (~alive), 1.0, 0.0),
    )
    for_key_back = jnp.where((row >= 9) & (row < 12), 1.0, for_key)
    return for_query, for_key, for_key_back


def head_rows(head, part, width):
    return pl.ds(pl.multiple_of(part * width + head * HEAD_DIM, HEAD_DIM), HEAD_DIM)


def key_band(start, size, tile, length):
    low = max(0, (start - 511) // tile * tile)
    high = min(length, -(-(start + size + 511) // tile) * tile)
    return low, high


def attend_forward(head, qkv_t, ctx_t, lse, mask_q, alive_row, q_aug, k_aug, v_aug, tile):
    width, length = ctx_t.shape
    high, low = scaled_queries(qkv_t[head_rows(head, 0, width), :])
    q_aug[0:64, :] = high
    q_aug[64:128, :] = low
    q_aug[128:144, :] = mask_q[...]
    keys = qkv_t[head_rows(head, 1, width), :]
    k_aug[0:64, :] = keys
    k_aug[64:128, :] = keys
    v_aug[0:64, :] = qkv_t[head_rows(head, 2, width), :]
    for start in range(0, length, tile):
        at = pl.ds(start, tile)
        scores = dot_tn(k_aug[...], q_aug[:, at])
        top = jnp.max(scores, axis=0, keepdims=True)
        weights = jnp.exp2(scores - top)
        total = jnp.sum(weights, axis=0, keepdims=True)
        context = dot_nn(v_aug[0:64, :], (weights * (1.0 / total)).astype(BF16))
        own = v_aug[0:64, at].astype(F32)
        ctx_t[head_rows(head, 0, width), at] = jnp.where(
            alive_row[:, at] > 0, context, own
        ).astype(BF16)
        lse[head, :, at] = top + jnp.log(total) * LOG2E


def attend_backward_begin(head, qkv_t, dctx_t, ctx_t, lse, mask_q, q_aug, k_aug, v_aug, d_aug, dk, dv):
    width, length = ctx_t.shape
    row = lax.broadcasted_iota(jnp.int32, (16, length), 0)
    high, low = scaled_queries(qkv_t[head_rows(head, 0, width), :])
    q_aug[0:64, :] = high
    q_aug[64:128, :] = low
    one, two, three = split_three(-lse[head])
    q_aug[128:144, :] = jnp.where(
        row == 9, one, jnp.where(row == 10, two, jnp.where(row == 11, three, mask_q[...].astype(F32)))
    ).astype(BF16)
    keys = qkv_t[head_rows(head, 1, width), :]
    k_aug[0:64, :] = keys
    k_aug[64:128, :] = keys
    v_aug[0:64, :] = qkv_t[head_rows(head, 2, width), :]
    grad = dctx_t[head_rows(head, 0, width), :]
    d_aug[0:64, :] = grad
    context = ctx_t[head_rows(head, 0, width), :].astype(F32)
    one, two, three = split_three(
        -jnp.sum(grad.astype(F32) * context, axis=0, keepdims=True)
    )
    d_aug[64:80, :] = jnp.where(
        row == 0, one, jnp.where(row == 1, two, jnp.where(row == 2, three, 0.0))
    ).astype(BF16)
    dk[...] = jnp.zeros(dk.shape, F32)
    dv[...] = jnp.zeros(dv.shape, F32)


def attend_backward_tile(head, qkv_t, q_aug, k_aug, v_aug, d_aug, dk, dv, start, tile):
    length = qkv_t.shape[1]
    queries = head_rows(head, 0, qkv_t.shape[0] // 3)
    first, last = key_band(start, tile, tile, length)
    at, near = pl.ds(start, tile), pl.ds(first, last - first)
    weights = jnp.exp2(dot_tn(q_aug[:, at], k_aug[:, near]))
    dweights = dot_tn(d_aug[:, at], v_aug[:, near])
    dscores = (weights * dweights).astype(BF16)
    dv[:, near] += dot_nn(d_aug[0:64, at], weights.astype(BF16))
    dk[:, near] += dot_nn(qkv_t[queries, at], dscores)
    qkv_t[queries, at] = (dot_nt(k_aug[0:64, near], dscores) * HEAD_DIM ** (-0.5)).astype(BF16)


def attend_backward_end(head, qkv_t, dk, dv):
    width = qkv_t.shape[0] // 3
    qkv_t[head_rows(head, 1, width), :] = (dk[...] * HEAD_DIM ** (-0.5)).astype(BF16)
    qkv_t[head_rows(head, 2, width), :] = dv[...].astype(BF16)


def gelu_parts(u):
    square = u * u
    bend = jnp.tanh(u * (GELU_A + (GELU_A * GELU_B) * square))
    half = 0.5 + 0.5 * bend
    slope = half + (0.5 * u) * (1.0 - bend * bend) * (GELU_A + (3.0 * GELU_A * GELU_B) * square)
    return u * half, slope


MESH = pl.DeviceIdType.MESH
GROUP = 8


class Numbers:
    def __init__(self):
        self.used = 0

    def take(self, count):
        first = self.used
        self.used += count
        return first


def number_copies(groups):
    numbers = Numbers()
    names = {}
    for name, count in [
        ("w1x", 2), ("w1y", 2), ("w1c", 1), ("w1d", 2), ("w2a", 2), ("w2b", 2), ("w2c", 1), ("w2d", 1),
        ("w3x", 2), ("w3y", 2), ("w3c", 1), ("w3d", 2), ("gc", 8), ("g1", 4), ("g3y", 4), ("g3x", 4),
        ("gzu", 2), ("gzm", 4), ("gyr", 2), ("gya", 4), ("gfa", 4), ("gfb", 4),
        ("vec_dp", 3), ("vec_ex", GROUP - 1), ("vec_far", groups - 1),
    ]:
        names[name] = numbers.take(count)
    for index, levels in enumerate(LEVELS):
        copies = sum(len(level_steps(level)) for level in levels)
        names["sum", index] = numbers.take(2 * copies + groups - 1)
    return names, numbers.used


ROUNDS = (512, 384, 384, 384, 384)
LEVELS = (("c", "x", "yz"), ("c", "y", "xz"), ("c", "x", "yz"), ("c", "y", "xz"), ("c", "x", "yz"))
ORDER = {
    "h0": [("a", 0, 0), ("p", "y"), ("y", "y"), ("x", 0), ("p", "n"), ("x", 1)],
    "h1": [("a", 0, 1), ("x", 2)],
    "h2": [("a", 1, 0), ("z", 0), ("x", 3), ("y", "n")],
    "h3": [("a", 1, 1), ("z", 1)],
    "h4": [("a", 2, 0), ("a", 0, 2)],
    "h5": [("a", 2, 1), ("z", 2)],
    "h6": [("a", 3, 0), ("z", 3), ("f", 0), ("f", 1)],
    "h7": [("a", 1, 2), ("a", 3, 1), ("a", 2, 2)],
    "E": [("a", 4, 0), ("a", 0, 3), ("f", 2), ("l", 0)],
    "L1": [("f", 3), ("a", 4, 1)],
    "L2": [("a", 1, 3), ("l", 1)],
    "L3": [("a", 3, 2)],
    "L4": [("a", 4, 2), ("a", 2, 3)],
    "tail": [
        ("a", 0, 4), ("a", 1, 4), ("l", 2), ("a", 3, 3), ("l", 3), ("a", 0, 5), ("a", 4, 3), ("a", 0, 6),
        ("vex",), ("a", 2, 4), ("a", 1, 5), ("a", 3, 4), ("a", 1, 6), ("a", 4, 4), ("a", 2, 5), ("a", 3, 5),
        ("a", 2, 6), ("vend",), ("a", 3, 6), ("a", 4, 5), ("a", 4, 6),
    ],
}
AXES = {"x": 2, "y": 2, "c": 2, "z": GROUP // 2}


def level_steps(level):
    ranges = [range(AXES[axis] if axis in level else 1) for axis in "xycz"]
    return [steps for steps in itertools.product(*ranges) if any(steps)]


def share(rows, axes, place):
    start, first = 0, 0
    count, lanes = rows, 512
    if "x" in axes:
        count = count // AXES["x"]
        start = start + count * place[0]
    if "z" in axes:
        count = count // AXES["z"]
        start = start + count * place[3]
    if "c" in axes:
        lanes = lanes // AXES["c"]
        first = first + lanes * place[2]
    if "y" in axes:
        lanes = lanes // AXES["y"]
        first = first + lanes * place[1]
    rows_at = pl.ds(0, count) if isinstance(start, int) else pl.ds(pl.multiple_of(start, 16), count)
    return rows_at, pl.ds(pl.multiple_of(first, 128), lanes)


def kernel(
    experts,
    tokens, cotangent, segments_in, live, ln1_gain_in, ln1_bias_in, ln2_gain_in, ln2_bias_in, wqkv_in,
    wattn_in, logits_in, expert_in, expert_out,
    out, grad_in, in_grad, out_grad, qkv_grad, attn_grad, vectors_out, logits_grad_out,
    segments, ln1_gain, ln1_bias, ln2_gain, ln2_bias, logits, vectors, logits_grad,
    x, dy, wqkv, wattn, w, a1, qkv_t, ctx_t, lse, mid, a2, dz, hid, dpre, total, da2,
    dctx_t, alive_row, mask_q, q_aug, k_aug, v_aug, d_aug, dk, dv, gate_sum,
    rc, r1, r3y, r3x, rz, ryr, fin, part, landed, across, done, vec_dp, vec_ex, vec_sum,
    load_sem, store_sem, send_sem, recv_sem,
):
    length, width = x.shape
    tile = 256
    groups = experts // GROUP
    names, _ = number_copies(groups)
    expert = lax.axis_index("expert")
    dp = lax.axis_index("dp")
    core, row_y = dp % 2, dp // 2
    dp_core = dp + 1 - 2 * core
    here = (expert % 2, row_y, core, expert % GROUP // 2)
    dp_y = (dp + 2) % 4
    place = expert % GROUP
    base = expert - place
    mate_core = (expert, dp_core)
    mate_y = (expert, dp_y)
    mate_x = (expert + 1 - 2 * (expert % 2), dp)
    above = ((expert + 2) % experts, dp)
    below = ((expert + experts - 2) % experts, dp)

    def copy(src, dst, index, device):
        return pltpu.make_async_remote_copy(
            src_ref=src, dst_ref=dst, send_sem=send_sem.at[index], recv_sem=recv_sem.at[index],
            device_id=device, device_id_type=MESH,
        )

    def peer(step):
        return (base + (place + step) % GROUP, dp)

    def far(step):
        return ((expert + GROUP * step) % experts, dp)

    barrier = pltpu.get_barrier_semaphore()
    others = [mate_core, mate_y, mate_x, above, below] + [far(step) for step in range(1, groups)]
    for other in others:
        pl.semaphore_signal(barrier, inc=1, device_id=other, device_id_type=MESH)

    loads = [
        pltpu.make_async_copy(src, dst, load_sem.at[i])
        for i, (src, dst) in enumerate(
            [
                (expert_in.at[:, pl.ds(0, 512)], w.at[0, 0]),
                (expert_out.at[pl.ds(0, 512), :], w.at[0, 1]),
                (expert_in.at[:, pl.ds(512, 512)], w.at[0, 2]),
                (expert_out.at[pl.ds(512, 512), :], w.at[0, 3]),
                (tokens, x),
                (wqkv_in, wqkv),
                (wattn_in, wattn),
                (cotangent, dy),
                (segments_in, segments),
                (ln1_gain_in, ln1_gain),
                (ln1_bias_in, ln1_bias),
                (ln2_gain_in, ln2_gain),
                (ln2_bias_in, ln2_bias),
                (logits_in, logits),
            ]
        )
    ]
    for load in loads[8:] + loads[4:5] + loads[:4] + loads[5:8]:
        load.start()
    live_count = live[0]
    alive_row[...] = jnp.where(
        lax.broadcasted_iota(jnp.int32, (1, length), 1) < live_count, 1.0, 0.0
    )
    for load in loads[8:]:
        load.wait()
    for_query, for_key, for_key_back = mask_rows(segments[...], live_count, length)
    mask_q[...] = for_query.astype(BF16)
    for head in range(2):
        k_aug[head, 128:144, :] = for_key.astype(BF16)
    gain1, bias1, gain2, bias2 = (
        ref[...].astype(F32).reshape(1, width) for ref in (ln1_gain, ln1_bias, ln2_gain, ln2_bias)
    )
    exponent = jnp.exp(logits[...] - jnp.max(logits[...], axis=1, keepdims=True))
    gates = exponent / jnp.sum(exponent, axis=1, keepdims=True)

    def halves(name, slot, unit, to_slot, device):
        return [
            copy(
                w.at[slot, unit, pl.ds(256 * h, 256), :], w.at[to_slot, unit, pl.ds(256 * h, 256), :],
                names[name] + h, device,
            )
            for h in range(2)
        ]

    w1x = halves("w1x", 0, dp, 1, mate_x)
    w1y = halves("w1y", 1, dp, 1, mate_y)
    w1d = halves("w1d", 1, dp_y, 1, mate_core)
    w1c = copy(w.at[1, dp], w.at[1, dp], names["w1c"], mate_core)
    w2a = halves("w2a", 0, dp, 2, below)
    w2b = halves("w2b", 0, dp_y, 2, below)
    w2c = copy(w.at[2, dp], w.at[2, dp], names["w2c"], mate_core)
    w2d = copy(w.at[2, dp_y], w.at[2, dp_y], names["w2d"], mate_core)
    w3x = halves("w3x", 2, dp, 3, mate_x)
    w3y = halves("w3y", 3, dp, 3, mate_y)
    w3d = halves("w3d", 3, dp_y, 3, mate_core)
    w3c = copy(w.at[3, dp], w.at[3, dp], names["w3c"], mate_core)

    loads[4].wait()
    for start in range(0, length, tile):
        at = pl.ds(start, tile)
        normal, inverse = norm_parts(x[at, :].astype(F32))
        a1[at, :] = (normal * gain1 + bias1).astype(BF16)
    for load in loads[:4]:
        load.wait()
    pl.semaphore_wait(barrier, len(others))
    for h in range(2):
        w1x[h].start()
        w2a[h].start()
    for h in range(2):
        w2b[h].start()

    loads[5].wait()
    for start in range(0, 3 * width, 512):
        at = pl.ds(start, 512)
        qkv_t[at, :] = dot_tt(wqkv[:, at], a1[...]).astype(BF16)

    def forward_heads(pair, carry):
        @pl.when(pair == 2)
        def _():
            w1x[0].wait_recv()
            w1y[0].start()
            w2a[0].wait_recv()
            w3x[0].start()

        for head in range(2):
            attend_forward(
                2 * pair + head, qkv_t, ctx_t, lse, mask_q, alive_row, q_aug.at[head], k_aug.at[head],
                v_aug.at[head], length,
            )
        return carry

    lax.fori_loop(0, width // HEAD_DIM // 2, forward_heads, 0)
    w1x[1].wait_recv()
    w1y[1].start()
    w1c.start()
    w2a[1].wait_recv()
    w3x[1].start()
    w2c.start()

    loads[6].wait()
    loads[7].wait()
    for start in range(0, length, tile):
        at = pl.ds(start, tile)
        middle = x[at, :].astype(F32) + dot_tn(ctx_t[:, at], wattn[...])
        mid[at, :] = middle
        total[at, :] = middle
        normal, inverse = norm_parts(middle)
        a2[at, :] = (normal * gain2 + bias2).astype(BF16)
        alive = start + lax.broadcasted_iota(jnp.int32, (tile, 1), 0) < live_count
        live_dy = jnp.where(alive, dy[at, :], jnp.zeros((), BF16))
        dy[at, :] = live_dy
        for k in range(2):
            dz[k, at, :] = (gates[:, k : k + 1] * live_dy.astype(F32)).astype(BF16)
    da2[...] = jnp.zeros(da2.shape, F32)
    gate_sum[...] = jnp.zeros(gate_sum.shape, F32)

    def add_into(target, *terms):
        value = target[...].astype(F32)
        for term in terms:
            value = value + term[...].astype(F32)
        target[...] = value.astype(BF16)

    own_rows = pl.ds(pl.multiple_of(256 * row_y, 256), 256)
    other_rows = pl.ds(pl.multiple_of(256 * (1 - row_y), 256), 256)

    def unit(slot, chunk, rows=pl.ds(0, 512)):
        return w.at[slot, 2 * chunk + core, rows, :]

    def gc(slot, chunk):
        return copy(
            w.at[slot, 2 * chunk + 1 - core], rc.at[slot, chunk], names["gc"] + 2 * slot + chunk, mate_core
        )

    def add_core(slot, chunk):
        gc(slot, chunk).wait_recv()
        add_into(unit(slot, chunk), rc.at[slot, chunk])

    def g1(chunk, h):
        rows = pl.ds(256 * h, 256)
        return copy(unit(1, chunk, rows), r1.at[chunk, rows, :], names["g1"] + 2 * chunk + h, mate_x)

    def final(chunk, rows):
        return fin.at[2 * chunk + core, rows, :]

    def quarter(own, h):
        start = row_y if own else 1 - row_y
        return pl.ds(pl.multiple_of(256 * start + 128 * h, 128), 128)

    def pieces(name, device, src, dst):
        return [
            copy(src(k, h), dst(k, h), names[name] + 2 * k + h, device) for k in range(2) for h in range(2)
        ]

    def half_of(ref, k, h):
        return ref.at[k, pl.ds(128 * h, 128), :]

    g3y = pieces("g3y", mate_y, lambda k, h: unit(3, k, quarter(False, h)), functools.partial(half_of, r3y))
    g3x = pieces("g3x", mate_x, lambda k, h: unit(3, k, quarter(True, h)), functools.partial(half_of, r3x))
    gzm = pieces(
        "gzm", above, lambda k, h: unit(2, k, quarter(True, h)), lambda k, h: rz.at[k, quarter(True, h), :]
    )

    def gzu(chunk):
        return copy(unit(2, chunk, other_rows), rz.at[chunk, other_rows, :], names["gzu"] + chunk, above)

    def gyr(chunk):
        return copy(unit(0, chunk, other_rows), ryr.at[chunk], names["gyr"] + chunk, mate_y)

    def own_final(k, h):
        return final(k, quarter(True, h))

    def other_final(k, h):
        return final(k, quarter(False, h))

    gya = pieces("gya", mate_y, own_final, own_final)
    gfa = pieces("gfa", mate_core, own_final, own_final)
    gfb = pieces("gfb", mate_core, other_final, other_final)

    def slot_pair(turn, carry):
        later = turn // 3
        slots = (2 * ((turn + 3) // 4) + (turn % 3) // 2, 1 + 2 * ((turn % 3) // 2) - later)
        flips = (later, (turn + 2) // 3)
        chunks = tuple(row_y + flip * (1 - 2 * row_y) for flip in flips)

        def part_of(index, at):
            slot, chunk = slots[index], chunks[index]
            k = slot // 2
            w_in, w_out = w.at[slot, 2 * chunk], w.at[slot, 2 * chunk + 1]
            hidden, slope = gelu_parts(dot_nn(a2[at, :], w_in[...]))
            hid[index, at, :] = hidden.astype(BF16)
            dhidden = dot_nt(dz[k, at, :], w_out[...])
            dpre[index, at, :] = (dhidden * slope).astype(BF16)

        blocks = [pl.ds(start, 256) for start in range(0, length, 256)]

        @pl.when(turn == 1)
        def _():
            w1y[1].wait_recv()
            w1d[1].start()
            w2c.wait_recv()

        @pl.when(turn == 2)
        def _():
            w3c.wait_recv()
            w3y[0].wait_recv()
            w3d[0].start()

        @pl.when(turn == 3)
        def _():
            w2d.wait_recv()

        for at in blocks:
            part_of(0, at)

        @pl.when(turn == 0)
        def _():
            w3x[0].wait_recv()
            w3y[0].start()
            w1y[0].wait_recv()
            w1d[0].start()
            w1c.wait_recv()

        @pl.when(turn == 1)
        def _():
            w3x[1].wait_recv()
            w3y[1].start()
            w3c.start()
            for h in range(2):
                w2b[h].wait_recv()
            w2d.start()
            for h in range(2):
                w1d[h].wait_recv()

        @pl.when(turn == 2)
        def _():
            w3y[1].wait_recv()
            w3d[1].start()
            add_core(2, row_y)
            add_core(1, 1 - row_y)
            for h in range(2):
                g1(1 - row_y, h).start()
            gzu(row_y).start()
            for h in range(2):
                w3d[h].wait_recv()

        for at in blocks:
            part_of(1, at)
            value = total[at, :]
            back = da2[at, :]
            live_dy = dy[at, :].astype(F32)
            for index in range(2):
                slot, chunk = slots[index], chunks[index]
                gate = jnp.where(slot < 2, gates[:, 0:1], gates[:, 1:2])
                branch = dot_nn(hid[index, at, :], w[slot, 2 * chunk + 1])
                gate_sum[slot // 2] += jnp.sum(branch * live_dy, axis=0, keepdims=True)
                value = value + gate * branch
                back = back + dot_nt(dpre[index, at, :], w[slot, 2 * chunk])
            total[at, :] = value
            da2[at, :] = back

        @pl.when(turn == 0)
        def _():
            for each in w1x + w2a + w1y + [w1c]:
                each.wait_send()

        @pl.when(turn == 1)
        def _():
            for each in w3x + w1d + [w2c]:
                each.wait_send()
            add_core(0, row_y)
            add_core(1, row_y)
            for h in range(2):
                g1(row_y, h).start()

        @pl.when(turn == 2)
        def _():
            for each in w3y + w3d + [w3c]:
                each.wait_send()

        @pl.when(turn == 3)
        def _():
            for each in w2b + [w2d]:
                each.wait_send()
            for k in range(2):
                add_core(3, k)
                for h in range(2):
                    g3y[2 * k + h].start()

        for index in range(2):
            slot, chunk = slots[index], chunks[index]
            k = slot // 2
            w[slot, 2 * chunk] = dot_tn(a2[...], dpre[index]).astype(BF16)
            w[slot, 2 * chunk + 1] = dot_tn(hid[index], dz[k]).astype(BF16)
            gc(slot, chunk).start()
        return carry

    lax.fori_loop(0, 4, slot_pair, 0)

    gain_sum = jnp.zeros((1, width), F32)
    bias_sum = jnp.zeros((1, width), F32)
    for start in range(0, length, tile):
        at = pl.ds(start, tile)
        normal, inverse = norm_parts(mid[at, :])
        grad = da2[at, :]
        gain_sum += jnp.sum(grad * normal, axis=0, keepdims=True)
        bias_sum += jnp.sum(grad, axis=0, keepdims=True)
        dmid = dy[at, :].astype(F32) + norm_back(grad * gain2, normal, inverse)
        mid[at, :] = dmid
        a2[at, :] = dmid.astype(BF16)
    vectors[2:3, :] = gain_sum
    vectors[3:4, :] = bias_sum
    vectors[4:5, :] = gate_sum[0]
    vectors[5:6, :] = gate_sum[1]
    vectors[6:8, :] = jnp.zeros((2, width), F32)
    add_core(2, 1 - row_y)
    gzu(1 - row_y).start()
    add_core(0, 1 - row_y)
    dctx_t[...] = dot_nt(wattn[...], a2[...]).astype(BF16)

    def sum_round(index):
        rows, levels = ROUNDS[index], LEVELS[index]
        mine, cross, result = part[index], across[index], done[index]
        number = names["sum", index]
        scatter, gather, done_axes = [], [], []
        axes = ""
        for level, buffer in zip(levels, landed[index]):
            axes = axes + level
            done_axes.append(axes)
            there, back = [], []
            for slot, steps in enumerate(level_steps(level)):
                x_there = here[0] + steps[0] * (1 - 2 * here[0])
                y_there = here[1] + steps[1] * (1 - 2 * here[1])
                c_there = here[2] + steps[2] * (1 - 2 * here[2])
                z_there = (here[3] + steps[3]) % AXES["z"]
                device = (base + 2 * z_there + x_there, 2 * y_there + c_there)
                away = share(rows, axes, (x_there, y_there, c_there, z_there))
                there.append(copy(mine.at[away], buffer.at[slot], number, device))
                at = share(rows, axes, here)
                back.append(copy(result.at[at], result.at[at], number + 1, device))
                number += 2
            scatter.append(there)
            gather.append(back)
        over = [copy(cross.at[0], cross.at[s], number + s - 1, far(s)) for s in range(1, groups)]
        last = len(levels) - 1

        def start_all(copies):
            for each in copies:
                each.start()

        def wait_all(copies):
            for each in copies:
                each.wait_recv()

        def begin():
            start_all(scatter[0])

        def add_up(level):
            wait_all(scatter[level])
            at = share(rows, done_axes[level], here)
            value = mine[at].astype(F32)
            for slot in range(len(scatter[level])):
                value = value + landed[index][level][slot].astype(F32)
            if level < last:
                mine[at] = value.astype(BF16)
                start_all(scatter[level + 1])
                return
            if groups > 1:
                cross[0] = value.astype(BF16)
                start_all(over)
                wait_all(over)

                def add_group(group, value):
                    step = (expert // GROUP - group + groups) % groups
                    return value + cross[step].astype(F32)

                value = lax.fori_loop(0, groups, add_group, jnp.zeros(value.shape, F32))
            result[at] = value.astype(BF16)
            start_all(gather[last])

        def pass_back(level):
            wait_all(gather[level])
            if level > 0:
                start_all(gather[level - 1])

        def finish():
            for copies in scatter + gather + [over]:
                for each in copies:
                    each.wait_send()

        steps = [begin] + [functools.partial(add_up, level) for level in range(last + 1)]
        steps += [functools.partial(pass_back, level) for level in range(last, -1, -1)]
        return steps, finish

    rounds = [sum_round(index) for index in range(len(ROUNDS))]
    def advance(index, step):
        steps = rounds[index][0]
        if step == 0 and index == 0:
            part[0][...] = dot_nn(ctx_t[...], a2[...]).astype(BF16)
        elif step == 0:
            qkv_rows(index - 1)
        steps[step]()
        if step == len(steps) - 1 and index == 0:
            store(done[0], attn_grad)
        elif step == len(steps) - 1:
            store_pair(index - 1)

    for head in range(2):
        k_aug[head, 128:144, :] = for_key_back.astype(BF16)
        v_aug[head, 64:80, :] = jnp.where(
            lax.broadcasted_iota(jnp.int32, (16, length), 0) < 3, 1.0, 0.0
        ).astype(BF16)

    def qkv_rows(pair):
        for index in range(3):
            at = pl.ds(index * width + 128 * pair, 128)
            part[1 + pair][128 * index : 128 * index + 128, :] = dot_nn(qkv_t[at, :], a1[...]).astype(BF16)

    def take_x(p):
        g3y[p].wait_recv()
        add_into(unit(3, p // 2, quarter(True, p % 2)), half_of(r3y, p // 2, p % 2))
        g3x[p].start()

    def take_z(p):
        g3x[p].wait_recv()
        add_into(unit(2, p // 2, quarter(True, p % 2)), half_of(r3x, p // 2, p % 2))
        gzm[p].start()

    def take_partner(k):
        for h in range(2):
            g1(k, h).wait_recv()
        add_into(unit(0, k), r1.at[k])

    def take_y(k):
        gzu(k).wait_recv()
        add_into(unit(0, k, other_rows), rz.at[k, other_rows, :])
        gyr(k).start()

    def take_final(p):
        k, h = p // 2, p % 2
        if h == 0:
            gyr(k).wait_recv()
        gzm[p].wait_recv()
        value = unit(0, k, quarter(True, h))[...].astype(F32) + rz[k, quarter(True, h), :].astype(F32)
        own_final(k, h)[...] = (value + ryr[k, pl.ds(128 * h, 128), :].astype(F32)).astype(BF16)
        gya[p].start()
        gfa[p].start()

    def take_last(p):
        gya[p].wait_recv()
        gfb[p].start()

    def take(steps):
        for name, *which in steps:
            if name == "a":
                advance(*which)
            elif name == "x":
                take_x(*which)
            elif name == "z":
                take_z(*which)
            elif name == "p":
                take_partner(row_y if which[0] == "y" else 1 - row_y)
            elif name == "y":
                take_y(row_y if which[0] == "y" else 1 - row_y)
            elif name == "f":
                take_final(*which)
            elif name == "l":
                take_last(*which)
            elif name == "vex":
                vectors_over_experts()
            else:
                vectors_end()

    def backward_heads(pair, carry):
        def hook(part_of_pair):
            for index in range(part_of_pair, width // HEAD_DIM, 2):
                pl.when(2 * pair + part_of_pair == index)(functools.partial(take, ORDER[f"h{index}"]))

        buffers = [[ref.at[head] for ref in (q_aug, k_aug, v_aug, d_aug, dk, dv)] for head in range(2)]
        hook(0)
        for head in range(2):
            attend_backward_begin(2 * pair + head, qkv_t, dctx_t, ctx_t, lse, mask_q, *buffers[head])
        for start in range(0, length, tile):
            if start == length // 2:
                hook(1)
            for head in range(2):
                attend_backward_tile(2 * pair + head, qkv_t, *buffers[head], start, tile)
        for head in range(2):
            attend_backward_end(2 * pair + head, qkv_t, dk.at[head], dv.at[head])
        return carry

    lax.fori_loop(0, width // HEAD_DIM // 2, backward_heads, 0)
    take(ORDER["E"])

    stores = []

    def store(src, dst):
        stores.append(pltpu.make_async_copy(src, dst, store_sem.at[len(stores)]))
        stores[-1].start()

    dz[0] = total[...].astype(BF16)
    store(dz.at[0], out)
    gain_sum = jnp.zeros((1, width), F32)
    bias_sum = jnp.zeros((1, width), F32)
    for index, start in enumerate(range(0, length, tile)):
        at = pl.ds(start, tile)
        grad = dot_tt(qkv_t[:, at], wqkv[...])
        normal, inverse = norm_parts(x[at, :].astype(F32))
        gain_sum += jnp.sum(grad * normal, axis=0, keepdims=True)
        bias_sum += jnp.sum(grad, axis=0, keepdims=True)
        a2[at, :] = (mid[at, :] + norm_back(grad * gain1, normal, inverse)).astype(BF16)
        take(ORDER[f"L{index + 1}"])
    store(a2, grad_in)
    vectors[0:1, :] = gain_sum
    vectors[1:2, :] = bias_sum

    vec_dp[dp] = vectors[...]
    to_dp = [
        copy(vec_dp.at[dp], vec_dp.at[dp], names["vec_dp"] + s - 1, (expert, (dp + s) % 4))
        for s in range(1, 4)
    ]
    for each in to_dp:
        each.start()
    to_ex = [
        copy(vec_ex.at[expert], vec_ex.at[expert], names["vec_ex"] + s - 1, peer(s))
        for s in range(1, GROUP)
    ]
    sums = [to_dp, to_ex]

    def vectors_over_experts():
        for each in to_dp:
            each.wait_recv()
        row_sum = vec_dp[0] + vec_dp[1] + vec_dp[2] + vec_dp[3]
        vec_ex[expert] = row_sum[0:4, :]
        for each in to_ex:
            each.start()
        scaled = jnp.sum(row_sum[4:6, :], axis=1, keepdims=True)
        pair_lane = lax.broadcasted_iota(jnp.int32, (1, 2), 1)
        dgate = jnp.where(pair_lane == 0, scaled[0:1, :], scaled[1:2, :])
        logits_grad[...] = gates * (dgate - jnp.sum(gates * dgate, axis=1, keepdims=True))

    def vectors_end():
        for each in to_ex:
            each.wait_recv()
        if groups > 1:
            vec_group = vec_ex[base]
            for s in range(1, GROUP):
                vec_group = vec_group + vec_ex[base + s]
            own = experts + expert // GROUP
            vec_ex[own] = vec_group
            to_far = [
                copy(vec_ex.at[own], vec_ex.at[own], names["vec_far"] + s - 1, far(s))
                for s in range(1, groups)
            ]
            for each in to_far:
                each.start()
            for each in to_far:
                each.wait_recv()
            sums.append(to_far)
            value = vec_ex[experts]
            for s in range(1, groups):
                value = value + vec_ex[experts + s]
        else:
            value = vec_ex[0]
            for s in range(1, GROUP):
                value = value + vec_ex[s]
        vec_sum[...] = value
        store(vec_sum, vectors_out)
        store(logits_grad, logits_grad_out)

    def store_pair(pair):
        for index in range(3):
            store(
                done[1 + pair].at[pl.ds(128 * index, 128), :],
                qkv_grad.at[pl.ds(index * width + 128 * pair, 128), :],
            )

    take(ORDER["tail"])
    for each in gfa + gfb:
        each.wait_recv()
    for chunk in range(2):
        at = pl.ds(512 * chunk, 512)
        store(fin.at[2 * chunk], in_grad.at[:, at])
        store(fin.at[2 * chunk + 1], out_grad.at[at, :])
    for chunk in range(2):
        for slot in range(4):
            gc(slot, chunk).wait_send()
        gzu(chunk).wait_send()
        gyr(chunk).wait_send()
        for h in range(2):
            g1(chunk, h).wait_send()
    for group in [g3y, g3x, gzm, gya, gfa, gfb] + sums:
        for each in group:
            each.wait_send()
    for _, finish in rounds:
        finish()
    for each in stores:
        each.wait()


def last_kernel(
    out_low, grad_low, in_low, outg_low, qkv_low, attn_low, vectors_in, logits_in,
    out, grad_in, gain1, bias1, qkv_grad, attn_grad, gain2, bias2, logits_grad, in_grad, out_grad,
    out_v, grad_v, in_v, outg_v, qkv_v, attn_v, vectors, logits_v, in_f, outg_f, qkv_f, attn_f, rows_f,
    load_sem, store_sem,
):
    loads = [
        pltpu.make_async_copy(src, dst, load_sem.at[i])
        for i, (src, dst) in enumerate(
            [
                (qkv_low, qkv_v), (in_low, in_v), (outg_low, outg_v), (attn_low, attn_v),
                (out_low, out_v), (grad_low, grad_v), (vectors_in, vectors), (logits_in, logits_v),
            ]
        )
    ]
    for each in loads[6:] + loads[:6]:
        each.start()
    stores = []

    def store(src, dst):
        stores.append(pltpu.make_async_copy(src, dst, store_sem.at[len(stores)]))
        stores[-1].start()

    loads[6].wait()
    loads[7].wait()
    for row, target in enumerate([gain1, bias1, gain2, bias2]):
        rows_f[row][...] = vectors[row : row + 1, :].reshape(target.shape)
        store(rows_f[row], target)
    store(logits_v, logits_grad)
    width = attn_v.shape[0]
    loads[0].wait()
    for index in range(3):
        at = pl.ds(index * width, width)
        qkv_f[:, at] = qkv_v[at, :].astype(F32).T
        store(qkv_f.at[:, at], qkv_grad.at[:, at])
    for index, (low, wide, target) in enumerate(
        [(in_v, in_f, in_grad), (outg_v, outg_f, out_grad), (attn_v, attn_f, attn_grad)]
    ):
        loads[1 + index].wait()
        wide[...] = low[...].astype(F32)
        store(wide, target)
    for index, (low, target) in enumerate([(out_v, out), (grad_v, grad_in)]):
        loads[4 + index].wait()
        store(low, target)
    for each in stores:
        each.wait()


def widen(out, grad_in, in_grad, out_grad, qkv_grad, attn_grad, vectors, logits_grad):
    width = attn_grad.shape[0]
    hbm = pl.BlockSpec(memory_space=pl.ANY)
    shape = jax.ShapeDtypeStruct
    low = [out.shape, grad_in.shape, in_grad.shape, out_grad.shape, qkv_grad.shape, attn_grad.shape]
    wide = [in_grad.shape, out_grad.shape, (width, 3 * width), attn_grad.shape]
    vector = shape((width,), F32)
    return pl.pallas_call(
        last_kernel,
        in_specs=[hbm] * 8,
        out_specs=[hbm] * 11,
        out_shape=[
            shape(out.shape, BF16), shape(grad_in.shape, BF16), vector, vector, shape(wide[2], F32),
            shape(wide[3], F32), vector, vector, shape(logits_grad.shape, F32), shape(wide[0], F32),
            shape(wide[1], F32),
        ],
        scratch_shapes=[pltpu.VMEM(each, BF16) for each in low]
        + [pltpu.VMEM(vectors.shape, F32), pltpu.VMEM(logits_grad.shape, F32)]
        + [pltpu.VMEM(each, F32) for each in wide]
        + [[pltpu.VMEM(vector.shape, F32) for _ in range(4)]]
        + [pltpu.SemaphoreType.DMA((8,)), pltpu.SemaphoreType.DMA((13,))],
        compiler_params=pltpu.CompilerParams(vmem_limit_bytes=63 * 1024 * 1024),
    )(out, grad_in, in_grad, out_grad, qkv_grad, attn_grad, vectors, logits_grad)


def one_device(
    experts, tokens, cotangent, segments, live, ln1_gain, ln1_bias, ln2_gain, ln2_bias, wqkv, wattn,
    logits, expert_in, expert_out,
):
    length, width = tokens.shape
    groups = experts // GROUP
    _, semaphores = number_copies(groups)
    smem = pl.BlockSpec(memory_space=pltpu.SMEM)
    hbm = pl.BlockSpec(memory_space=pl.ANY)
    shape = jax.ShapeDtypeStruct

    def by_round(*leading):
        return [pltpu.VMEM((*leading, rows, width), BF16) for rows in ROUNDS]

    def level_buffers(rows, levels):
        axes, buffers = "", []
        for level in levels:
            axes = axes + level
            at, lanes = share(rows, axes, (0, 0, 0, 0))
            buffers.append(pltpu.VMEM((len(level_steps(level)), at.size, lanes.size), BF16))
        return buffers

    def crossing(rows, levels):
        at, lanes = share(rows, "".join(levels), (0, 0, 0, 0))
        return pltpu.VMEM((groups, at.size, lanes.size), BF16)

    scratch = [
        pltpu.VMEM(segments.shape, jnp.int32),
        pltpu.VMEM(ln1_gain.shape, BF16),
        pltpu.VMEM(ln1_bias.shape, BF16),
        pltpu.VMEM(ln2_gain.shape, BF16),
        pltpu.VMEM(ln2_bias.shape, BF16),
        pltpu.VMEM(logits.shape, F32),
        pltpu.VMEM((8, width), F32),
        pltpu.VMEM(logits.shape, F32),
        pltpu.VMEM((length, width), BF16),
        pltpu.VMEM((length, width), BF16),
        pltpu.VMEM(wqkv.shape, BF16),
        pltpu.VMEM(wattn.shape, BF16),
        pltpu.VMEM((4, 4, 512, 512), BF16),
        pltpu.VMEM((length, width), BF16),
        pltpu.VMEM((3 * width, length), BF16),
        pltpu.VMEM((width, length), BF16),
        pltpu.VMEM((width // HEAD_DIM, 1, length), F32),
        pltpu.VMEM((length, width), F32),
        pltpu.VMEM((length, width), BF16),
        pltpu.VMEM((2, length, width), BF16),
        pltpu.VMEM((2, length, 512), BF16),
        pltpu.VMEM((2, length, 512), BF16),
        pltpu.VMEM((length, width), F32),
        pltpu.VMEM((length, width), F32),
        pltpu.VMEM((width, length), BF16),
        pltpu.VMEM((1, length), F32),
        pltpu.VMEM((16, length), BF16),
        pltpu.VMEM((2, 144, length), BF16),
        pltpu.VMEM((2, 144, length), BF16),
        pltpu.VMEM((2, 80, length), BF16),
        pltpu.VMEM((2, 80, length), BF16),
        pltpu.VMEM((2, HEAD_DIM, length), F32),
        pltpu.VMEM((2, HEAD_DIM, length), F32),
        pltpu.VMEM((2, 1, 512), F32),
        pltpu.VMEM((4, 2, 512, 512), BF16),
        pltpu.VMEM((2, 512, 512), BF16),
        pltpu.VMEM((2, 256, 512), BF16),
        pltpu.VMEM((2, 256, 512), BF16),
        pltpu.VMEM((2, 512, 512), BF16),
        pltpu.VMEM((2, 256, 512), BF16),
        pltpu.VMEM((4, 512, 512), BF16),
        by_round(),
        [level_buffers(rows, levels) for rows, levels in zip(ROUNDS, LEVELS)],
        [crossing(rows, levels) for rows, levels in zip(ROUNDS, LEVELS)],
        by_round(),
        pltpu.VMEM((4, 8, width), F32),
        pltpu.VMEM((experts + groups, 4, width), F32),
        pltpu.VMEM((4, width), F32),
        pltpu.SemaphoreType.DMA((14,)),
        pltpu.SemaphoreType.DMA((21,)),
        pltpu.SemaphoreType.DMA((semaphores,)),
        pltpu.SemaphoreType.DMA((semaphores,)),
    ]
    return pl.pallas_call(
        functools.partial(kernel, experts),
        in_specs=[hbm] * 3 + [smem] + [hbm] * 9,
        out_specs=[hbm] * 8,
        out_shape=[
            shape(tokens.shape, BF16),
            shape(tokens.shape, BF16),
            shape(expert_in.shape, BF16),
            shape(expert_out.shape, BF16),
            shape((3 * width, width), BF16),
            shape(wattn.shape, BF16),
            shape((4, width), F32),
            shape((1, 2), F32),
        ],
        scratch_shapes=scratch,
        compiler_params=pltpu.CompilerParams(
            vmem_limit_bytes=63 * 1024 * 1024, collective_id=0, has_side_effects=True
        ),
    )(
        tokens, cotangent, segments, live, ln1_gain, ln1_bias, ln2_gain, ln2_bias, wqkv, wattn, logits,
        expert_in, expert_out,
    )


def body(
    tokens, segment_ids, live_tokens, cotangent, ln1_gain, ln1_bias, qkv_weight, attn_weight,
    ln2_gain, ln2_bias, task_logits, expert_in, expert_out,
):
    out, grad_in, in_grad, out_grad, qkv_grad, attn_grad, vectors, logits_grad = one_device(
        lax.axis_size("expert"), tokens[0], cotangent[0], segment_ids, live_tokens, ln1_gain, ln1_bias,
        ln2_gain, ln2_bias, qkv_weight, attn_weight, task_logits, expert_in[0], expert_out[0],
    )
    (
        out, grad_in, gain1, bias1, qkv_grad, attn_grad, gain2, bias2, logits_grad, in_grad, out_grad
    ) = widen(out, grad_in, in_grad, out_grad, qkv_grad, attn_grad, vectors, logits_grad)
    return (
        out[None], grad_in[None], gain1, bias1, qkv_grad, attn_grad, gain2, bias2, logits_grad,
        in_grad[None], out_grad[None],
    )


def solution(mesh):
    rows = ("expert", "dp")
    in_specs = (
        P(rows, None, None), P(rows, None), P(rows), P(rows, None, None), P(), P(), P(), P(), P(), P(),
        P("expert", None), P("expert", None, None), P("expert", None, None),
    )
    out_specs = (
        P(rows, None, None), P(rows, None, None), P(), P(), P(), P(), P(), P(),
        P("expert", None), P("expert", None, None), P("expert", None, None),
    )
    return jax.shard_map(body, mesh=mesh, in_specs=in_specs, out_specs=out_specs, check_vma=False)
```
